128 devices in a mesh: tm: 64 (over x, y, z), space: 2 (over core).
Axes of the slice: x: 4, y: 4, z: 4, core: 2. Of those that a mesh axis runs over, the one named last changes fastest.
Arguments:
- clean: bfloat16 [320, 16, 16, 1280], P('tm', 'space'), may hold values from -6 to 6
- noise: bfloat16 [320, 16, 16, 1280], P('tm', 'space'), may hold values from -6 to 6
- timestep: int32 [1], replicated, may hold values from 0 to 999
- spatial_weight: bfloat16 [1280, 3, 3, 640], replicated, may hold values from -0.0546875 to 0.0546875
- temporal_weight: bfloat16 [640, 3, 640], replicated, may hold values from -0.125 to 0.125
Outputs:
- loss: float32 [], replicated
- spatial_grad: float32 [1280, 3, 3, 640], P(('tm', 'space'))
- temporal_grad: float32 [640, 3, 640], P(('tm', 'space'))
The draws below stay inside these ranges and needn't reach their ends.
All inputs are finite; a program needn't handle non-finite values.
Results may differ from the reference program's by a relative error of at most 0.0036.
Values may be sent and summed in bfloat16 or wider, within the bound.
No kernel may reach another device: no remote copies, remote signals or barrier semaphores. Data moves between devices by JAX's collectives and lax.ppermute only.
A program may use at most 256 MiB of HBM per device.

```python
import math
import jax
import jax.numpy as jnp
from jax import lax

CHANNELS = 1280
FEATURES = 640
HEIGHT = 16
BREADTH = 16
CLIP = 80
STEPS = 1000
FRAMES = 320


def level_of(own_key, dims, shards, smallest, largest):
    loudness = 1.0
    for dim, blocks in shards:
        draws = jax.random.uniform(jax.random.fold_in(jax.random.fold_in(own_key, 6), dim), (blocks,), jnp.float32, smallest / len(shards), largest / len(shards))
        loudness = loudness * jnp.repeat(jnp.exp(draws), dims[dim] // blocks).reshape((-1,) + (1,) * (len(dims) - 1 - dim))
    return loudness


def bell_draw(stream_key, dims, spread, limit, cuts=(), kind=jnp.bfloat16):
    array = jax.random.normal(stream_key, dims, jnp.float32) * spread
    if len(cuts) > 0:
        array = level_of(stream_key, dims, cuts, -0.22, 0.18) * array
    return jnp.clip(array, min=-limit, max=limit).astype(kind)


def setup_inputs(seed: int = 0) -> dict:
    arg_keys = jax.random.split(jax.random.key(seed), 6)
    return {
        "clean": bell_draw(arg_keys[0], (FRAMES, HEIGHT, BREADTH, CHANNELS), 1.0, 6.0, ((0, 64), (1, 2))),
        "noise": bell_draw(arg_keys[1], (FRAMES, HEIGHT, BREADTH, CHANNELS), 1.0, 6.0, ((0, 64), (1, 2))),
        "timestep": jax.random.randint(arg_keys[2], (1,), 0, STEPS).astype(jnp.int32),
        "spatial_weight": bell_draw(arg_keys[3], (CHANNELS, 3, 3, FEATURES), (9 * CHANNELS) ** -0.5, 0.0546875),
        "temporal_weight": bell_draw(arg_keys[4], (FEATURES, 3, FEATURES), (3 * FEATURES) ** -0.5, 0.125),
    }


def spatial_forward(padded, weight, rows, cols):
    total = jnp.zeros((padded.shape[0] * rows * cols, weight.shape[3]), jnp.float32)
    for first in range(3):
        for second in range(3):
            piece = padded[:, first:first + rows, second:second + cols, :].reshape(-1, padded.shape[3])
            total = total + jnp.dot(piece, weight[:, first, second, :], preferred_element_type=jnp.float32)
    return total

def spatial_backward(padded, grad_hidden, rows, cols):
    flat = grad_hidden.reshape(-1, grad_hidden.shape[-1])
    blocks = []
    for first in range(3):
        for second in range(3):
            piece = padded[:, first:first + rows, second:second + cols, :].reshape(-1, padded.shape[3])
            blocks.append(lax.dot_general(piece, flat, (((0,), (0,)), ((), ())), preferred_element_type=jnp.float32))
    return jnp.stack(blocks, axis=1).reshape(padded.shape[3], 3, 3, flat.shape[1])

def clip_neighbours(values):
    position = (jnp.arange(FRAMES, dtype=jnp.int32) + CLIP // 4) % CLIP
    not_first = (position != 0)[:, None, None]
    not_last = (position != CLIP - 1)[:, None, None]
    padded = jnp.pad(values, ((1, 1), (0, 0), (0, 0)))
    earlier = jnp.where(not_first, padded[0:FRAMES], jnp.zeros_like(values))
    later = jnp.where(not_last, padded[2:FRAMES + 2], jnp.zeros_like(values))
    return (earlier, later)

def reference(clean, noise, timestep, spatial_weight, temporal_weight):
    step_value = timestep[0].astype(jnp.float32)
    angle = math.pi / 2.0 * (step_value + 1.0) / (STEPS + 1.0)
    signal = jnp.cos(angle)
    sigma = jnp.sin(angle)
    clean32 = clean.astype(jnp.float32)
    noise32 = noise.astype(jnp.float32)
    noisy = (signal * clean32 + sigma * noise32).astype(jnp.bfloat16)
    padded = jnp.pad(noisy, ((0, 0), (1, 1), (1, 1), (0, 0)))
    hidden = spatial_forward(padded, spatial_weight, HEIGHT, BREADTH)
    act = jax.nn.silu(hidden).astype(jnp.bfloat16).reshape(FRAMES, HEIGHT * BREADTH, FEATURES)
    act_before, act_after = clip_neighbours(act)
    act_taps = [act_before, act, act_after]
    pred = jnp.zeros((FRAMES * HEIGHT * BREADTH, FEATURES), jnp.float32)
    for tap in range(3):
        pred = pred + jnp.dot(act_taps[tap].reshape(-1, FEATURES), temporal_weight[:, tap, :], preferred_element_type=jnp.float32)
    target = (signal * noise32 - sigma * clean32)[..., :FEATURES].reshape(-1, FEATURES)
    diff = pred - target
    positions = FRAMES * HEIGHT * BREADTH
    loss = jnp.sum(diff * diff) / (positions * FEATURES)
    grad_pred = (2.0 * diff / math.sqrt(positions)).astype(jnp.bfloat16)
    flat_grad = grad_pred
    grad_3 = grad_pred.reshape(FRAMES, HEIGHT * BREADTH, FEATURES)
    grad_before, grad_after = clip_neighbours(grad_3)
    grad_taps = [grad_after, grad_3, grad_before]
    temporal_blocks = []
    grad_act = jnp.zeros((FRAMES * HEIGHT * BREADTH, FEATURES), jnp.float32)
    for tap in range(3):
        shifted = act_taps[tap].reshape(-1, FEATURES)
        temporal_blocks.append(lax.dot_general(shifted, flat_grad, (((0,), (0,)), ((), ())), preferred_element_type=jnp.float32))
        later = grad_taps[tap].reshape(-1, FEATURES)
        grad_act = grad_act + lax.dot_general(later, temporal_weight[:, tap, :], (((1,), (1,)), ((), ())), preferred_element_type=jnp.float32)
    temporal_grad = jnp.stack(temporal_blocks, axis=1)
    sig = jax.nn.sigmoid(hidden)
    grad_hidden = (grad_act * sig * (1.0 + hidden * (1.0 - sig))).astype(jnp.bfloat16)
    spatial_grad = spatial_backward(padded, grad_hidden, HEIGHT, BREADTH)
    return (loss, spatial_grad, temporal_grad)
```

```python
import functools
import math

import jax
import jax.numpy as jnp
import numpy as np
from jax import lax
from jax.experimental import pallas as pl
from jax.experimental.pallas import tpu as pltpu
from jax.sharding import PartitionSpec as P

CLIP = 80
STEPS = 1000
BF = jnp.bfloat16
F32 = jnp.float32
MIB = 1 << 20
STRIDES = (16, 4, 1)
RING = 4
ORDERS = ((0, 1, 2), (1, 2, 0), (2, 0, 1))
LOSS = 16
EXTRA = 64


def params(mib):
    return pltpu.CompilerParams(vmem_limit_bytes=mib * MIB)


def cost(flops, nbytes):
    return pl.CostEstimate(flops=int(flops), bytes_accessed=int(nbytes), transcendentals=0)


def spatial_forward_kernel(x_ref, above_ref, below_ref, w_ref, act_ref, der_ref, xp, acc):
    step = pl.program_id(0)
    group = step // 3
    first = jnp.where(group == 0, 1, jnp.where(group == 1, 0, 2))
    second = step % 3
    frames, span, channels = x_ref.shape
    cols = above_ref.shape[1]
    features = w_ref.shape[3]

    @pl.when(step == 0)
    def _():
        xp[:, 0:cols, :] = above_ref[...]
        xp[:, cols : cols + span, :] = x_ref[...]
        xp[:, cols + span : span + 2 * cols, :] = below_ref[...]

    start = pl.multiple_of(first * cols, cols)
    piece = xp[:, pl.ds(start, span), :].reshape(frames * span, channels)
    prod = jnp.dot(piece, w_ref[0, 0], preferred_element_type=F32)

    @pl.when(step < 3)
    def _():
        acc[second] = prod

    @pl.when(step >= 3)
    def _():
        acc[second] += prod

    @pl.when(step == 8)
    def _():
        col = lax.broadcasted_iota(jnp.int32, (span, features), 0) % cols

        def one(f, carry):
            rows = pl.ds(pl.multiple_of(f * span, span), span)
            left = jnp.where(col == 0, 0.0, pltpu.roll(acc[0, rows, :], 1, 0))
            right = jnp.where(col == cols - 1, 0.0, pltpu.roll(acc[2, rows, :], span - 1, 0))
            hidden = left + acc[1, rows, :] + right
            sig = 1.0 / (1.0 + jnp.exp(-hidden))
            act_ref[f] = (hidden * sig).astype(BF)
            der_ref[f] = sig * (1.0 + hidden * (1.0 - sig))
            return carry

        lax.fori_loop(0, frames, one, 0)


def spatial_forward(x, above, below, weight):
    frames, span, channels = x.shape
    cols = above.shape[1]
    features = weight.shape[3]
    whole = lambda s: (0, 0, 0)

    def tap(s):
        g = s // 3
        return (jnp.where(g == 0, 1, jnp.where(g == 1, 0, 2)), s % 3, 0, 0)

    return pl.pallas_call(
        spatial_forward_kernel,
        grid=(9,),
        in_specs=[
            pl.BlockSpec(x.shape, whole),
            pl.BlockSpec(above.shape, whole),
            pl.BlockSpec(below.shape, whole),
            pl.BlockSpec((1, 1, channels, features), tap),
        ],
        out_specs=[
            pl.BlockSpec((frames, span, features), whole),
            pl.BlockSpec((frames, span, features), whole),
        ],
        out_shape=[
            jax.ShapeDtypeStruct((frames, span, features), BF),
            jax.ShapeDtypeStruct((frames, span, features), F32),
        ],
        scratch_shapes=[
            pltpu.VMEM((frames, span + 2 * cols, channels), BF),
            pltpu.VMEM((3, frames * span, features), F32),
        ],
        compiler_params=params(24),
        cost_estimate=cost(
            2 * 9 * frames * span * channels * features, 2 * 9 * channels * features
        ),
        name="spatial_forward",
    )(x, above, below, weight)


def temporal_forward_kernel(
    scale, act_ref, before_ref, after_ref, w_ref, clean_ref, noise_ref, gp_ref, loss_ref, ap
):
    frames, span, features = act_ref.shape
    factor = scale[2]
    ap[0:1] = before_ref[...]
    ap[1 : frames + 1] = act_ref[...]
    ap[frames + 1 : frames + 2] = after_ref[...]
    pred = jnp.zeros((frames * span, features), F32)
    for tap in range(3):
        pred = pred + jnp.dot(
            ap[tap : tap + frames].reshape(frames * span, features),
            w_ref[tap],
            preferred_element_type=F32,
        )
    clean = clean_ref[...].reshape(frames * span, features).astype(F32)
    noise = noise_ref[...].reshape(frames * span, features).astype(F32)
    diff = pred - (scale[0] * noise - scale[1] * clean)
    gp_ref[...] = (2.0 * diff / factor).astype(BF).reshape(frames, span, features)
    loss_ref[...] = jnp.sum(diff * diff, axis=0, keepdims=True)


def temporal_forward(scale, act, before, after, weight, clean, noise):
    frames, span, features = act.shape
    whole = lambda i: (0, 0, 0)
    head = pl.BlockSpec((frames, span, features), whole)
    halo = pl.BlockSpec((1, span, features), whole)
    return pl.pallas_call(
        temporal_forward_kernel,
        grid=(1,),
        in_specs=[
            pl.BlockSpec(memory_space=pltpu.SMEM),
            head,
            halo,
            halo,
            pl.BlockSpec(weight.shape, whole),
            head,
            head,
        ],
        out_specs=[head, pl.BlockSpec((1, features), lambda i: (0, 0))],
        out_shape=[
            jax.ShapeDtypeStruct((frames, span, features), BF),
            jax.ShapeDtypeStruct((1, features), F32),
        ],
        scratch_shapes=[pltpu.VMEM((frames + 2, span, features), BF)],
        compiler_params=params(14),
        cost_estimate=cost(2 * 3 * frames * span * features * features, 6 * features * features),
        name="temporal_forward",
    )(scale, act, before, after, weight, clean, noise)


def thirds(value):
    high = value.astype(BF)
    rest = value - high.astype(F32)
    middle = rest.astype(BF)
    return high, middle, (rest - middle.astype(F32)).astype(BF)


def stacked(value, rows):
    high, middle, low = thirds(value)
    row = lax.broadcasted_iota(jnp.int32, (rows, value.shape[1]), 0)
    parts = [p.astype(F32) for p in (high, middle, low)]
    return jnp.where(
        row == 0, parts[0], jnp.where(row == 1, parts[1], jnp.where(row == 2, parts[2], 0.0))
    )


def joined(rows):
    return (rows[0:1] + rows[1:2]) + rows[2:3]


def select_act_kernel(
    core_ref, act_ref, before_ref, after_ref, choice_ref, loss_ref, own_ref, send_ref, ap
):
    core = core_ref[0]
    frames, span, features = act_ref.shape
    half = features // 2
    ap[0:1] = before_ref[...]
    ap[1 : frames + 1] = act_ref[...]
    ap[frames + 1 : frames + 2] = after_ref[...]
    act = ap[...].reshape(-1, features)
    for out, which in ((send_ref, 1 - core), (own_ref, core)):
        out[0:half, :] = lax.dot_general(
            choice_ref[which], act, (((1,), (1,)), ((), ())), preferred_element_type=F32
        ).astype(BF)
    send_ref[half:, :] = jnp.zeros((send_ref.shape[0] - half, send_ref.shape[1]), BF)
    send_ref[half : half + LOSS, 0:features] = stacked(loss_ref[...], LOSS).astype(BF)


def selected_act(core, act, before, after, choice, loss):
    frames, span, features = act.shape
    width = (frames + 2) * span
    vmem = pl.BlockSpec(memory_space=pltpu.VMEM)
    return pl.pallas_call(
        select_act_kernel,
        in_specs=[pl.BlockSpec(memory_space=pltpu.SMEM)] + [vmem] * 5,
        out_specs=[vmem, vmem],
        out_shape=[
            jax.ShapeDtypeStruct((features // 2, width), BF),
            jax.ShapeDtypeStruct((features // 2 + LOSS, width), BF),
        ],
        scratch_shapes=[pltpu.VMEM((frames + 2, span, features), BF)],
        compiler_params=params(16),
        cost_estimate=cost(2 * features * features * width, 4 * features * width),
        name="select_act",
    )(core, act, before, after, choice, loss)


def temporal_grad_kernel(
    bits_ref,
    own_ref,
    other_ref,
    gp_ref,
    gp_other_ref,
    reorder_ref,
    loss_ref,
    send_ref,
    keep_ref,
    sum_ref,
    total,
):
    frames, span, features = gp_ref.shape
    half = own_ref.shape[0]
    rows = half // 2
    gp = gp_ref[...].reshape(frames * span, features)
    gp_other = gp_other_ref[...].reshape(frames * span, features)
    for tap in range(3):
        lanes = slice(tap * span, (tap + frames) * span)
        mine, theirs = own_ref[:, lanes], other_ref[0:half, lanes]
        if tap > 0:
            order = reorder_ref[bits_ref[3], tap - 1]
            mine = jnp.dot(order, mine, preferred_element_type=F32).astype(BF)
            theirs = jnp.dot(order, theirs, preferred_element_type=F32).astype(BF)
        total[...] = jnp.dot(mine, gp, preferred_element_type=F32) + jnp.dot(
            theirs, gp_other, preferred_element_type=F32
        )
        bit = bits_ref[tap]
        kept = pl.ds(pl.multiple_of(bit * rows, rows), rows)
        sent = pl.ds(pl.multiple_of((1 - bit) * rows, rows), rows)
        keep_ref[tap] = total[kept, :]
        send_ref[tap, 0:rows, :] = total[sent, :].astype(BF)
        send_ref[tap, rows:, :] = jnp.zeros((send_ref.shape[1] - rows, features), BF)
    met = other_ref[half : half + LOSS, 0:features].astype(F32)
    loss = loss_ref[...] + joined(met)
    sum_ref[...] = loss
    send_ref[0, rows : rows + LOSS, :] = stacked(loss, LOSS).astype(BF)


def temporal_grad_local(bits, own, other, gp, gp_other, reorder, loss):
    frames, span, features = gp.shape
    rows = features // 4
    return pl.pallas_call(
        temporal_grad_kernel,
        in_specs=[pl.BlockSpec(memory_space=pltpu.SMEM)]
        + [pl.BlockSpec(memory_space=pltpu.VMEM)] * 6,
        out_shape=[
            jax.ShapeDtypeStruct((3, 3 * EXTRA, features), BF),
            jax.ShapeDtypeStruct((3, rows, features), F32),
            jax.ShapeDtypeStruct((1, features), F32),
        ],
        out_specs=[pl.BlockSpec(memory_space=pltpu.VMEM)] * 3,
        scratch_shapes=[pltpu.VMEM((features // 2, features), F32)],
        compiler_params=params(14),
        cost_estimate=cost(
            2 * 3 * frames * span * features * features, 6 * features * features
        ),
        name="temporal_grad",
    )(bits, own, other, gp, gp_other, reorder, loss)


def temporal_backward_kernel(gp_ref, before_ref, after_ref, w_ref, der_ref, out_ref, pad):
    frames, span, features = gp_ref.shape
    pad[0:1] = before_ref[...]
    pad[1 : frames + 1] = gp_ref[...]
    pad[frames + 1 : frames + 2] = after_ref[...]
    total = jnp.zeros((frames * span, features), F32)
    for tap in range(3):
        total = total + lax.dot_general(
            pad[2 - tap : 2 - tap + frames].reshape(frames * span, features),
            w_ref[tap],
            (((1,), (1,)), ((), ())),
            preferred_element_type=F32,
        )
    der = der_ref[...].reshape(frames * span, features)
    out_ref[...] = (total * der).astype(BF).reshape(frames, span, features)


def temporal_backward(gp, before, after, weight, der):
    frames, span, features = gp.shape
    return pl.pallas_call(
        temporal_backward_kernel,
        out_shape=jax.ShapeDtypeStruct((frames, span, features), BF),
        scratch_shapes=[pltpu.VMEM((frames + 2, span, features), BF)],
        compiler_params=params(14),
        cost_estimate=cost(2 * 3 * frames * span * features * features, 6 * features * features),
        name="temporal_backward",
    )(gp, before, after, weight, der)


def select_latent_kernel(core_ref, x_ref, choice_ref, own_ref, send_ref):
    core = core_ref[0]
    x = x_ref[...].reshape(-1, x_ref.shape[2])
    for out, which in ((send_ref, 1 - core), (own_ref, core)):
        out[...] = lax.dot_general(
            choice_ref[which], x, (((1,), (1,)), ((), ())), preferred_element_type=F32
        ).astype(BF)


def selected_latent(core, x, choice):
    frames, span, channels = x.shape
    shape = jax.ShapeDtypeStruct((channels // 2, frames * span), BF)
    vmem = pl.BlockSpec(memory_space=pltpu.VMEM)
    return pl.pallas_call(
        select_latent_kernel,
        in_specs=[pl.BlockSpec(memory_space=pltpu.SMEM), vmem, vmem],
        out_specs=[vmem, vmem],
        out_shape=[shape, shape],
        compiler_params=params(20),
        cost_estimate=cost(2 * frames * span * channels * channels, 4 * channels * channels),
        name="select_latent",
    )(core, x, choice)


def arrange_latent_kernel(core_ref, own_ref, other_ref, reorder_ref, out_ref):
    core = core_ref[0]
    span = out_ref.shape[2] // 10
    for f in range(5):
        here = pl.multiple_of((2 * f + core) * span, span)
        there = pl.multiple_of((2 * f + 1 - core) * span, span)
        out_ref[0, :, pl.ds(here, span)] = own_ref[:, f * span : (f + 1) * span]
        out_ref[0, :, pl.ds(there, span)] = other_ref[:, f * span : (f + 1) * span]
    for third in range(1, 3):
        out_ref[third] = jnp.dot(
            reorder_ref[0, third - 1], out_ref[0], preferred_element_type=F32
        ).astype(BF)


def arranged_latent(core, own, other, reorder):
    half, positions = own.shape
    return pl.pallas_call(
        arrange_latent_kernel,
        grid_spec=pltpu.PrefetchScalarGridSpec(
            num_scalar_prefetch=1,
            grid=(1,),
            in_specs=[
                pl.BlockSpec(own.shape, lambda i, c: (0, 0)),
                pl.BlockSpec(own.shape, lambda i, c: (0, 0)),
                pl.BlockSpec((1, 2, half, half), lambda i, c: (c[0], 0, 0, 0)),
            ],
            out_specs=pl.BlockSpec((3, half, 2 * positions), lambda i, c: (0, 0, 0)),
        ),
        out_shape=jax.ShapeDtypeStruct((3, half, 2 * positions), BF),
        compiler_params=params(24),
        cost_estimate=cost(8 * half * half * positions, 20 * half * positions),
        name="arrange_latent",
    )(core, own, other, reorder)


def spatial_backward_kernel(has_extra, where, lat_ref, own_ref, other_ref, *rest):
    extra_ref = rest[0] if has_extra else None
    outs, pad = rest[-4:-1], rest[-1]
    step = pl.program_id(0)
    first = step // 3
    second = step % 3
    core = where[0]
    frames, span, features = own_ref.shape
    cols = (pad.shape[2] - 2 * span) // 2
    height = lat_ref.shape[1]

    @pl.when(step == 0)
    def _():
        col = lax.broadcasted_iota(jnp.int32, (span, features), 0) % cols
        rim = jnp.zeros((cols, features), BF)

        def one(f, carry):
            for b in range(3):
                pad[b, f, 0:cols, :] = rim
                pad[b, f, cols + 2 * span : 2 * cols + 2 * span, :] = rim
            for ref, place in ((own_ref, core), (other_ref, 1 - core)):
                rows = pl.ds(pl.multiple_of(cols + place * span, cols), span)
                here = ref[f]
                wide = here.astype(F32)
                later = jnp.where(col == cols - 1, 0.0, pltpu.roll(wide, span - 1, 0))
                sooner = jnp.where(col == 0, 0.0, pltpu.roll(wide, 1, 0))
                pad[0, f, rows, :] = later.astype(BF)
                pad[1, f, rows, :] = here
                pad[2, f, rows, :] = sooner.astype(BF)
            return carry

        lax.fori_loop(0, frames, one, 0)

    start = pl.multiple_of((2 - first) * cols, cols)
    grad = pad[second, :, pl.ds(start, 2 * span), :].reshape(2 * frames * span, features)
    total = jnp.dot(lat_ref[0], grad, preferred_element_type=F32)
    for row in range(3):

        @pl.when(first == row)
        def _():
            outs[row][0, 0:height, :] = total.astype(outs[row].dtype)
            if has_extra:
                outs[row][0, height:, :] = extra_ref[0]


def spatial_backward(where, lat, own, other, extra, kind, name):
    frames, span, features = own.shape
    rows = lat.shape[1] // 2
    cols = 16
    tall = rows + (0 if extra is None else EXTRA)

    def out_map(row):
        return lambda s, w: (jnp.clip(s - 3 * row, 0, 2), 0, 0)

    more_specs = [] if extra is None else [
        pl.BlockSpec((1, EXTRA, features), lambda s, w: (s // 3, s % 3, 0))
    ]
    more = [] if extra is None else [extra]
    return pl.pallas_call(
        functools.partial(spatial_backward_kernel, extra is not None),
        grid_spec=pltpu.PrefetchScalarGridSpec(
            num_scalar_prefetch=1,
            grid=(9,),
            in_specs=[
                pl.BlockSpec((1, rows, lat.shape[2]), lambda s, w: (s // 3, w[1 + s // 3], 0)),
                pl.BlockSpec(own.shape, lambda s, w: (0, 0, 0)),
                pl.BlockSpec(own.shape, lambda s, w: (0, 0, 0)),
            ]
            + more_specs,
            out_specs=[pl.BlockSpec((1, tall, features), out_map(r)) for r in range(3)],
            scratch_shapes=[pltpu.VMEM((3, frames, 2 * span + 2 * cols, features), BF)],
        ),
        out_shape=[jax.ShapeDtypeStruct((3, tall, features), kind) for _ in range(3)],
        compiler_params=params(24),
        cost_estimate=cost(
            2 * 9 * rows * 2 * frames * span * features,
            9 * rows * features * jnp.dtype(kind).itemsize,
        ),
        name=name,
    )(where, lat, own, other, *more)


def bit_of(value, kind):
    if kind == 0:
        return value // 2
    return (value + 1) // 2 % 2


def swap_pairs(axis, step, size):
    pairs = []
    stride = STRIDES[axis]
    for device in range(size):
        tm, core = divmod(device, 2)
        value = tm // stride % RING
        partner = (value ^ 1) if (step + core) % 2 == 0 else (RING - 1 - value)
        pairs.append((device, (tm + (partner - value) * stride) * 2 + core))
    return pairs


def owners(order, core):
    found = []
    for n in range(RING**3):
        place = 0
        for k, axis in enumerate(order):
            digit = n // RING ** (2 - k) % RING
            first, second = divmod(digit, 2)
            low, high = (second, first) if core == 0 else (first, second)
            value = 2 * low + (low ^ high)
            place += value * STRIDES[axis]
        found.append(2 * place + core)
    return np.array(found)


def one_hot(rows, width):
    return (rows[:, None] == np.arange(width)[None, :]).astype(np.float32)


def selections(channels):
    each = channels // (2 * RING**3)
    return np.stack(
        [
            one_hot((owners(ORDERS[0], c)[:, None] * each + np.arange(each)).reshape(-1), channels)
            for c in range(2)
        ]
    )


def reorders(channels):
    each = channels // (2 * RING**3)
    found = []
    for c in range(2):
        base = list(owners(ORDERS[0], c))
        for order in ORDERS[1:]:
            at = np.array([base.index(o) for o in owners(order, c)])
            rows = (at[:, None] * each + np.arange(each)).reshape(-1)
            found.append(one_hot(rows, channels // 2))
    return np.stack(found).reshape(2, 2, channels // 2, channels // 2)


def up_to(n, multiple):
    return -(-n // multiple) * multiple


def payload_rows(rows, more, has_loss):
    return 3 * up_to(rows, 16) + (LOSS if has_loss else 0) + up_to(more, 16)


def places(rows, has_loss, initial):
    if initial:
        tall = rows + EXTRA
        pieces = [(rows, EXTRA, 0), (tall + rows, EXTRA, EXTRA), (2 * tall + rows, 32, 2 * EXTRA)]
        return [0, tall, 2 * tall], 2 * tall + rows + 32, pieces
    slab = up_to(rows, 16)
    behind = 3 * slab + (LOSS if has_loss else 0)
    return [0, slab, 2 * slab], 3 * slab, [(behind, None, 0)]


def combine_kernel(rows, more, has_loss, initial, bit_ref, met_ref, sp_ref, tp_ref, *rest):
    if has_loss:
        loss_ref, send_ref, sp_out, tp_out, loss_out, full, full_more = rest
    else:
        send_ref, sp_out, tp_out, full, full_more = rest
    bit = bit_ref[0]
    slabs, loss_at, pieces = places(rows, has_loss, initial)

    def halve(ref, count, send_at, out_ref):
        part = count // 2
        sent = up_to(part, 16)
        kept = up_to(part, 8)
        if part % 16 == 0:
            mine = ref[pl.ds(pl.multiple_of(bit * part, part), part), :]
            theirs = ref[pl.ds(pl.multiple_of((1 - bit) * part, part), part), :]
        else:
            whole = ref[...]
            tall = whole.shape[0]
            mine = pltpu.roll(whole, (tall - bit * part) % tall, 0)[:kept]
            theirs = pltpu.roll(whole, (tall - (1 - bit) * part) % tall, 0)[:sent]
        send_ref[send_at : send_at + sent, :] = theirs.astype(send_ref.dtype)
        return mine

    next_slab = up_to(rows // 2, 16)
    for b in range(3):
        tall = full.shape[1]
        full[b] = sp_ref[b] + met_ref[slabs[b] : slabs[b] + tall, :].astype(F32)
        sp_out[b] = halve(full.at[b], rows, b * next_slab, sp_out)
    for at, count, to in pieces:
        count = full_more.shape[0] if count is None else count
        full_more[to : to + count, :] = tp_ref[to : to + count, :] + met_ref[
            at : at + count, :
        ].astype(F32)
    behind = 3 * next_slab
    if has_loss:
        loss = loss_ref[...] + joined(met_ref[loss_at : loss_at + LOSS, :].astype(F32))
        loss_out[...] = loss
        send_ref[behind : behind + LOSS, :] = stacked(loss, LOSS).astype(send_ref.dtype)
        behind += LOSS
    tp_out[...] = halve(full_more, more, behind, tp_out)


def combine(bit, met, sp, tp, loss, rows, more, initial, kind, name):
    has_loss = loss is not None
    width = met.shape[1]
    out_shape = [
        jax.ShapeDtypeStruct((payload_rows(rows // 2, more // 2, has_loss), width), kind),
        jax.ShapeDtypeStruct((3, up_to(rows // 2, 8), width), F32),
        jax.ShapeDtypeStruct((up_to(more // 2, 8), width), F32),
    ]
    operands = [bit, met, sp, tp]
    if has_loss:
        out_shape.append(jax.ShapeDtypeStruct((1, width), F32))
        operands.append(loss)
    vmem = pl.BlockSpec(memory_space=pltpu.VMEM)
    done = pl.pallas_call(
        functools.partial(combine_kernel, rows, more, has_loss, initial),
        in_specs=[pl.BlockSpec(memory_space=pltpu.SMEM)] + [vmem] * (len(operands) - 1),
        out_specs=[vmem] * len(out_shape),
        out_shape=out_shape,
        scratch_shapes=[pltpu.VMEM(sp.shape, F32), pltpu.VMEM(tp.shape, F32)],
        compiler_params=params(14),
        cost_estimate=cost(0, 8 * sp.size),
        name=name,
    )(*operands)
    return done if has_loss else (*done, None)


def on_device(clean, noise, timestep, spatial_weight, temporal_weight):
    frames, rows, cols, channels = clean.shape
    features = temporal_weight.shape[0]
    span = rows * cols
    blocks = lax.axis_size("tm")
    size = 2 * blocks
    tm = lax.axis_index("tm")
    core = lax.axis_index("space")
    both = ("tm", "space")
    step_value = timestep[0].astype(F32)
    angle = math.pi / 2.0 * (step_value + 1.0) / (STEPS + 1.0)
    signal = jnp.cos(angle)
    sigma = jnp.sin(angle)
    positions = frames * blocks * rows * 2 * cols
    scale = jnp.stack([signal, sigma, jnp.float32(math.sqrt(positions))])
    w_spatial = jnp.transpose(spatial_weight, (1, 2, 0, 3))
    w_temporal = jnp.transpose(temporal_weight, (1, 0, 2))

    def mix(c, n):
        return (signal * c.astype(F32) + sigma * n.astype(F32)).astype(BF)

    edge_at = (1 - core) * (rows - 1)
    edge = mix(
        lax.dynamic_slice_in_dim(clean, edge_at, 1, axis=1),
        lax.dynamic_slice_in_dim(noise, edge_at, 1, axis=1),
    )
    met = lax.ppermute(edge, "space", [(0, 1), (1, 0)]).reshape(frames, cols, channels)
    above = jnp.where(core == 0, jnp.zeros_like(met), met)
    below = jnp.where(core == 0, met, jnp.zeros_like(met))
    noisy = mix(clean, noise).reshape(frames, span, channels)
    cross = [(0, 1), (1, 0)]
    core_index = jnp.reshape(core, (1,)).astype(jnp.int32)
    act, der = spatial_forward(noisy, above, below, w_spatial)

    per_clip = CLIP // frames
    shift = CLIP // 4 // frames
    up = [(i, i + 1) for i in range(blocks - 1) if (i + 1 + shift) % per_clip != 0]
    down = [(j, i) for i, j in up]
    act_before = lax.ppermute(act[-1:], "tm", up)
    act_after = lax.ppermute(act[:1], "tm", down)
    lat_own, lat_send = selected_latent(core_index, noisy, jnp.asarray(selections(channels), BF))
    lat_other = lax.ppermute(lat_send, "space", cross)
    flat = (frames, span, channels)
    gp, loss_lanes = temporal_forward(
        scale, act, act_before, act_after, w_temporal, clean.reshape(flat), noise.reshape(flat)
    )
    gp_before = lax.ppermute(gp[-1:], "tm", up)
    gp_after = lax.ppermute(gp[:1], "tm", down)
    gp_other = lax.ppermute(gp, "space", cross)
    act_own, act_send = selected_act(
        core_index, act, act_before, act_after, jnp.asarray(selections(features), BF), loss_lanes
    )
    act_other = lax.ppermute(act_send, "space", cross)
    lat = arranged_latent(core_index, lat_own, lat_other, jnp.asarray(reorders(channels), BF))
    gh = temporal_backward(gp, gp_before, gp_after, w_temporal, der)
    gh_other = lax.ppermute(gh, "space", cross)

    bits = []
    for order in ORDERS:
        own = []
        for axis in order:
            value = tm // STRIDES[axis] % RING
            low, high = bit_of(value, 0), bit_of(value, 1)
            own.append(jnp.where(core == 0, high, low))
            own.append(jnp.where(core == 0, low, high))
        bits.append([b.astype(jnp.int32) for b in own])
    first_bits = jnp.stack([b[0] for b in bits])
    extra, extra_keep, loss = temporal_grad_local(
        jnp.concatenate([first_bits, core_index]),
        act_own,
        act_other,
        gp,
        gp_other,
        jnp.asarray(reorders(features), BF),
        loss_lanes,
    )
    sends = spatial_backward(
        jnp.concatenate([core_index, 1 - first_bits]), lat, gh, gh_other, extra, BF, "spatial_send"
    )
    keeps = spatial_backward(
        jnp.concatenate([core_index, first_bits]), lat, gh, gh_other, None, F32, "spatial_keep"
    )

    state = [
        (sends[t].reshape(-1, features), keeps[t], extra_keep[t], loss if t == 0 else None)
        for t in range(3)
    ]
    count, more = channels // 4, features // 4
    for step in range(6):
        met = [
            lax.ppermute(state[t][0], both, swap_pairs(ORDERS[t][step // 2], step, size))
            for t in range(3)
        ]
        if step == 5:
            break
        kind = BF if step < 4 else F32
        for t in range(3):
            _, sp, tp, total = state[t]
            bit = jnp.reshape(bits[t][step + 1], (1,))
            name = "combine_%d_%d" % (step, t)
            state[t] = combine(bit, met[t], sp, tp, total, count, more, step == 0, kind, name)
        count, more = count // 2, more // 2

    spatial_parts, temporal_parts = [], []
    for t in range(3):
        _, sp, tp, total = state[t]
        slabs, loss_at, ((behind, _, _),) = places(count, total is not None, False)
        spatial_parts.append(
            jnp.stack([sp[b, :count] + met[t][s : s + count] for b, s in enumerate(slabs)])
        )
        temporal_parts.append(tp[:more] + met[t][behind : behind + more])
        if total is not None:
            loss_sum = jnp.sum(total + joined(met[t][loss_at : loss_at + LOSS]))
    spatial_grad = jnp.transpose(jnp.stack(spatial_parts), (2, 0, 1, 3))
    temporal_grad = jnp.transpose(jnp.stack(temporal_parts), (1, 0, 2))
    return (loss_sum / (positions * features), spatial_grad, temporal_grad)


def solution(mesh):
    placed = (P("tm", "space", None, None), P("tm", "space", None, None), P(), P(), P())
    return jax.shard_map(
        on_device,
        mesh=mesh,
        in_specs=placed,
        out_specs=(P(), P(("tm", "space"), None, None, None), P(("tm", "space"), None, None)),
        check_vma=False,
    )
```

```python
import functools
import math

import jax
import jax.numpy as jnp
import numpy as np
from jax import lax
from jax.experimental import pallas as pl
from jax.experimental.pallas import tpu as pltpu
from jax.sharding import PartitionSpec as P

CLIP = 80
STEPS = 1000
BF = jnp.bfloat16
F32 = jnp.float32
MIB = 1 << 20
STRIDES = (16, 4, 1)
RING = 4
ORDERS = ((0, 1, 2), (1, 2, 0), (2, 0, 1))
LOSS = 16
EXTRA = 64


def params(mib):
    return pltpu.CompilerParams(vmem_limit_bytes=mib * MIB)


def in_hbm(x):
    return pltpu.with_memory_space_constraint(x, pltpu.HBM)


def in_vmem(x):
    return pltpu.with_memory_space_constraint(x, pltpu.VMEM)


def cost(flops, nbytes):
    return pl.CostEstimate(flops=int(flops), bytes_accessed=int(nbytes), transcendentals=0)


def tap_of(step):
    group = step // 3
    return jnp.where(group == 0, 1, jnp.where(group == 1, 0, 2)), step % 3


def spatial_forward_kernel(
    odd, x_ref, above_ref, below_ref, w_ref, act_ref, one_ref, two_ref, der_ref, xp, acc, taps, sems
):
    step = pl.program_id(0)
    first, second = tap_of(step)
    frames, span, channels = x_ref.shape
    cols = above_ref.shape[1]
    features = w_ref.shape[3]

    @pl.when(step == 0)
    def _():
        for k in range(9):
            row = (1, 0, 2)[k // 3]
            pltpu.make_async_copy(w_ref.at[row, k % 3], taps.at[k], sems.at[k]).start()
        xp[:, 0:cols, :] = above_ref[...]
        xp[:, cols : cols + span, :] = x_ref[...]
        xp[:, cols + span : span + 2 * cols, :] = below_ref[...]

    pltpu.make_async_copy(w_ref.at[first, second], taps.at[step], sems.at[step]).wait()
    start = pl.multiple_of(first * cols, cols)
    piece = xp[:, pl.ds(start, span), :].reshape(frames * span, channels)
    prod = jnp.dot(piece, taps[step], preferred_element_type=F32)

    @pl.when(step < 3)
    def _():
        acc[second] = prod

    @pl.when(step >= 3)
    def _():
        acc[second] += prod

    @pl.when(step == 8)
    def _():
        col = lax.broadcasted_iota(jnp.int32, (span, features), 0) % cols

        def one(f, carry):
            rows = pl.ds(pl.multiple_of(f * span, span), span)
            left = jnp.where(col == 0, 0.0, pltpu.roll(acc[0, rows, :], 1, 0))
            right = jnp.where(col == cols - 1, 0.0, pltpu.roll(acc[2, rows, :], span - 1, 0))
            hidden = left + acc[1, rows, :] + right
            sig = 1.0 / (1.0 + jnp.exp(-hidden))
            act_ref[f] = (hidden * sig).astype(BF)
            der_ref[f] = sig * (1.0 + hidden * (1.0 - sig))
            return carry

        lax.fori_loop(0, frames, one, 0)
        one_ref[0] = act_ref[(1 - odd[0]) * (frames - 1)]
        two_ref[0] = act_ref[odd[0] * (frames - 1)]


def spatial_forward(odd, x, above, below, weight):
    frames, span, channels = x.shape
    cols = above.shape[1]
    features = weight.shape[3]
    whole = lambda s: (0, 0, 0)
    return pl.pallas_call(
        spatial_forward_kernel,
        grid=(9,),
        in_specs=[
            pl.BlockSpec(memory_space=pltpu.SMEM),
            pl.BlockSpec(x.shape, whole),
            pl.BlockSpec(above.shape, whole),
            pl.BlockSpec(below.shape, whole),
            pl.BlockSpec(memory_space=pltpu.HBM),
        ],
        out_specs=[
            pl.BlockSpec((frames, span, features), whole),
            pl.BlockSpec((1, span, features), whole),
            pl.BlockSpec((1, span, features), whole),
            pl.BlockSpec((frames, span, features), whole),
        ],
        out_shape=[
            jax.ShapeDtypeStruct((frames, span, features), BF),
            jax.ShapeDtypeStruct((1, span, features), BF),
            jax.ShapeDtypeStruct((1, span, features), BF),
            pltpu.VMEM((frames, span, features), F32),
        ],
        scratch_shapes=[
            pltpu.VMEM((frames, span + 2 * cols, channels), BF),
            pltpu.VMEM((3, frames * span, features), F32),
            pltpu.VMEM((9, channels, features), BF),
            pltpu.SemaphoreType.DMA((9,)),
        ],
        compiler_params=params(40),
        cost_estimate=cost(
            2 * 9 * frames * span * channels * features, 2 * 9 * channels * features
        ),
        name="spatial_forward",
    )(odd, x, above, below, in_hbm(weight))


def temporal_forward_kernel(
    scale, odd, act_ref, one_ref, two_ref, w_ref, clean_ref, noise_ref, *rest
):
    gp_ref, one_out, two_out, loss_ref, rim_ref, ap = rest[1:]
    frames, span, features = act_ref.shape
    factor = scale[2]
    ap[(1 - odd[0]) * (frames + 1)] = one_ref[0]
    ap[odd[0] * (frames + 1)] = two_ref[0]
    ap[1 : frames + 1] = act_ref[...]
    pred = jnp.zeros((frames * span, features), F32)
    for tap in range(3):
        pred = pred + jnp.dot(
            ap[tap : tap + frames].reshape(frames * span, features),
            w_ref[tap],
            preferred_element_type=F32,
        )
    clean = clean_ref[...].reshape(frames * span, features).astype(F32)
    noise = noise_ref[...].reshape(frames * span, features).astype(F32)
    diff = pred - (scale[0] * noise - scale[1] * clean)
    gp_ref[...] = (2.0 * diff / factor).astype(BF).reshape(frames, span, features)
    one_out[0] = gp_ref[(1 - odd[0]) * (frames - 1)]
    two_out[0] = gp_ref[odd[0] * (frames - 1)]
    loss = jnp.sum(diff * diff, axis=0, keepdims=True)
    loss_ref[...] = loss
    rim_ref[0:span, :] = ap[0]
    rim_ref[span : 2 * span, :] = ap[frames + 1]
    rim_ref[2 * span :, :] = stacked(loss, LOSS).astype(BF)


def temporal_forward(scale, odd, act, one, two, weight, clean, noise, token):
    frames, span, features = act.shape
    whole = lambda i: (0, 0, 0)
    head = pl.BlockSpec((frames, span, features), whole)
    halo = pl.BlockSpec((1, span, features), whole)
    return pl.pallas_call(
        temporal_forward_kernel,
        grid=(1,),
        in_specs=[
            pl.BlockSpec(memory_space=pltpu.SMEM),
            pl.BlockSpec(memory_space=pltpu.SMEM),
            head,
            halo,
            halo,
            pl.BlockSpec(weight.shape, whole),
            head,
            head,
            pl.BlockSpec(memory_space=pl.ANY),
        ],
        out_specs=[
            head,
            halo,
            halo,
            pl.BlockSpec((1, features), lambda i: (0, 0)),
            pl.BlockSpec((2 * span + LOSS, features), lambda i: (0, 0)),
        ],
        out_shape=[
            jax.ShapeDtypeStruct((frames, span, features), BF),
            jax.ShapeDtypeStruct((1, span, features), BF),
            jax.ShapeDtypeStruct((1, span, features), BF),
            jax.ShapeDtypeStruct((1, features), F32),
            jax.ShapeDtypeStruct((2 * span + LOSS, features), BF),
        ],
        scratch_shapes=[pltpu.VMEM((frames + 2, span, features), BF)],
        compiler_params=params(16),
        cost_estimate=cost(2 * 3 * frames * span * features * features, 6 * features * features),
        name="temporal_forward",
    )(scale, odd, act, one, two, weight, clean, noise, token)


def thirds(value):
    high = value.astype(BF)
    rest = value - high.astype(F32)
    middle = rest.astype(BF)
    return high, middle, (rest - middle.astype(F32)).astype(BF)


def stacked(value, rows):
    high, middle, low = thirds(value)
    row = lax.broadcasted_iota(jnp.int32, (rows, value.shape[1]), 0)
    parts = [p.astype(F32) for p in (high, middle, low)]
    return jnp.where(
        row == 0, parts[0], jnp.where(row == 1, parts[1], jnp.where(row == 2, parts[2], 0.0))
    )


def joined(rows):
    return (rows[0:1] + rows[1:2]) + rows[2:3]


def temporal_grad_kernel(
    bits_ref,
    act_ref,
    rim_ref,
    act_other_ref,
    rim_other_ref,
    gp_ref,
    gp_other_ref,
    choice_ref,
    reorder_ref,
    loss_ref,
    send_ref,
    keep_0,
    keep_1,
    keep_2,
    sum_ref,
    padded,
    chosen,
    gps,
    total,
):
    frames, span, features = gp_ref.shape
    core = bits_ref[3]
    half = features // 2
    rows = half // 2
    loss = loss_ref[...] + joined(rim_other_ref[2 * span : 2 * span + LOSS, :].astype(F32))
    sum_ref[...] = loss
    for which, (act, rim) in enumerate(((act_ref, rim_ref), (act_other_ref, rim_other_ref))):
        padded[which, 0] = rim[0:span, :]
        padded[which, 1 : frames + 1] = act[...]
        padded[which, frames + 1] = rim[span : 2 * span, :]
    chosen[...] = lax.dot_general(
        choice_ref[core],
        padded[...].reshape(-1, features),
        (((1,), (1,)), ((), ())),
        preferred_element_type=F32,
    ).astype(BF)
    gps[0:frames] = gp_ref[...]
    gps[frames:] = gp_other_ref[...]
    for tap, keep in enumerate((keep_0, keep_1, keep_2)):
        here = tap * span
        there = here + (frames + 2) * span
        long = frames * span
        left = jnp.concatenate(
            [chosen[:, here : here + long], chosen[:, there : there + long]], axis=1
        )
        if tap > 0:
            left = jnp.dot(
                reorder_ref[core, tap - 1], left, preferred_element_type=F32
            ).astype(BF)
        total[...] = jnp.dot(
            left, gps[...].reshape(2 * long, features), preferred_element_type=F32
        )
        bit = bits_ref[tap]
        kept = pl.ds(pl.multiple_of(bit * rows, rows), rows)
        sent = pl.ds(pl.multiple_of((1 - bit) * rows, rows), rows)
        keep[...] = total[kept, :]
        send_ref[tap, 0:rows, :] = total[sent, :].astype(BF)
        send_ref[tap, rows : rows + LOSS, :] = stacked(loss, LOSS).astype(BF)
        send_ref[tap, rows + LOSS :, :] = jnp.zeros(
            (send_ref.shape[1] - rows - LOSS, features), BF
        )


def temporal_grad_local(
    bits, act, rim, act_other, rim_other, gp, gp_other, choice, reorder, loss
):
    frames, span, features = gp.shape
    rows = features // 4
    vmem = pl.BlockSpec(memory_space=pltpu.VMEM)
    return pl.pallas_call(
        temporal_grad_kernel,
        in_specs=[pl.BlockSpec(memory_space=pltpu.SMEM)]
        + [vmem] * 9,
        out_shape=[
            pltpu.VMEM((3, 3 * EXTRA, features), BF),
            *[pltpu.HBM((rows, features), F32) for _ in range(3)],
            pltpu.VMEM((1, features), F32),
        ],
        out_specs=[vmem] * 5,
        scratch_shapes=[
            pltpu.VMEM((2, frames + 2, span, features), BF),
            pltpu.VMEM((features // 2, 2 * (frames + 2) * span), BF),
            pltpu.VMEM((2 * frames, span, features), BF),
            pltpu.VMEM((features // 2, features), F32),
        ],
        compiler_params=params(20),
        cost_estimate=cost(
            2 * 4 * frames * span * features * features, 6 * features * features
        ),
        name="temporal_grad",
    )(bits, act, rim, act_other, rim_other, gp, gp_other, choice, reorder, loss)


def temporal_backward_kernel(
    odd, gp_ref, one_ref, two_ref, w_ref, der_ref, token, out_ref, pad
):
    frames, span, features = gp_ref.shape
    pad[(1 - odd[0]) * (frames + 1)] = one_ref[0]
    pad[odd[0] * (frames + 1)] = two_ref[0]
    pad[1 : frames + 1] = gp_ref[...]
    total = jnp.zeros((frames * span, features), F32)
    for tap in range(3):
        total = total + lax.dot_general(
            pad[2 - tap : 2 - tap + frames].reshape(frames * span, features),
            w_ref[tap],
            (((1,), (1,)), ((), ())),
            preferred_element_type=F32,
        )
    der = der_ref[...].reshape(frames * span, features)
    out_ref[...] = (total * der).astype(BF).reshape(frames, span, features)


def temporal_backward(odd, gp, one, two, weight, der, token):
    frames, span, features = gp.shape
    return pl.pallas_call(
        temporal_backward_kernel,
        in_specs=[pl.BlockSpec(memory_space=pltpu.SMEM)]
        + [pl.BlockSpec(memory_space=pltpu.VMEM)] * 5
        + [pl.BlockSpec(memory_space=pl.ANY)],
        out_shape=pltpu.VMEM((frames, span, features), BF),
        scratch_shapes=[pltpu.VMEM((frames + 2, span, features), BF)],
        compiler_params=params(12),
        cost_estimate=cost(2 * 3 * frames * span * features * features, 6 * features * features),
        name="temporal_backward",
    )(odd, gp, one, two, weight, der, token)


def select_latent_kernel(core_ref, x_ref, choice_ref, token, own_ref, send_ref):
    core = core_ref[0]
    x = x_ref[...].reshape(-1, x_ref.shape[2])
    for out, which in ((send_ref, 1 - core), (own_ref, core)):
        out[...] = lax.dot_general(
            choice_ref[which], x, (((1,), (1,)), ((), ())), preferred_element_type=F32
        ).astype(BF)


def selected_latent(core, x, choice, token):
    frames, span, channels = x.shape
    shape = jax.ShapeDtypeStruct((channels // 2, frames * span), BF)
    vmem = pl.BlockSpec(memory_space=pltpu.VMEM)
    return pl.pallas_call(
        select_latent_kernel,
        in_specs=[
            pl.BlockSpec(memory_space=pltpu.SMEM),
            vmem,
            vmem,
            pl.BlockSpec(memory_space=pl.ANY),
        ],
        out_specs=[vmem, vmem],
        out_shape=[shape, shape],
        compiler_params=params(16),
        cost_estimate=cost(2 * frames * span * channels * channels, 4 * channels * channels),
        name="select_latent",
    )(core, x, choice, token)


def arrange_latent_kernel(
    core_ref, own_ref, other_ref, reorder_ref, token, out_ref, reorder, sem
):
    core = core_ref[0]
    copy = pltpu.make_async_copy(reorder_ref.at[core], reorder, sem)
    copy.start()
    frames = 5
    span = own_ref.shape[1] // frames
    for f in range(frames):
        here = pl.multiple_of((2 * f + core) * span, span)
        there = pl.multiple_of((2 * f + 1 - core) * span, span)
        out_ref[0, :, pl.ds(here, span)] = own_ref[:, f * span : (f + 1) * span]
        out_ref[0, :, pl.ds(there, span)] = other_ref[:, f * span : (f + 1) * span]
    copy.wait()
    for third in range(1, 3):
        out_ref[third] = jnp.dot(
            reorder[third - 1], out_ref[0], preferred_element_type=F32
        ).astype(BF)


def arranged_latent(core, own, other, reorder, token):
    half, positions = own.shape
    vmem = pl.BlockSpec(memory_space=pltpu.VMEM)
    return pl.pallas_call(
        arrange_latent_kernel,
        in_specs=[
            pl.BlockSpec(memory_space=pltpu.SMEM),
            vmem,
            vmem,
            pl.BlockSpec(memory_space=pltpu.HBM),
            pl.BlockSpec(memory_space=pl.ANY),
        ],
        out_specs=vmem,
        out_shape=pltpu.VMEM((3, half, 2 * positions), BF),
        scratch_shapes=[pltpu.VMEM(reorder.shape[1:], BF), pltpu.SemaphoreType.DMA],
        compiler_params=params(16),
        cost_estimate=cost(8 * half * half * positions, 20 * half * positions),
        name="arrange_latent",
    )(core, own, other, in_hbm(reorder), token)


def shifted_gradient(core, own_ref, other_ref, pad):
    frames, span, features = own_ref.shape
    cols = (pad.shape[2] - 2 * span) // 2
    col = lax.broadcasted_iota(jnp.int32, (span, features), 0) % cols
    rim = jnp.zeros((cols, features), BF)

    def one(f, carry):
        for b in range(3):
            pad[b, f, 0:cols, :] = rim
            pad[b, f, cols + 2 * span : 2 * cols + 2 * span, :] = rim
        for ref, place in ((own_ref, core), (other_ref, 1 - core)):
            rows = pl.ds(pl.multiple_of(cols + place * span, cols), span)
            here = ref[f]
            wide = here.astype(F32)
            later = jnp.where(col == cols - 1, 0.0, pltpu.roll(wide, span - 1, 0))
            sooner = jnp.where(col == 0, 0.0, pltpu.roll(wide, 1, 0))
            pad[0, f, rows, :] = later.astype(BF)
            pad[1, f, rows, :] = here
            pad[2, f, rows, :] = sooner.astype(BF)
        return carry

    lax.fori_loop(0, frames, one, 0)


def gradient_rows(where, lat_ref, pad, outs):
    frames = pad.shape[1]
    cols = 16
    span = pad.shape[2] // 2 - cols
    height = lat_ref.shape[1] // 2
    for first in range(3):
        rows = pl.ds(pl.multiple_of(where[1 + first] * height, height), height)
        start = (2 - first) * cols
        for second in range(3):
            grad = pad[second, :, start : start + 2 * span, :]
            outs[first][second, 0:height, :] = jnp.dot(
                lat_ref[first, rows, :],
                grad.reshape(2 * frames * span, -1),
                preferred_element_type=F32,
            ).astype(outs[first].dtype)


def spatial_send_kernel(where, lat_ref, own_ref, other_ref, extra_ref, *outs):
    outs, pad = outs[:3], outs[3]
    shifted_gradient(where[0], own_ref, other_ref, pad)
    for first in range(3):
        for second in range(3):
            outs[first][second, lat_ref.shape[1] // 2 :, :] = extra_ref[
                first, second * EXTRA : (second + 1) * EXTRA, :
            ]
    gradient_rows(where, lat_ref, pad, outs)


def spatial_keep_kernel(where, lat_ref, own_ref, other_ref, *outs):
    outs, pad = outs[:3], outs[3]
    shifted_gradient(where[0], own_ref, other_ref, pad)
    gradient_rows(where, lat_ref, pad, outs)


def spatial_send(where, lat, own, other, extra):
    frames, span, features = own.shape
    rows = lat.shape[1] // 2
    cols = 16
    vmem = pl.BlockSpec(memory_space=pltpu.VMEM)
    return pl.pallas_call(
        spatial_send_kernel,
        in_specs=[pl.BlockSpec(memory_space=pltpu.SMEM)] + [vmem] * 4,
        out_specs=[vmem] * 3,
        out_shape=[pltpu.VMEM((3, rows + EXTRA, features), BF)] * 3,
        scratch_shapes=[pltpu.VMEM((3, frames, 2 * span + 2 * cols, features), BF)],
        compiler_params=params(24),
        cost_estimate=cost(
            2 * 9 * rows * 2 * frames * span * features, 2 * 9 * rows * features
        ),
        name="spatial_send",
    )(where, in_vmem(lat), own, other, in_vmem(extra))


def spatial_keep(where, lat, own, other):
    frames, span, features = own.shape
    rows = lat.shape[1] // 2
    cols = 16
    vmem = pl.BlockSpec(memory_space=pltpu.VMEM)
    return pl.pallas_call(
        spatial_keep_kernel,
        in_specs=[pl.BlockSpec(memory_space=pltpu.SMEM)]
        + [vmem] * 3,
        out_specs=[vmem] * 3,
        out_shape=[pltpu.HBM((3, rows, features), F32)] * 3,
        scratch_shapes=[pltpu.VMEM((3, frames, 2 * span + 2 * cols, features), BF)],
        compiler_params=params(24),
        cost_estimate=cost(1, 1),
        name="spatial_keep",
    )(where, in_vmem(lat), own, other)


def bit_of(value, kind):
    if kind == 0:
        return value // 2
    return (value + 1) // 2 % 2


def swap_pairs(axis, step, size):
    pairs = []
    stride = STRIDES[axis]
    for device in range(size):
        tm, core = divmod(device, 2)
        value = tm // stride % RING
        partner = (value ^ 1) if (step + core) % 2 == 0 else (RING - 1 - value)
        pairs.append((device, (tm + (partner - value) * stride) * 2 + core))
    return pairs


def owners(order, core):
    found = []
    for n in range(RING**3):
        place = 0
        for k, axis in enumerate(order):
            digit = n // RING ** (2 - k) % RING
            first, second = divmod(digit, 2)
            low, high = (second, first) if core == 0 else (first, second)
            value = 2 * low + (low ^ high)
            place += value * STRIDES[axis]
        found.append(2 * place + core)
    return np.array(found)


def one_hot(rows, width):
    return (rows[:, None] == np.arange(width)[None, :]).astype(np.float32)


def selections(channels):
    each = channels // (2 * RING**3)
    return np.stack(
        [
            one_hot((owners(ORDERS[0], c)[:, None] * each + np.arange(each)).reshape(-1), channels)
            for c in range(2)
        ]
    )


def reorders(channels):
    each = channels // (2 * RING**3)
    found = []
    for c in range(2):
        base = list(owners(ORDERS[0], c))
        for order in ORDERS[1:]:
            at = np.array([base.index(o) for o in owners(order, c)])
            rows = (at[:, None] * each + np.arange(each)).reshape(-1)
            found.append(one_hot(rows, channels // 2))
    return np.stack(found).reshape(2, 2, channels // 2, channels // 2)


def up_to(n, multiple):
    return -(-n // multiple) * multiple


def payload_rows(rows, more, has_loss):
    return 3 * up_to(rows, 16) + (LOSS if has_loss else 0) + up_to(more, 16)


def places(rows, has_loss):
    slab = up_to(rows, 16)
    return [0, slab, 2 * slab], 3 * slab, 3 * slab + (LOSS if has_loss else 0)


def halve(ref, bit, count, send_ref, send_at):
    part = count // 2
    sent = up_to(part, 16)
    kept = up_to(part, 8)
    if part % 16 == 0:
        mine = ref[pl.ds(pl.multiple_of(bit * part, part), part), :]
        theirs = ref[pl.ds(pl.multiple_of((1 - bit) * part, part), part), :]
    else:
        whole = ref[...]
        tall = whole.shape[0]
        mine = pltpu.roll(whole, (tall - bit * part) % tall, 0)[:kept]
        theirs = pltpu.roll(whole, (tall - (1 - bit) * part) % tall, 0)[:sent]
    send_ref[send_at : send_at + sent, :] = theirs.astype(send_ref.dtype)
    return mine


def combine_early_kernel(step, has_loss, bits, *refs):
    refs = list(refs)
    keep_ref, mets = refs[0], refs[1 : 2 + step]
    refs = refs[2 + step :]
    tp_ref = refs.pop(0)
    loss_ref = refs.pop(0) if has_loss else None
    send_ref = refs.pop(0)
    sp_out = refs.pop(0) if step == 2 else None
    tp_out = refs.pop(0)
    loss_out = refs.pop(0) if has_loss else None
    full_more = refs.pop(0)
    full = refs.pop(0) if step == 2 else None
    region, extra_buf, keep_buf, tp_buf, sems = refs
    rows = keep_ref.shape[1]
    half, quarter = rows // 2, rows // 4
    if step == 0:
        count, offsets = half, [(1 - bits[1]) * half]
    elif step == 1:
        count = quarter
        offsets = [bits[1] * half + (1 - bits[2]) * quarter, (1 - bits[2]) * quarter]
    else:
        count = quarter
        offsets = [bits[1] * half + bits[2] * quarter, bits[2] * quarter, 0]

    at = pl.multiple_of(offsets[0], count)
    copies = [
        pltpu.make_async_copy(keep_ref.at[:, pl.ds(at, count), :], keep_buf, sems.at[0]),
        pltpu.make_async_copy(mets[0].at[:, pl.ds(at, count), :], region, sems.at[1]),
    ]
    if step == 0:
        copies += [
            pltpu.make_async_copy(mets[0].at[:, pl.ds(rows, EXTRA), :], extra_buf, sems.at[2]),
            pltpu.make_async_copy(tp_ref, tp_buf, sems.at[3]),
        ]
        tp_ref = tp_buf
    for c in copies:
        c.start()
    for c in copies:
        c.wait()

    tall = full_more.shape[0]
    if step == 0:
        extra = extra_buf[...].reshape(3 * EXTRA, keep_ref.shape[2]).astype(F32)
        arrived, met_loss = extra[:tall], extra[tall : tall + LOSS]
    else:
        extra = mets[step][3 * (rows >> step) :, :].astype(F32)
        skip = LOSS if has_loss else 0
        arrived, met_loss = extra[skip : skip + tall], extra[:LOSS]
    full_more[...] = tp_ref[...] + arrived
    slab = up_to(rows >> (step + 1), 16)
    for b in range(3):
        total = keep_buf[b] + region[b].astype(F32)
        for k in range(1, step + 1):
            here = pl.multiple_of(b * (rows >> k) + offsets[k], count)
            total = total + mets[k][pl.ds(here, count), :].astype(F32)
        if step < 2:
            send_ref[b * slab : (b + 1) * slab, :] = total.astype(BF)
        else:
            full[b] = total
            sp_out[b] = halve(full.at[b], bits[3], count, send_ref, b * slab)
    behind = 3 * slab
    if has_loss:
        loss = loss_ref[...] + joined(met_loss)
        loss_out[...] = loss
        send_ref[behind : behind + LOSS, :] = stacked(loss, LOSS).astype(BF)
        behind += LOSS
    tp_out[...] = halve(full_more, bits[step + 1], 2 * (rows // 4 >> step), send_ref, behind)


def combine_early(step, bits, keep, mets, tp, loss, name):
    has_loss = loss is not None
    rows, width = keep.shape[1:]
    more = rows // 2 >> step
    half = rows >> (step + 1)
    vmem = pl.BlockSpec(memory_space=pltpu.VMEM)
    hbm = pl.BlockSpec(memory_space=pltpu.HBM)
    out_shape = [pltpu.VMEM((payload_rows(half, more // 2, has_loss), width), BF)]
    if step == 2:
        out_shape.append(pltpu.VMEM((3, up_to(half, 8), width), F32))
    out_shape.append(pltpu.VMEM((up_to(more // 2, 8), width), F32))
    if has_loss:
        out_shape.append(pltpu.VMEM((1, width), F32))
    scratch = [pltpu.VMEM((more, width), F32)]
    if step == 2:
        scratch.append(pltpu.VMEM((3, rows // 4, width), F32))
    scratch += [
        pltpu.VMEM((3, rows // 2 if step == 0 else rows // 4, width), BF),
        pltpu.VMEM((3, EXTRA, width), BF),
        pltpu.VMEM((3, rows // 2 if step == 0 else rows // 4, width), F32),
        pltpu.VMEM((rows // 2, width), F32),
        pltpu.SemaphoreType.DMA((4,)),
    ]
    done = list(
        pl.pallas_call(
            functools.partial(combine_early_kernel, step, has_loss),
            in_specs=[
                pl.BlockSpec(memory_space=pltpu.SMEM),
                hbm,
                hbm,
            ]
            + [vmem] * (len(mets) - 1)
            + [hbm if step == 0 else vmem]
            + [vmem] * has_loss,
            out_specs=[vmem] * len(out_shape),
            out_shape=out_shape,
            scratch_shapes=scratch,
            compiler_params=params(12),
            cost_estimate=cost(0, 8 * rows * width),
            name=name,
        )(
            bits,
            in_hbm(keep),
            in_hbm(mets[0]),
            *[in_vmem(x) for x in mets[1:]],
            in_hbm(tp) if step == 0 else in_vmem(tp),
            *([in_vmem(loss)] if has_loss else []),
        )
    )
    send = done.pop(0)
    sp = done.pop(0) if step == 2 else None
    tp = done.pop(0)
    return send, sp, tp, (done.pop(0) if has_loss else None)


def combine_kernel(rows, more, has_loss, bit_ref, met_ref, sp_ref, tp_ref, *rest):
    if has_loss:
        loss_ref, send_ref, sp_out, tp_out, loss_out, full, full_more = rest
    else:
        send_ref, sp_out, tp_out, full, full_more = rest
    bit = bit_ref[0]
    slabs, loss_at, behind = places(rows, has_loss)
    next_slab = up_to(rows // 2, 16)
    for b in range(3):
        tall = full.shape[1]
        full[b] = sp_ref[b] + met_ref[slabs[b] : slabs[b] + tall, :].astype(F32)
        sp_out[b] = halve(full.at[b], bit, rows, send_ref, b * next_slab)
    tall = full_more.shape[0]
    full_more[...] = tp_ref[...] + met_ref[behind : behind + tall, :].astype(F32)
    behind = 3 * next_slab
    if has_loss:
        loss = loss_ref[...] + joined(met_ref[loss_at : loss_at + LOSS, :].astype(F32))
        loss_out[...] = loss
        send_ref[behind : behind + LOSS, :] = stacked(loss, LOSS).astype(send_ref.dtype)
        behind += LOSS
    tp_out[...] = halve(full_more, bit, more, send_ref, behind)


def combine(bit, met, sp, tp, loss, rows, more, name):
    has_loss = loss is not None
    width = met.shape[1]
    out_shape = [
        pltpu.VMEM((payload_rows(rows // 2, more // 2, has_loss), width), BF),
        pltpu.VMEM((3, up_to(rows // 2, 8), width), F32),
        pltpu.VMEM((up_to(more // 2, 8), width), F32),
    ]
    operands = [bit, in_vmem(met), in_vmem(sp), in_vmem(tp)]
    if has_loss:
        out_shape.append(pltpu.VMEM((1, width), F32))
        operands.append(in_vmem(loss))
    vmem = pl.BlockSpec(memory_space=pltpu.VMEM)
    done = pl.pallas_call(
        functools.partial(combine_kernel, rows, more, has_loss),
        in_specs=[pl.BlockSpec(memory_space=pltpu.SMEM)] + [vmem] * (len(operands) - 1),
        out_specs=[vmem] * len(out_shape),
        out_shape=out_shape,
        scratch_shapes=[pltpu.VMEM(sp.shape, F32), pltpu.VMEM(tp.shape, F32)],
        compiler_params=params(12),
        cost_estimate=cost(0, 8 * sp.size),
        name=name,
    )(*operands)
    return done if has_loss else (*done, None)


def on_device(clean, noise, timestep, spatial_weight, temporal_weight):
    frames, rows, cols, channels = clean.shape
    features = temporal_weight.shape[0]
    span = rows * cols
    blocks = lax.axis_size("tm")
    size = 2 * blocks
    tm = lax.axis_index("tm")
    core = lax.axis_index("space")
    both = ("tm", "space")
    step_value = timestep[0].astype(F32)
    angle = math.pi / 2.0 * (step_value + 1.0) / (STEPS + 1.0)
    signal = jnp.cos(angle)
    sigma = jnp.sin(angle)
    positions = frames * blocks * rows * 2 * cols
    scale = jnp.stack([signal, sigma, jnp.float32(math.sqrt(positions))])
    w_spatial = jnp.transpose(spatial_weight, (1, 2, 0, 3))
    w_temporal = jnp.transpose(temporal_weight, (1, 0, 2))

    def mix(c, n):
        return (signal * c.astype(F32) + sigma * n.astype(F32)).astype(BF)

    edge_at = (1 - core) * (rows - 1)
    edge = mix(
        lax.dynamic_slice_in_dim(clean, edge_at, 1, axis=1),
        lax.dynamic_slice_in_dim(noise, edge_at, 1, axis=1),
    )
    met = lax.ppermute(edge, "space", [(0, 1), (1, 0)]).reshape(frames, cols, channels)
    above = jnp.where(core == 0, jnp.zeros_like(met), met)
    below = jnp.where(core == 0, met, jnp.zeros_like(met))
    noisy = mix(clean, noise).reshape(frames, span, channels)
    cross = [(0, 1), (1, 0)]
    core_index = jnp.reshape(core, (1,)).astype(jnp.int32)
    odd = jnp.reshape(tm % 2, (1,)).astype(jnp.int32)
    act, act_one, act_two, der = spatial_forward(odd, noisy, above, below, w_spatial)

    per_clip = CLIP // frames
    shift = CLIP // 4 // frames
    swaps = []
    for low in range(2):
        pairs = [(i, i + 1) for i in range(low, blocks - 1, 2) if (i + 1 + shift) % per_clip != 0]
        swaps.append(pairs + [(j, i) for i, j in pairs])
    act_one = lax.ppermute(act_one, "tm", swaps[0])
    act_two = lax.ppermute(act_two, "tm", swaps[1])
    act_other = lax.ppermute(act, "space", cross)
    lat_own, lat_send = selected_latent(
        core_index, noisy, jnp.asarray(selections(channels), BF), der
    )
    lat_other = lax.ppermute(lat_send, "space", cross)
    flat = (frames, span, channels)
    gp, gp_one, gp_two, loss_lanes, rim = temporal_forward(
        scale,
        odd,
        act,
        act_one,
        act_two,
        w_temporal,
        clean.reshape(flat),
        noise.reshape(flat),
        lat_own,
    )
    gp_one = lax.ppermute(gp_one, "tm", swaps[0])
    gp_two = lax.ppermute(gp_two, "tm", swaps[1])
    gp_other = lax.ppermute(gp, "space", cross)
    rim_other = lax.ppermute(rim, "space", cross)
    bits = []
    for order in ORDERS:
        own = []
        for axis in order:
            value = tm // STRIDES[axis] % RING
            low, high = bit_of(value, 0), bit_of(value, 1)
            own.append(jnp.where(core == 0, high, low))
            own.append(jnp.where(core == 0, low, high))
        bits.append([b.astype(jnp.int32) for b in own])
    first_bits = jnp.stack([b[0] for b in bits])
    extra, *more_keeps, loss = temporal_grad_local(
        jnp.concatenate([first_bits, core_index]),
        act,
        rim,
        act_other,
        rim_other,
        gp,
        gp_other,
        jnp.asarray(selections(features), BF),
        jnp.asarray(reorders(features), BF),
        loss_lanes,
    )
    gh = temporal_backward(odd, gp, gp_one, gp_two, w_temporal, der, loss)
    gh_other = lax.ppermute(gh, "space", cross)
    lat = arranged_latent(
        core_index, lat_own, lat_other, jnp.asarray(reorders(channels), BF), gh
    )
    sends = spatial_send(
        jnp.concatenate([core_index, 1 - first_bits]), lat, gh, gh_other, extra
    )
    keeps = spatial_keep(jnp.concatenate([core_index, first_bits]), lat, gh, gh_other)

    state = [
        (sends[t].reshape(-1, features), None, more_keeps[t], loss if t == 0 else None)
        for t in range(3)
    ]
    arrived = [[], [], []]
    count, more = channels // 4, features // 4
    for step in range(6):
        met = [
            lax.ppermute(state[t][0], both, swap_pairs(ORDERS[t][step // 2], step, size))
            for t in range(3)
        ]
        if step == 5:
            break
        for t in range(3):
            _, sp, tp, total = state[t]
            name = "combine_%d_%d" % (step, t)
            if step < 3:
                arrived[t].append(met[t].reshape(sends[t].shape) if step == 0 else met[t])
                state[t] = combine_early(
                    step, jnp.stack(bits[t]), keeps[t], arrived[t], tp, total, name
                )
            else:
                bit = jnp.reshape(bits[t][step + 1], (1,))
                state[t] = combine(bit, met[t], sp, tp, total, count, more, name)
        count, more = count // 2, more // 2

    spatial_parts, temporal_parts = [], []
    for t in range(3):
        _, sp, tp, total = state[t]
        slabs, loss_at, behind = places(count, total is not None)
        spatial_parts.append(
            jnp.stack(
                [sp[b, :count] + met[t][s : s + count].astype(F32) for b, s in enumerate(slabs)]
            )
        )
        temporal_parts.append(tp[:more] + met[t][behind : behind + more].astype(F32))
        if total is not None:
            loss_sum = jnp.sum(total + joined(met[t][loss_at : loss_at + LOSS].astype(F32)))
    spatial_grad = jnp.transpose(jnp.stack(spatial_parts), (2, 0, 1, 3))
    temporal_grad = jnp.transpose(jnp.stack(temporal_parts), (1, 0, 2))
    return (loss_sum / (positions * features), spatial_grad, temporal_grad)


def solution(mesh):
    placed = (P("tm", "space", None, None), P("tm", "space", None, None), P(), P(), P())
    return jax.shard_map(
        on_device,
        mesh=mesh,
        in_specs=placed,
        out_specs=(P(), P(("tm", "space"), None, None, None), P(("tm", "space"), None, None)),
        check_vma=False,
    )
```

```python
import functools
import math

import jax
import jax.numpy as jnp
import numpy as np
from jax import lax
from jax.experimental import pallas as pl
from jax.experimental.pallas import tpu as pltpu
from jax.sharding import PartitionSpec as P

CLIP = 80
STEPS = 1000
BF = jnp.bfloat16
F32 = jnp.float32
MIB = 1 << 20
STRIDES = (16, 4, 1)
RING = 4
ORDERS = ((0, 1, 2), (1, 2, 0), (2, 0, 1))
LOSS = 16
EXTRA = 64


def params(mib):
    return pltpu.CompilerParams(vmem_limit_bytes=mib * MIB)


def in_hbm(x):
    return pltpu.with_memory_space_constraint(x, pltpu.HBM)


def in_vmem(x):
    return pltpu.with_memory_space_constraint(x, pltpu.VMEM)


def cost(flops, nbytes):
    return pl.CostEstimate(flops=int(flops), bytes_accessed=int(nbytes), transcendentals=0)


def spatial_forward_kernel(
    odd, x_ref, above_ref, below_ref, w_ref, act_ref, one_ref, two_ref, der_ref, xp, acc, taps, sems
):
    order = (1, 0, 2)
    step = pl.program_id(0)
    first = jnp.where(step == 0, 1, jnp.where(step == 1, 0, 2))
    frames, span, channels = x_ref.shape
    cols = above_ref.shape[1]
    features = w_ref.shape[3]
    wide = features // 256 * 256
    rest = features - wide

    @pl.when(step == 0)
    def _():
        for k in range(9):
            pltpu.make_async_copy(w_ref.at[order[k // 3], k % 3], taps.at[k], sems.at[k]).start()
        xp[:, 0:cols, :] = above_ref[...]
        xp[:, cols : cols + span, :] = x_ref[...]
        xp[:, cols + span : span + 2 * cols, :] = below_ref[...]
        acc[...] = jnp.zeros_like(acc)

    start = pl.multiple_of(first * cols, cols)
    piece = xp[:, pl.ds(start, span), :].reshape(frames * span, channels)
    for b in range(3):
        k = 3 * step + b
        pltpu.make_async_copy(w_ref.at[first, b], taps.at[k], sems.at[k]).wait()
        acc[b, :, 0:wide] += jnp.dot(piece, taps[k, :, 0:wide], preferred_element_type=F32)
    ends = jnp.concatenate([taps[3 * step + b, :, wide:] for b in range(3)], axis=1)
    prod = jnp.dot(piece, ends, preferred_element_type=F32)
    for b in range(3):
        acc[b, :, wide:] += prod[:, b * rest : (b + 1) * rest]

    @pl.when(step == 2)
    def _():
        col = lax.broadcasted_iota(jnp.int32, (span, features), 0) % cols

        def one(f, carry):
            rows = pl.ds(pl.multiple_of(f * span, span), span)
            left = jnp.where(col == 0, 0.0, pltpu.roll(acc[0, rows, :], 1, 0))
            right = jnp.where(col == cols - 1, 0.0, pltpu.roll(acc[2, rows, :], span - 1, 0))
            hidden = left + acc[1, rows, :] + right
            sig = 1.0 / (1.0 + jnp.exp(-hidden))
            act_ref[f] = (hidden * sig).astype(BF)
            der_ref[f] = sig * (1.0 + hidden * (1.0 - sig))
            return carry

        lax.fori_loop(0, frames, one, 0)
        one_ref[0] = act_ref[(1 - odd[0]) * (frames - 1)]
        two_ref[0] = act_ref[odd[0] * (frames - 1)]


def spatial_forward(odd, x, above, below, weight):
    frames, span, channels = x.shape
    cols = above.shape[1]
    features = weight.shape[3]
    whole = lambda s: (0, 0, 0)
    return pl.pallas_call(
        spatial_forward_kernel,
        grid=(3,),
        in_specs=[
            pl.BlockSpec(memory_space=pltpu.SMEM),
            pl.BlockSpec(x.shape, whole),
            pl.BlockSpec(above.shape, whole),
            pl.BlockSpec(below.shape, whole),
            pl.BlockSpec(memory_space=pltpu.HBM),
        ],
        out_specs=[
            pl.BlockSpec((frames, span, features), whole),
            pl.BlockSpec((1, span, features), whole),
            pl.BlockSpec((1, span, features), whole),
            pl.BlockSpec((frames, span, features), whole),
        ],
        out_shape=[
            jax.ShapeDtypeStruct((frames, span, features), BF),
            jax.ShapeDtypeStruct((1, span, features), BF),
            jax.ShapeDtypeStruct((1, span, features), BF),
            pltpu.VMEM((frames, span, features), F32),
        ],
        scratch_shapes=[
            pltpu.VMEM((frames, span + 2 * cols, channels), BF),
            pltpu.VMEM((3, frames * span, features), F32),
            pltpu.VMEM((9, channels, features), BF),
            pltpu.SemaphoreType.DMA((9,)),
        ],
        compiler_params=params(40),
        cost_estimate=cost(
            2 * 9 * frames * span * channels * features, 2 * 9 * channels * features
        ),
        name="spatial_forward",
    )(odd, x, above, below, in_hbm(weight))


def temporal_forward_kernel(
    scale, odd, act_ref, one_ref, two_ref, w_ref, clean_ref, noise_ref, *rest
):
    gp_ref, one_out, two_out, loss_ref, rim_ref, ap = rest[1:]
    frames, span, features = act_ref.shape
    factor = scale[2]
    ap[(1 - odd[0]) * (frames + 1)] = one_ref[0]
    ap[odd[0] * (frames + 1)] = two_ref[0]
    ap[1 : frames + 1] = act_ref[...]
    pred = jnp.zeros((frames * span, features), F32)
    for tap in range(3):
        pred = pred + jnp.dot(
            ap[tap : tap + frames].reshape(frames * span, features),
            w_ref[tap],
            preferred_element_type=F32,
        )
    clean = clean_ref[...].reshape(frames * span, features).astype(F32)
    noise = noise_ref[...].reshape(frames * span, features).astype(F32)
    diff = pred - (scale[0] * noise - scale[1] * clean)
    gp_ref[...] = (2.0 * diff / factor).astype(BF).reshape(frames, span, features)
    one_out[0] = gp_ref[(1 - odd[0]) * (frames - 1)]
    two_out[0] = gp_ref[odd[0] * (frames - 1)]
    loss = jnp.sum(diff * diff, axis=0, keepdims=True)
    loss_ref[...] = loss
    rim_ref[0:span, :] = ap[0]
    rim_ref[span : 2 * span, :] = ap[frames + 1]
    rim_ref[2 * span :, :] = stacked(loss, LOSS).astype(BF)


def temporal_forward(scale, odd, act, one, two, weight, clean, noise, token):
    frames, span, features = act.shape
    whole = lambda i: (0, 0, 0)
    head = pl.BlockSpec((frames, span, features), whole)
    halo = pl.BlockSpec((1, span, features), whole)
    return pl.pallas_call(
        temporal_forward_kernel,
        grid=(1,),
        in_specs=[
            pl.BlockSpec(memory_space=pltpu.SMEM),
            pl.BlockSpec(memory_space=pltpu.SMEM),
            head,
            halo,
            halo,
            pl.BlockSpec(weight.shape, whole),
            head,
            head,
            pl.BlockSpec(memory_space=pl.ANY),
        ],
        out_specs=[
            head,
            halo,
            halo,
            pl.BlockSpec((1, features), lambda i: (0, 0)),
            pl.BlockSpec((2 * span + LOSS, features), lambda i: (0, 0)),
        ],
        out_shape=[
            jax.ShapeDtypeStruct((frames, span, features), BF),
            jax.ShapeDtypeStruct((1, span, features), BF),
            jax.ShapeDtypeStruct((1, span, features), BF),
            jax.ShapeDtypeStruct((1, features), F32),
            jax.ShapeDtypeStruct((2 * span + LOSS, features), BF),
        ],
        scratch_shapes=[pltpu.VMEM((frames + 2, span, features), BF)],
        compiler_params=params(16),
        cost_estimate=cost(2 * 3 * frames * span * features * features, 6 * features * features),
        name="temporal_forward",
    )(scale, odd, act, one, two, weight, clean, noise, token)


def thirds(value):
    high = value.astype(BF)
    rest = value - high.astype(F32)
    middle = rest.astype(BF)
    return high, middle, (rest - middle.astype(F32)).astype(BF)


def stacked(value, rows):
    high, middle, low = thirds(value)
    row = lax.broadcasted_iota(jnp.int32, (rows, value.shape[1]), 0)
    parts = [p.astype(F32) for p in (high, middle, low)]
    return jnp.where(
        row == 0, parts[0], jnp.where(row == 1, parts[1], jnp.where(row == 2, parts[2], 0.0))
    )


def joined(rows):
    return (rows[0:1] + rows[1:2]) + rows[2:3]


def temporal_grad_kernel(
    bits_ref,
    act_ref,
    rim_ref,
    act_other_ref,
    rim_other_ref,
    gp_ref,
    gp_other_ref,
    choice_ref,
    reorder_ref,
    loss_ref,
    send_ref,
    keep_0,
    keep_1,
    keep_2,
    sum_ref,
    padded,
    chosen,
    gps,
    total,
    choice,
    reorder,
    sems,
):
    frames, span, features = gp_ref.shape
    core = bits_ref[3]
    half = features // 2
    rows = half // 2
    lanes = loss_ref[...] + joined(rim_other_ref[2 * span : 2 * span + LOSS, :].astype(F32))
    lane = lax.broadcasted_iota(jnp.int32, lanes.shape, 1)
    loss = jnp.where(lane == bits_ref[4], jnp.sum(lanes, axis=1, keepdims=True), 0.0)
    sum_ref[...] = loss
    copies = [
        pltpu.make_async_copy(choice_ref.at[core], choice, sems.at[0]),
        pltpu.make_async_copy(reorder_ref.at[core], reorder, sems.at[1]),
    ]
    for c in copies:
        c.start()
    for which, (act, rim) in enumerate(((act_ref, rim_ref), (act_other_ref, rim_other_ref))):
        padded[which, 0] = rim[0:span, :]
        padded[which, 1 : frames + 1] = act[...]
        padded[which, frames + 1] = rim[span : 2 * span, :]
    for c in copies:
        c.wait()
    chosen[...] = lax.dot_general(
        choice[...],
        padded[...].reshape(-1, features),
        (((1,), (1,)), ((), ())),
        preferred_element_type=F32,
    ).astype(BF)
    gps[0:frames] = gp_ref[...]
    gps[frames:] = gp_other_ref[...]
    for tap, keep in enumerate((keep_0, keep_1, keep_2)):
        here = tap * span
        there = here + (frames + 2) * span
        long = frames * span
        left = jnp.concatenate(
            [chosen[:, here : here + long], chosen[:, there : there + long]], axis=1
        )
        if tap > 0:
            left = jnp.dot(
                reorder[tap - 1], left, preferred_element_type=F32
            ).astype(BF)
        total[...] = jnp.dot(
            left, gps[...].reshape(2 * long, features), preferred_element_type=F32
        )
        bit = bits_ref[tap]
        kept = pl.ds(pl.multiple_of(bit * rows, rows), rows)
        sent = pl.ds(pl.multiple_of((1 - bit) * rows, rows), rows)
        keep[...] = total[kept, :]
        send_ref[tap, 0:rows, :] = total[sent, :].astype(BF)
        send_ref[tap, rows : rows + LOSS, :] = stacked(loss, LOSS).astype(BF)
        send_ref[tap, rows + LOSS :, :] = jnp.zeros(
            (send_ref.shape[1] - rows - LOSS, features), BF
        )


def temporal_grad_local(
    bits, act, rim, act_other, rim_other, gp, gp_other, choice, reorder, loss
):
    frames, span, features = gp.shape
    rows = features // 4
    vmem = pl.BlockSpec(memory_space=pltpu.VMEM)
    return pl.pallas_call(
        temporal_grad_kernel,
        in_specs=[pl.BlockSpec(memory_space=pltpu.SMEM)]
        + [vmem] * 6
        + [pl.BlockSpec(memory_space=pltpu.HBM)] * 2
        + [vmem],
        out_shape=[
            pltpu.VMEM((3, 3 * EXTRA, features), BF),
            *[pltpu.HBM((rows, features), F32) for _ in range(3)],
            pltpu.VMEM((1, features), F32),
        ],
        out_specs=[vmem] * 5,
        scratch_shapes=[
            pltpu.VMEM((2, frames + 2, span, features), BF),
            pltpu.VMEM((features // 2, 2 * (frames + 2) * span), BF),
            pltpu.VMEM((2 * frames, span, features), BF),
            pltpu.VMEM((features // 2, features), F32),
            pltpu.VMEM(choice.shape[1:], BF),
            pltpu.VMEM(reorder.shape[1:], BF),
            pltpu.SemaphoreType.DMA((2,)),
        ],
        compiler_params=params(20),
        cost_estimate=cost(
            2 * 4 * frames * span * features * features, 6 * features * features
        ),
        name="temporal_grad",
    )(bits, act, rim, act_other, rim_other, gp, gp_other, in_hbm(choice), in_hbm(reorder), loss)


def temporal_backward_kernel(
    odd, gp_ref, one_ref, two_ref, w_ref, der_ref, token, out_ref, pad
):
    frames, span, features = gp_ref.shape
    pad[(1 - odd[0]) * (frames + 1)] = one_ref[0]
    pad[odd[0] * (frames + 1)] = two_ref[0]
    pad[1 : frames + 1] = gp_ref[...]
    total = jnp.zeros((frames * span, features), F32)
    for tap in range(3):
        total = total + lax.dot_general(
            pad[2 - tap : 2 - tap + frames].reshape(frames * span, features),
            w_ref[tap],
            (((1,), (1,)), ((), ())),
            preferred_element_type=F32,
        )
    der = der_ref[...].reshape(frames * span, features)
    out_ref[...] = (total * der).astype(BF).reshape(frames, span, features)


def temporal_backward(odd, gp, one, two, weight, der, token):
    frames, span, features = gp.shape
    return pl.pallas_call(
        temporal_backward_kernel,
        in_specs=[pl.BlockSpec(memory_space=pltpu.SMEM)]
        + [pl.BlockSpec(memory_space=pltpu.VMEM)] * 5
        + [pl.BlockSpec(memory_space=pl.ANY)],
        out_shape=pltpu.VMEM((frames, span, features), BF),
        scratch_shapes=[pltpu.VMEM((frames + 2, span, features), BF)],
        compiler_params=params(12),
        cost_estimate=cost(2 * 3 * frames * span * features * features, 6 * features * features),
        name="temporal_backward",
    )(odd, gp, one, two, weight, der, token)


def select_latent_kernel(core_ref, x_ref, choice_ref, token, own_ref, send_ref):
    core = core_ref[0]
    x = x_ref[...].reshape(-1, x_ref.shape[2])
    for out, which in ((send_ref, 1 - core), (own_ref, core)):
        out[...] = lax.dot_general(
            choice_ref[which], x, (((1,), (1,)), ((), ())), preferred_element_type=F32
        ).astype(BF)


def selected_latent(core, x, choice, token):
    frames, span, channels = x.shape
    shape = jax.ShapeDtypeStruct((channels // 2, frames * span), BF)
    vmem = pl.BlockSpec(memory_space=pltpu.VMEM)
    return pl.pallas_call(
        select_latent_kernel,
        in_specs=[
            pl.BlockSpec(memory_space=pltpu.SMEM),
            vmem,
            vmem,
            pl.BlockSpec(memory_space=pl.ANY),
        ],
        out_specs=[vmem, vmem],
        out_shape=[shape, shape],
        compiler_params=params(16),
        cost_estimate=cost(2 * frames * span * channels * channels, 4 * channels * channels),
        name="select_latent",
    )(core, x, choice, token)


def arrange_latent_kernel(
    core_ref, own_ref, other_ref, reorder_ref, token, out_hbm, out_ref, reorder, sem, sems
):
    core = core_ref[0]
    copy = pltpu.make_async_copy(reorder_ref.at[core], reorder, sem)
    copy.start()
    frames = 5
    span = own_ref.shape[1] // frames
    for f in range(frames):
        here = pl.multiple_of((2 * f + core) * span, span)
        there = pl.multiple_of((2 * f + 1 - core) * span, span)
        out_ref[0, :, pl.ds(here, span)] = own_ref[:, f * span : (f + 1) * span]
        out_ref[0, :, pl.ds(there, span)] = other_ref[:, f * span : (f + 1) * span]
    copy.wait()
    copies = [pltpu.make_async_copy(out_ref.at[k], out_hbm.at[k], sems.at[k]) for k in range(3)]
    copies[0].start()
    for third in range(1, 3):
        out_ref[third] = jnp.dot(
            reorder[third - 1], out_ref[0], preferred_element_type=F32
        ).astype(BF)
        copies[third].start()
    for c in copies:
        c.wait()


def arranged_latent(core, own, other, reorder, token):
    half, positions = own.shape
    vmem = pl.BlockSpec(memory_space=pltpu.VMEM)
    return pl.pallas_call(
        arrange_latent_kernel,
        in_specs=[
            pl.BlockSpec(memory_space=pltpu.SMEM),
            vmem,
            vmem,
            pl.BlockSpec(memory_space=pltpu.HBM),
            pl.BlockSpec(memory_space=pl.ANY),
        ],
        out_specs=pl.BlockSpec(memory_space=pltpu.HBM),
        out_shape=pltpu.HBM((3, half, 2 * positions), BF),
        scratch_shapes=[
            pltpu.VMEM((3, half, 2 * positions), BF),
            pltpu.VMEM(reorder.shape[1:], BF),
            pltpu.SemaphoreType.DMA,
            pltpu.SemaphoreType.DMA((3,)),
        ],
        compiler_params=params(16),
        cost_estimate=cost(8 * half * half * positions, 20 * half * positions),
        name="arrange_latent",
    )(core, own, other, in_hbm(reorder), token)


def shifted_gradient(core, own_ref, other_ref, pad):
    frames, span, features = own_ref.shape
    cols = (pad.shape[2] - 2 * span) // 2
    col = lax.broadcasted_iota(jnp.int32, (span, features), 0) % cols
    rim = jnp.zeros((cols, features), BF)

    def one(f, carry):
        for b in range(3):
            pad[b, f, 0:cols, :] = rim
            pad[b, f, cols + 2 * span : 2 * cols + 2 * span, :] = rim
        for ref, place in ((own_ref, core), (other_ref, 1 - core)):
            rows = pl.ds(pl.multiple_of(cols + place * span, cols), span)
            here = ref[f]
            wide = here.astype(F32)
            later = jnp.where(col == cols - 1, 0.0, pltpu.roll(wide, span - 1, 0))
            sooner = jnp.where(col == 0, 0.0, pltpu.roll(wide, 1, 0))
            pad[0, f, rows, :] = later.astype(BF)
            pad[1, f, rows, :] = here
            pad[2, f, rows, :] = sooner.astype(BF)
        return carry

    lax.fori_loop(0, frames, one, 0)


def gradient_half_kernel(thirds, has_extra, where, lat_ref, own_ref, other_ref, *rest):
    rest = list(rest)
    extra_ref = rest.pop(0) if has_extra else None
    outs = [rest.pop(0) for _ in thirds]
    pad, lat, lat_sems = rest[:3]
    frames, span, features = own_ref.shape
    cols = pad.shape[2] // 2 - span
    height = lat.shape[1]
    copies = []
    for k, first in enumerate(thirds):
        rows = pl.ds(pl.multiple_of(where[1 + first] * height, height), height)
        copies.append(
            pltpu.make_async_copy(lat_ref.at[first, rows, :], lat.at[k], lat_sems.at[k])
        )
    for c in copies:
        c.start()
    shifted_gradient(where[0], own_ref, other_ref, pad)
    leaving = []
    for k, first in enumerate(thirds):
        copies[k].wait()
        start = (2 - first) * cols
        for second in range(3):
            grad = pad[second, :, start : start + 2 * span, :]
            total = jnp.dot(
                lat[k], grad.reshape(2 * frames * span, features), preferred_element_type=F32
            )
            if has_extra:
                outs[k][second, 0:height, :] = total.astype(BF)
                outs[k][second, height:, :] = extra_ref[
                    first, second * EXTRA : (second + 1) * EXTRA, :
                ]
            else:
                rest[3][k, second] = total
        if not has_extra:
            leaving.append(pltpu.make_async_copy(rest[3].at[k], outs[k], rest[4].at[k]))
            leaving[k].start()
    for c in leaving:
        c.wait()


def gradient_half(thirds, where, lat, own, other, extra, name):
    frames, span, features = own.shape
    rows = lat.shape[1] // 2
    cols = 16
    n = len(thirds)
    vmem = pl.BlockSpec(memory_space=pltpu.VMEM)
    hbm = pl.BlockSpec(memory_space=pltpu.HBM)
    scratch = [
        pltpu.VMEM((3, frames, 2 * span + 2 * cols, features), BF),
        pltpu.VMEM((n, rows, lat.shape[2]), BF),
        pltpu.SemaphoreType.DMA((n,)),
    ]
    if extra is None:
        shape, out_spec, more = pltpu.HBM((3, rows, features), F32), hbm, []
        scratch += [pltpu.VMEM((n, 3, rows, features), F32), pltpu.SemaphoreType.DMA((n,))]
    else:
        shape, out_spec = pltpu.VMEM((3, rows + EXTRA, features), BF), vmem
        more = [in_vmem(extra)]
    return pl.pallas_call(
        functools.partial(gradient_half_kernel, thirds, extra is not None),
        in_specs=[pl.BlockSpec(memory_space=pltpu.SMEM), hbm] + [vmem] * (2 + len(more)),
        out_specs=[out_spec] * n,
        out_shape=[shape] * n,
        scratch_shapes=scratch,
        compiler_params=params(28),
        cost_estimate=cost(1, 1),
        name=name,
    )(where, in_hbm(lat), own, other, *more)


def bit_of(value, kind):
    if kind == 0:
        return value // 2
    return (value + 1) // 2 % 2


def swap_pairs(axis, step, size):
    pairs = []
    stride = STRIDES[axis]
    for device in range(size):
        tm, core = divmod(device, 2)
        value = tm // stride % RING
        partner = (value ^ 1) if (step + core) % 2 == 0 else (RING - 1 - value)
        pairs.append((device, (tm + (partner - value) * stride) * 2 + core))
    return pairs


def owners(order, core):
    found = []
    for n in range(RING**3):
        place = 0
        for k, axis in enumerate(order):
            digit = n // RING ** (2 - k) % RING
            first, second = divmod(digit, 2)
            low, high = (second, first) if core == 0 else (first, second)
            value = 2 * low + (low ^ high)
            place += value * STRIDES[axis]
        found.append(2 * place + core)
    return np.array(found)


def one_hot(rows, width):
    return (rows[:, None] == np.arange(width)[None, :]).astype(np.float32)


def selections(channels):
    each = channels // (2 * RING**3)
    return np.stack(
        [
            one_hot((owners(ORDERS[0], c)[:, None] * each + np.arange(each)).reshape(-1), channels)
            for c in range(2)
        ]
    )


def reorders(channels):
    each = channels // (2 * RING**3)
    found = []
    for c in range(2):
        base = list(owners(ORDERS[0], c))
        for order in ORDERS[1:]:
            at = np.array([base.index(o) for o in owners(order, c)])
            rows = (at[:, None] * each + np.arange(each)).reshape(-1)
            found.append(one_hot(rows, channels // 2))
    return np.stack(found).reshape(2, 2, channels // 2, channels // 2)


def up_to(n, multiple):
    return -(-n // multiple) * multiple


def payload_rows(rows, more, has_loss):
    return 3 * up_to(rows, 16) + (LOSS if has_loss else 0) + up_to(more, 16)


def places(rows, has_loss):
    slab = up_to(rows, 16)
    return [0, slab, 2 * slab], 3 * slab, 3 * slab + (LOSS if has_loss else 0)


def halve(ref, bit, count, send_ref, send_at):
    part = count // 2
    sent = up_to(part, 16)
    kept = up_to(part, 8)
    if part % 16 == 0:
        mine = ref[pl.ds(pl.multiple_of(bit * part, part), part), :]
        theirs = ref[pl.ds(pl.multiple_of((1 - bit) * part, part), part), :]
    else:
        whole = ref[...]
        tall = whole.shape[0]
        mine = pltpu.roll(whole, (tall - bit * part) % tall, 0)[:kept]
        theirs = pltpu.roll(whole, (tall - (1 - bit) * part) % tall, 0)[:sent]
    send_ref[send_at : send_at + sent, :] = theirs.astype(send_ref.dtype)
    return mine


def combine_first_kernel(has_loss, bits, keep_ref, met_ref, tp_ref, *refs):
    refs = list(refs)
    loss_ref = refs.pop(0) if has_loss else None
    send_ref, sp_out, tp_out = refs[:3]
    refs = refs[3:]
    loss_out = refs.pop(0) if has_loss else None
    keep_buf, region, extra_buf, tp_buf, sems = refs
    rows, features = keep_ref.shape[1:]
    count = rows // 2
    copies = [
        pltpu.make_async_copy(met_ref.at[:, pl.ds(rows, EXTRA), :], extra_buf, sems.at[0]),
        pltpu.make_async_copy(tp_ref, tp_buf, sems.at[1]),
    ]
    for k, bit in enumerate((1 - bits[1], bits[1])):
        at = pl.multiple_of(bit * count, count)
        part = pl.ds(at, count)
        copies += [
            pltpu.make_async_copy(keep_ref.at[:, part, :], keep_buf.at[k], sems.at[2 + 2 * k]),
            pltpu.make_async_copy(met_ref.at[:, part, :], region.at[k], sems.at[3 + 2 * k]),
        ]
    for c in copies:
        c.start()
    for c in copies[:4]:
        c.wait()
    for b in range(3):
        total = keep_buf[0, b] + region[0, b].astype(F32)
        send_ref[b * count : (b + 1) * count, :] = total.astype(BF)
    tall = tp_buf.shape[0]
    extra = extra_buf[...].reshape(3 * EXTRA, features).astype(F32)
    tp_buf[...] += extra[:tall]
    behind = 3 * count
    if has_loss:
        loss = loss_ref[...] + joined(extra[tall : tall + LOSS])
        loss_out[...] = loss
        send_ref[behind : behind + LOSS, :] = stacked(loss, LOSS).astype(BF)
        behind += LOSS
    tp_out[...] = halve(tp_buf, bits[1], tall, send_ref, behind)
    for c in copies[4:]:
        c.wait()
    for b in range(3):
        sp_out[b] = keep_buf[1, b] + region[1, b].astype(F32)


def combine_first(bits, keep, met, tp, loss, name):
    has_loss = loss is not None
    rows, width = keep.shape[1:]
    half = rows // 2
    vmem = pl.BlockSpec(memory_space=pltpu.VMEM)
    hbm = pl.BlockSpec(memory_space=pltpu.HBM)
    out_shape = [
        pltpu.VMEM((payload_rows(half, half // 2, has_loss), width), BF),
        pltpu.VMEM((3, half, width), F32),
        pltpu.VMEM((half // 2, width), F32),
    ]
    if has_loss:
        out_shape.append(pltpu.VMEM((1, width), F32))
    done = pl.pallas_call(
        functools.partial(combine_first_kernel, has_loss),
        in_specs=[pl.BlockSpec(memory_space=pltpu.SMEM), hbm, hbm, hbm] + [vmem] * has_loss,
        out_specs=[vmem] * len(out_shape),
        out_shape=out_shape,
        scratch_shapes=[
            pltpu.VMEM((2, 3, half, width), F32),
            pltpu.VMEM((2, 3, half, width), BF),
            pltpu.VMEM((3, EXTRA, width), BF),
            pltpu.VMEM((half, width), F32),
            pltpu.SemaphoreType.DMA((6,)),
        ],
        compiler_params=params(16),
        cost_estimate=cost(0, 8 * rows * width),
        name=name,
    )(bits, in_hbm(keep), in_hbm(met), in_hbm(tp), *([in_vmem(loss)] if has_loss else []))
    return done if has_loss else (*done, None)


def combine_kernel(rows, more, has_loss, bit_ref, met_ref, sp_ref, tp_ref, *rest):
    if has_loss:
        loss_ref, send_ref, sp_out, tp_out, loss_out, full, full_more = rest
    else:
        send_ref, sp_out, tp_out, full, full_more = rest
    bit = bit_ref[0]
    slabs, loss_at, behind = places(rows, has_loss)
    next_slab = up_to(rows // 2, 16)
    for b in range(3):
        tall = full.shape[1]
        full[b] = sp_ref[b] + met_ref[slabs[b] : slabs[b] + tall, :].astype(F32)
        sp_out[b] = halve(full.at[b], bit, rows, send_ref, b * next_slab)
    tall = full_more.shape[0]
    full_more[...] = tp_ref[...] + met_ref[behind : behind + tall, :].astype(F32)
    behind = 3 * next_slab
    if has_loss:
        loss = loss_ref[...] + joined(met_ref[loss_at : loss_at + LOSS, :].astype(F32))
        loss_out[...] = loss
        send_ref[behind : behind + LOSS, :] = stacked(loss, LOSS).astype(send_ref.dtype)
        behind += LOSS
    tp_out[...] = halve(full_more, bit, more, send_ref, behind)


def combine(bit, met, sp, tp, loss, rows, more, name):
    has_loss = loss is not None
    width = met.shape[1]
    out_shape = [
        pltpu.VMEM((payload_rows(rows // 2, more // 2, has_loss), width), BF),
        pltpu.VMEM((3, up_to(rows // 2, 8), width), F32),
        pltpu.VMEM((up_to(more // 2, 8), width), F32),
    ]
    operands = [bit, in_vmem(met), in_vmem(sp), in_vmem(tp)]
    if has_loss:
        out_shape.append(pltpu.VMEM((1, width), F32))
        operands.append(in_vmem(loss))
    vmem = pl.BlockSpec(memory_space=pltpu.VMEM)
    done = pl.pallas_call(
        functools.partial(combine_kernel, rows, more, has_loss),
        in_specs=[pl.BlockSpec(memory_space=pltpu.SMEM)] + [vmem] * (len(operands) - 1),
        out_specs=[vmem] * len(out_shape),
        out_shape=out_shape,
        scratch_shapes=[pltpu.VMEM(sp.shape, F32), pltpu.VMEM(tp.shape, F32)],
        compiler_params=params(12),
        cost_estimate=cost(0, 8 * sp.size),
        name=name,
    )(*operands)
    return done if has_loss else (*done, None)


def on_device(clean, noise, timestep, spatial_weight, temporal_weight):
    frames, rows, cols, channels = clean.shape
    features = temporal_weight.shape[0]
    span = rows * cols
    blocks = lax.axis_size("tm")
    size = 2 * blocks
    tm = lax.axis_index("tm")
    core = lax.axis_index("space")
    both = ("tm", "space")
    step_value = timestep[0].astype(F32)
    angle = math.pi / 2.0 * (step_value + 1.0) / (STEPS + 1.0)
    signal = jnp.cos(angle)
    sigma = jnp.sin(angle)
    positions = frames * blocks * rows * 2 * cols
    scale = jnp.stack([signal, sigma, jnp.float32(math.sqrt(positions))])
    w_spatial = jnp.transpose(spatial_weight, (1, 2, 0, 3))
    w_temporal = jnp.transpose(temporal_weight, (1, 0, 2))

    def mix(c, n):
        return (signal * c.astype(F32) + sigma * n.astype(F32)).astype(BF)

    edge_at = (1 - core) * (rows - 1)
    edge = mix(
        lax.dynamic_slice_in_dim(clean, edge_at, 1, axis=1),
        lax.dynamic_slice_in_dim(noise, edge_at, 1, axis=1),
    )
    met = lax.ppermute(edge, "space", [(0, 1), (1, 0)]).reshape(frames, cols, channels)
    above = jnp.where(core == 0, jnp.zeros_like(met), met)
    below = jnp.where(core == 0, met, jnp.zeros_like(met))
    noisy = mix(clean, noise).reshape(frames, span, channels)
    cross = [(0, 1), (1, 0)]
    core_index = jnp.reshape(core, (1,)).astype(jnp.int32)
    odd = jnp.reshape(tm % 2, (1,)).astype(jnp.int32)
    act, act_one, act_two, der = spatial_forward(odd, noisy, above, below, w_spatial)

    per_clip = CLIP // frames
    shift = CLIP // 4 // frames
    swaps = []
    for low in range(2):
        pairs = [(i, i + 1) for i in range(low, blocks - 1, 2) if (i + 1 + shift) % per_clip != 0]
        swaps.append(pairs + [(j, i) for i, j in pairs])
    act_one = lax.ppermute(act_one, "tm", swaps[0])
    act_two = lax.ppermute(act_two, "tm", swaps[1])
    act_other = lax.ppermute(act, "space", cross)
    lat_own, lat_send = selected_latent(
        core_index, noisy, jnp.asarray(selections(channels), BF), der
    )
    lat_other = lax.ppermute(lat_send, "space", cross)
    flat = (frames, span, channels)
    gp, gp_one, gp_two, loss_lanes, rim = temporal_forward(
        scale,
        odd,
        act,
        act_one,
        act_two,
        w_temporal,
        clean.reshape(flat),
        noise.reshape(flat),
        lat_own,
    )
    gp_one = lax.ppermute(gp_one, "tm", swaps[0])
    gp_two = lax.ppermute(gp_two, "tm", swaps[1])
    gp_other = lax.ppermute(gp, "space", cross)
    rim_other = lax.ppermute(rim, "space", cross)
    bits = []
    for order in ORDERS:
        own = []
        for axis in order:
            value = tm // STRIDES[axis] % RING
            low, high = bit_of(value, 0), bit_of(value, 1)
            own.append(jnp.where(core == 0, high, low))
            own.append(jnp.where(core == 0, low, high))
        bits.append([b.astype(jnp.int32) for b in own])
    first_bits = jnp.stack([b[0] for b in bits])
    extra, *more_keeps, loss = temporal_grad_local(
        jnp.concatenate([first_bits, core_index, jnp.reshape(tm, (1,)).astype(jnp.int32)]),
        act,
        rim,
        act_other,
        rim_other,
        gp,
        gp_other,
        jnp.asarray(selections(features), BF),
        jnp.asarray(reorders(features), BF),
        loss_lanes,
    )
    gh = temporal_backward(odd, gp, gp_one, gp_two, w_temporal, der, loss)
    gh_other = lax.ppermute(gh, "space", cross)
    lat = arranged_latent(
        core_index, lat_own, lat_other, jnp.asarray(reorders(channels), BF), gh
    )
    send_at = jnp.concatenate([core_index, 1 - first_bits])
    keep_at = jnp.concatenate([core_index, first_bits])
    (send_1,) = gradient_half((1,), send_at, lat, gh, gh_other, extra, "spatial_send_first")
    send_2, send_0 = gradient_half((2, 0), send_at, lat, gh, gh_other, extra, "spatial_send_rest")
    sends = [send_0, send_1, send_2]
    keeps = gradient_half((0, 1, 2), keep_at, lat, gh, gh_other, None, "spatial_keep")

    state = [
        (sends[t].reshape(-1, features), None, more_keeps[t], loss if t == 0 else None)
        for t in range(3)
    ]
    count, more = channels // 4, features // 4
    for step in range(6):
        met = [
            lax.ppermute(state[t][0], both, swap_pairs(ORDERS[t][step // 2], step, size))
            for t in range(3)
        ]
        if step == 5:
            break
        for t in range(3):
            _, sp, tp, total = state[t]
            name = "combine_%d_%d" % (step, t)
            if step == 0:
                arrived = met[t].reshape(sends[t].shape)
                state[t] = combine_first(jnp.stack(bits[t]), keeps[t], arrived, tp, total, name)
            else:
                bit = jnp.reshape(bits[t][step + 1], (1,))
                state[t] = combine(bit, met[t], sp, tp, total, count, more, name)
        count, more = count // 2, more // 2

    spatial_parts, temporal_parts = [], []
    for t in range(3):
        _, sp, tp, total = state[t]
        slabs, loss_at, behind = places(count, total is not None)
        spatial_parts.append(
            jnp.stack(
                [sp[b, :count] + met[t][s : s + count].astype(F32) for b, s in enumerate(slabs)]
            )
        )
        temporal_parts.append(tp[:more] + met[t][behind : behind + more].astype(F32))
        if total is not None:
            loss_sum = jnp.sum(total + joined(met[t][loss_at : loss_at + LOSS].astype(F32)))
    spatial_grad = jnp.transpose(jnp.stack(spatial_parts), (2, 0, 1, 3))
    temporal_grad = jnp.transpose(jnp.stack(temporal_parts), (1, 0, 2))
    return (loss_sum / (positions * features), spatial_grad, temporal_grad)


def solution(mesh):
    placed = (P("tm", "space", None, None), P("tm", "space", None, None), P(), P(), P())
    return jax.shard_map(
        on_device,
        mesh=mesh,
        in_specs=placed,
        out_specs=(P(), P(("tm", "space"), None, None, None), P(("tm", "space"), None, None)),
        check_vma=False,
    )
```

```python
import functools
import math

import jax
import jax.numpy as jnp
import numpy as np
from jax import lax
from jax.experimental import pallas as pl
from jax.experimental.pallas import tpu as pltpu
from jax.sharding import PartitionSpec as P

CLIP = 80
STEPS = 1000
BF = jnp.bfloat16
F32 = jnp.float32
MIB = 1 << 20
STRIDES = (16, 4, 1)
RING = 4
ORDERS = ((0, 1, 2), (1, 2, 0), (2, 0, 1))
LOSS = 16
EXTRA = 64


def params(mib):
    return pltpu.CompilerParams(vmem_limit_bytes=mib * MIB)


def in_hbm(x):
    return pltpu.with_memory_space_constraint(x, pltpu.HBM)


def in_vmem(x):
    return pltpu.with_memory_space_constraint(x, pltpu.VMEM)


def cost(flops, nbytes):
    return pl.CostEstimate(flops=int(flops), bytes_accessed=int(nbytes), transcendentals=0)


def spatial_forward_kernel(
    odd, x_ref, above_ref, below_ref, w_ref, act_ref, one_ref, two_ref, der_ref, xp, acc, taps, sems
):
    order = (1, 0, 2)
    step = pl.program_id(0)
    first = jnp.where(step == 0, 1, jnp.where(step == 1, 0, 2))
    frames, span, channels = x_ref.shape
    cols = above_ref.shape[1]
    features = w_ref.shape[3]
    wide = features // 256 * 256
    rest = features - wide

    @pl.when(step == 0)
    def _():
        for k in range(9):
            pltpu.make_async_copy(w_ref.at[order[k // 3], k % 3], taps.at[k], sems.at[k]).start()
        xp[:, 0:cols, :] = above_ref[...]
        xp[:, cols : cols + span, :] = x_ref[...]
        xp[:, cols + span : span + 2 * cols, :] = below_ref[...]
        acc[...] = jnp.zeros_like(acc)

    start = pl.multiple_of(first * cols, cols)
    piece = xp[:, pl.ds(start, span), :].reshape(frames * span, channels)
    for b in range(3):
        k = 3 * step + b
        pltpu.make_async_copy(w_ref.at[first, b], taps.at[k], sems.at[k]).wait()
        acc[b, :, 0:wide] += jnp.dot(piece, taps[k, :, 0:wide], preferred_element_type=F32)
    ends = jnp.concatenate([taps[3 * step + b, :, wide:] for b in range(3)], axis=1)
    prod = jnp.dot(piece, ends, preferred_element_type=F32)
    for b in range(3):
        acc[b, :, wide:] += prod[:, b * rest : (b + 1) * rest]

    @pl.when(step == 2)
    def _():
        col = lax.broadcasted_iota(jnp.int32, (span, features), 0) % cols

        def one(f, carry):
            rows = pl.ds(pl.multiple_of(f * span, span), span)
            left = jnp.where(col == 0, 0.0, pltpu.roll(acc[0, rows, :], 1, 0))
            right = jnp.where(col == cols - 1, 0.0, pltpu.roll(acc[2, rows, :], span - 1, 0))
            hidden = left + acc[1, rows, :] + right
            sig = 1.0 / (1.0 + jnp.exp(-hidden))
            act_ref[f] = (hidden * sig).astype(BF)
            der_ref[f] = sig * (1.0 + hidden * (1.0 - sig))
            return carry

        lax.fori_loop(0, frames, one, 0)
        one_ref[0] = act_ref[(1 - odd[0]) * (frames - 1)]
        two_ref[0] = act_ref[odd[0] * (frames - 1)]


def spatial_forward(odd, x, above, below, weight):
    frames, span, channels = x.shape
    cols = above.shape[1]
    features = weight.shape[3]
    whole = lambda s: (0, 0, 0)
    return pl.pallas_call(
        spatial_forward_kernel,
        grid=(3,),
        in_specs=[
            pl.BlockSpec(memory_space=pltpu.SMEM),
            pl.BlockSpec(x.shape, whole),
            pl.BlockSpec(above.shape, whole),
            pl.BlockSpec(below.shape, whole),
            pl.BlockSpec(memory_space=pltpu.HBM),
        ],
        out_specs=[
            pl.BlockSpec((frames, span, features), whole),
            pl.BlockSpec((1, span, features), whole),
            pl.BlockSpec((1, span, features), whole),
            pl.BlockSpec((frames, span, features), whole),
        ],
        out_shape=[
            jax.ShapeDtypeStruct((frames, span, features), BF),
            jax.ShapeDtypeStruct((1, span, features), BF),
            jax.ShapeDtypeStruct((1, span, features), BF),
            pltpu.VMEM((frames, span, features), F32),
        ],
        scratch_shapes=[
            pltpu.VMEM((frames, span + 2 * cols, channels), BF),
            pltpu.VMEM((3, frames * span, features), F32),
            pltpu.VMEM((9, channels, features), BF),
            pltpu.SemaphoreType.DMA((9,)),
        ],
        compiler_params=params(40),
        cost_estimate=cost(
            2 * 9 * frames * span * channels * features, 2 * 9 * channels * features
        ),
        name="spatial_forward",
    )(odd, x, above, below, in_hbm(weight))


def temporal_forward_kernel(
    scale, odd, act_ref, one_ref, two_ref, w_ref, clean_ref, noise_ref, *rest
):
    gp_ref, one_out, two_out, loss_ref, rim_ref, ap = rest[1:]
    frames, span, features = act_ref.shape
    factor = scale[2]
    ap[(1 - odd[0]) * (frames + 1)] = one_ref[0]
    ap[odd[0] * (frames + 1)] = two_ref[0]
    ap[1 : frames + 1] = act_ref[...]
    pred = jnp.zeros((frames * span, features), F32)
    for tap in range(3):
        pred = pred + jnp.dot(
            ap[tap : tap + frames].reshape(frames * span, features),
            w_ref[tap],
            preferred_element_type=F32,
        )
    clean = clean_ref[...].reshape(frames * span, features).astype(F32)
    noise = noise_ref[...].reshape(frames * span, features).astype(F32)
    diff = pred - (scale[0] * noise - scale[1] * clean)
    gp_ref[...] = (2.0 * diff / factor).astype(BF).reshape(frames, span, features)
    one_out[0] = gp_ref[(1 - odd[0]) * (frames - 1)]
    two_out[0] = gp_ref[odd[0] * (frames - 1)]
    loss = jnp.sum(diff * diff, axis=0, keepdims=True)
    loss_ref[...] = loss
    rim_ref[0:span, :] = ap[0]
    rim_ref[span : 2 * span, :] = ap[frames + 1]
    rim_ref[2 * span :, :] = stacked(loss, LOSS).astype(BF)


def temporal_forward(scale, odd, act, one, two, weight, clean, noise, token):
    frames, span, features = act.shape
    whole = lambda i: (0, 0, 0)
    head = pl.BlockSpec((frames, span, features), whole)
    halo = pl.BlockSpec((1, span, features), whole)
    return pl.pallas_call(
        temporal_forward_kernel,
        grid=(1,),
        in_specs=[
            pl.BlockSpec(memory_space=pltpu.SMEM),
            pl.BlockSpec(memory_space=pltpu.SMEM),
            head,
            halo,
            halo,
            pl.BlockSpec(weight.shape, whole),
            head,
            head,
            pl.BlockSpec(memory_space=pl.ANY),
        ],
        out_specs=[
            head,
            halo,
            halo,
            pl.BlockSpec((1, features), lambda i: (0, 0)),
            pl.BlockSpec((2 * span + LOSS, features), lambda i: (0, 0)),
        ],
        out_shape=[
            jax.ShapeDtypeStruct((frames, span, features), BF),
            jax.ShapeDtypeStruct((1, span, features), BF),
            jax.ShapeDtypeStruct((1, span, features), BF),
            jax.ShapeDtypeStruct((1, features), F32),
            jax.ShapeDtypeStruct((2 * span + LOSS, features), BF),
        ],
        scratch_shapes=[pltpu.VMEM((frames + 2, span, features), BF)],
        compiler_params=params(16),
        cost_estimate=cost(2 * 3 * frames * span * features * features, 6 * features * features),
        name="temporal_forward",
    )(scale, odd, act, one, two, weight, clean, noise, token)


def thirds(value):
    high = value.astype(BF)
    rest = value - high.astype(F32)
    middle = rest.astype(BF)
    return high, middle, (rest - middle.astype(F32)).astype(BF)


def stacked(value, rows):
    high, middle, low = thirds(value)
    row = lax.broadcasted_iota(jnp.int32, (rows, value.shape[1]), 0)
    parts = [p.astype(F32) for p in (high, middle, low)]
    return jnp.where(
        row == 0, parts[0], jnp.where(row == 1, parts[1], jnp.where(row == 2, parts[2], 0.0))
    )


def joined(rows):
    return (rows[0:1] + rows[1:2]) + rows[2:3]


def temporal_grad_kernel(
    bits_ref,
    act_ref,
    rim_ref,
    act_other_ref,
    rim_other_ref,
    gp_ref,
    gp_other_ref,
    choice_ref,
    reorder_ref,
    loss_ref,
    send_ref,
    keep_0,
    keep_1,
    keep_2,
    sum_ref,
    padded,
    chosen,
    gps,
    total,
    choice,
    reorder,
    sems,
):
    frames, span, features = gp_ref.shape
    core = bits_ref[3]
    half = features // 2
    rows = half // 2
    lanes = loss_ref[...] + joined(rim_other_ref[2 * span : 2 * span + LOSS, :].astype(F32))
    lane = lax.broadcasted_iota(jnp.int32, lanes.shape, 1)
    loss = jnp.where(lane == bits_ref[4], jnp.sum(lanes, axis=1, keepdims=True), 0.0)
    sum_ref[...] = loss
    copies = [
        pltpu.make_async_copy(choice_ref.at[core], choice, sems.at[0]),
        pltpu.make_async_copy(reorder_ref.at[core], reorder, sems.at[1]),
    ]
    for c in copies:
        c.start()
    for which, (act, rim) in enumerate(((act_ref, rim_ref), (act_other_ref, rim_other_ref))):
        padded[which, 0] = rim[0:span, :]
        padded[which, 1 : frames + 1] = act[...]
        padded[which, frames + 1] = rim[span : 2 * span, :]
    for c in copies:
        c.wait()
    chosen[...] = lax.dot_general(
        choice[...],
        padded[...].reshape(-1, features),
        (((1,), (1,)), ((), ())),
        preferred_element_type=F32,
    ).astype(BF)
    gps[0:frames] = gp_ref[...]
    gps[frames:] = gp_other_ref[...]
    for tap, keep in enumerate((keep_0, keep_1, keep_2)):
        here = tap * span
        there = here + (frames + 2) * span
        long = frames * span
        left = jnp.concatenate(
            [chosen[:, here : here + long], chosen[:, there : there + long]], axis=1
        )
        if tap > 0:
            left = jnp.dot(
                reorder[tap - 1], left, preferred_element_type=F32
            ).astype(BF)
        total[...] = jnp.dot(
            left, gps[...].reshape(2 * long, features), preferred_element_type=F32
        )
        bit = bits_ref[tap]
        kept = pl.ds(pl.multiple_of(bit * rows, rows), rows)
        sent = pl.ds(pl.multiple_of((1 - bit) * rows, rows), rows)
        keep[...] = total[kept, :]
        send_ref[tap, 0:rows, :] = total[sent, :].astype(BF)
        send_ref[tap, rows : rows + LOSS, :] = stacked(loss, LOSS).astype(BF)
        send_ref[tap, rows + LOSS :, :] = jnp.zeros(
            (send_ref.shape[1] - rows - LOSS, features), BF
        )


def temporal_grad_local(
    bits, act, rim, act_other, rim_other, gp, gp_other, choice, reorder, loss
):
    frames, span, features = gp.shape
    rows = features // 4
    vmem = pl.BlockSpec(memory_space=pltpu.VMEM)
    return pl.pallas_call(
        temporal_grad_kernel,
        in_specs=[pl.BlockSpec(memory_space=pltpu.SMEM)]
        + [vmem] * 6
        + [pl.BlockSpec(memory_space=pltpu.HBM)] * 2
        + [vmem],
        out_shape=[
            pltpu.VMEM((3, 3 * EXTRA, features), BF),
            *[pltpu.HBM((rows, features), F32) for _ in range(3)],
            pltpu.VMEM((1, features), F32),
        ],
        out_specs=[vmem] * 5,
        scratch_shapes=[
            pltpu.VMEM((2, frames + 2, span, features), BF),
            pltpu.VMEM((features // 2, 2 * (frames + 2) * span), BF),
            pltpu.VMEM((2 * frames, span, features), BF),
            pltpu.VMEM((features // 2, features), F32),
            pltpu.VMEM(choice.shape[1:], BF),
            pltpu.VMEM(reorder.shape[1:], BF),
            pltpu.SemaphoreType.DMA((2,)),
        ],
        compiler_params=params(20),
        cost_estimate=cost(
            2 * 4 * frames * span * features * features, 6 * features * features
        ),
        name="temporal_grad",
    )(bits, act, rim, act_other, rim_other, gp, gp_other, in_hbm(choice), in_hbm(reorder), loss)


def temporal_backward_kernel(
    odd, gp_ref, one_ref, two_ref, w_ref, der_ref, token, out_ref, pad
):
    frames, span, features = gp_ref.shape
    pad[(1 - odd[0]) * (frames + 1)] = one_ref[0]
    pad[odd[0] * (frames + 1)] = two_ref[0]
    pad[1 : frames + 1] = gp_ref[...]
    total = jnp.zeros((frames * span, features), F32)
    for tap in range(3):
        total = total + lax.dot_general(
            pad[2 - tap : 2 - tap + frames].reshape(frames * span, features),
            w_ref[tap],
            (((1,), (1,)), ((), ())),
            preferred_element_type=F32,
        )
    der = der_ref[...].reshape(frames * span, features)
    out_ref[...] = (total * der).astype(BF).reshape(frames, span, features)


def temporal_backward(odd, gp, one, two, weight, der, token):
    frames, span, features = gp.shape
    return pl.pallas_call(
        temporal_backward_kernel,
        in_specs=[pl.BlockSpec(memory_space=pltpu.SMEM)]
        + [pl.BlockSpec(memory_space=pltpu.VMEM)] * 5
        + [pl.BlockSpec(memory_space=pl.ANY)],
        out_shape=pltpu.VMEM((frames, span, features), BF),
        scratch_shapes=[pltpu.VMEM((frames + 2, span, features), BF)],
        compiler_params=params(12),
        cost_estimate=cost(2 * 3 * frames * span * features * features, 6 * features * features),
        name="temporal_backward",
    )(odd, gp, one, two, weight, der, token)


def select_latent_kernel(core_ref, x_ref, choice_ref, token, own_ref, send_ref):
    core = core_ref[0]
    x = x_ref[...].reshape(-1, x_ref.shape[2])
    for out, which in ((send_ref, 1 - core), (own_ref, core)):
        out[...] = lax.dot_general(
            choice_ref[which], x, (((1,), (1,)), ((), ())), preferred_element_type=F32
        ).astype(BF)


def selected_latent(core, x, choice, token):
    frames, span, channels = x.shape
    shape = jax.ShapeDtypeStruct((channels // 2, frames * span), BF)
    vmem = pl.BlockSpec(memory_space=pltpu.VMEM)
    return pl.pallas_call(
        select_latent_kernel,
        in_specs=[
            pl.BlockSpec(memory_space=pltpu.SMEM),
            vmem,
            vmem,
            pl.BlockSpec(memory_space=pl.ANY),
        ],
        out_specs=[vmem, vmem],
        out_shape=[shape, shape],
        compiler_params=params(16),
        cost_estimate=cost(2 * frames * span * channels * channels, 4 * channels * channels),
        name="select_latent",
    )(core, x, choice, token)


def arrange_latent_kernel(
    core_ref, own_ref, other_ref, reorder_ref, token, out_ref, reorder, sem
):
    core = core_ref[0]
    copy = pltpu.make_async_copy(reorder_ref.at[core], reorder, sem)
    copy.start()
    frames = 5
    span = own_ref.shape[1] // frames
    for f in range(frames):
        here = pl.multiple_of((2 * f + core) * span, span)
        there = pl.multiple_of((2 * f + 1 - core) * span, span)
        out_ref[0, :, pl.ds(here, span)] = own_ref[:, f * span : (f + 1) * span]
        out_ref[0, :, pl.ds(there, span)] = other_ref[:, f * span : (f + 1) * span]
    copy.wait()
    for third in range(1, 3):
        out_ref[third] = jnp.dot(
            reorder[third - 1], out_ref[0], preferred_element_type=F32
        ).astype(BF)


def arranged_latent(core, own, other, reorder, token):
    half, positions = own.shape
    vmem = pl.BlockSpec(memory_space=pltpu.VMEM)
    return pl.pallas_call(
        arrange_latent_kernel,
        in_specs=[
            pl.BlockSpec(memory_space=pltpu.SMEM),
            vmem,
            vmem,
            pl.BlockSpec(memory_space=pltpu.HBM),
            pl.BlockSpec(memory_space=pl.ANY),
        ],
        out_specs=vmem,
        out_shape=pltpu.VMEM((3, half, 2 * positions), BF),
        scratch_shapes=[pltpu.VMEM(reorder.shape[1:], BF), pltpu.SemaphoreType.DMA],
        compiler_params=params(16),
        cost_estimate=cost(8 * half * half * positions, 20 * half * positions),
        name="arrange_latent",
    )(core, own, other, in_hbm(reorder), token)


def shifted_gradient(core, own_ref, other_ref, pad):
    frames, span, features = own_ref.shape
    cols = (pad.shape[2] - 2 * span) // 2
    col = lax.broadcasted_iota(jnp.int32, (span, features), 0) % cols
    rim = jnp.zeros((cols, features), BF)

    def one(f, carry):
        for b in range(3):
            pad[b, f, 0:cols, :] = rim
            pad[b, f, cols + 2 * span : 2 * cols + 2 * span, :] = rim
        for ref, place in ((own_ref, core), (other_ref, 1 - core)):
            rows = pl.ds(pl.multiple_of(cols + place * span, cols), span)
            here = ref[f]
            wide = here.astype(F32)
            later = jnp.where(col == cols - 1, 0.0, pltpu.roll(wide, span - 1, 0))
            sooner = jnp.where(col == 0, 0.0, pltpu.roll(wide, 1, 0))
            pad[0, f, rows, :] = later.astype(BF)
            pad[1, f, rows, :] = here
            pad[2, f, rows, :] = sooner.astype(BF)
        return carry

    lax.fori_loop(0, frames, one, 0)


def spatial_grad_kernel(thirds, has_extra, where, lat_ref, own_ref, other_ref, *rest):
    extra_ref = rest[0] if has_extra else None
    outs, pad = rest[-1 - len(thirds) : -1], rest[-1]
    frames, span, features = own_ref.shape
    cols = pad.shape[2] // 2 - span
    height = lat_ref.shape[1] // 2
    shifted_gradient(where[0], own_ref, other_ref, pad)
    for out, first in zip(outs, thirds):
        rows = pl.ds(pl.multiple_of(where[1 + first] * height, height), height)
        start = (2 - first) * cols
        for second in range(3):
            grad = pad[second, :, start : start + 2 * span, :]
            out[second, 0:height, :] = jnp.dot(
                lat_ref[first, rows, :],
                grad.reshape(2 * frames * span, features),
                preferred_element_type=F32,
            ).astype(out.dtype)
            if has_extra:
                out[second, height:, :] = extra_ref[first, second * EXTRA : (second + 1) * EXTRA, :]


def gradient_half(thirds, where, lat, own, other, extra, name):
    frames, span, features = own.shape
    rows = lat.shape[1] // 2
    cols = 16
    vmem = pl.BlockSpec(memory_space=pltpu.VMEM)
    if extra is None:
        shape = pltpu.HBM((3, rows, features), F32)
    else:
        shape = pltpu.VMEM((3, rows + EXTRA, features), BF)
    more = [] if extra is None else [in_vmem(extra)]
    return pl.pallas_call(
        functools.partial(spatial_grad_kernel, thirds, extra is not None),
        in_specs=[pl.BlockSpec(memory_space=pltpu.SMEM)] + [vmem] * (3 + len(more)),
        out_specs=[vmem] * len(thirds),
        out_shape=[shape] * len(thirds),
        scratch_shapes=[pltpu.VMEM((3, frames, 2 * span + 2 * cols, features), BF)],
        compiler_params=params(24),
        cost_estimate=cost(1, 1),
        name=name,
    )(where, in_vmem(lat), own, other, *more)


def bit_of(value, kind):
    if kind == 0:
        return value // 2
    return (value + 1) // 2 % 2


def swap_pairs(axis, step, size):
    pairs = []
    stride = STRIDES[axis]
    for device in range(size):
        tm, core = divmod(device, 2)
        value = tm // stride % RING
        partner = (value ^ 1) if (step + core) % 2 == 0 else (RING - 1 - value)
        pairs.append((device, (tm + (partner - value) * stride) * 2 + core))
    return pairs


def owners(order, core):
    found = []
    for n in range(RING**3):
        place = 0
        for k, axis in enumerate(order):
            digit = n // RING ** (2 - k) % RING
            first, second = divmod(digit, 2)
            low, high = (second, first) if core == 0 else (first, second)
            value = 2 * low + (low ^ high)
            place += value * STRIDES[axis]
        found.append(2 * place + core)
    return np.array(found)


def one_hot(rows, width):
    return (rows[:, None] == np.arange(width)[None, :]).astype(np.float32)


def selections(channels):
    each = channels // (2 * RING**3)
    return np.stack(
        [
            one_hot((owners(ORDERS[0], c)[:, None] * each + np.arange(each)).reshape(-1), channels)
            for c in range(2)
        ]
    )


def reorders(channels):
    each = channels // (2 * RING**3)
    found = []
    for c in range(2):
        base = list(owners(ORDERS[0], c))
        for order in ORDERS[1:]:
            at = np.array([base.index(o) for o in owners(order, c)])
            rows = (at[:, None] * each + np.arange(each)).reshape(-1)
            found.append(one_hot(rows, channels // 2))
    return np.stack(found).reshape(2, 2, channels // 2, channels // 2)


def up_to(n, multiple):
    return -(-n // multiple) * multiple


def payload_rows(rows, more, has_loss):
    return 3 * up_to(rows, 16) + (LOSS if has_loss else 0) + up_to(more, 16)


def places(rows, has_loss):
    slab = up_to(rows, 16)
    return [0, slab, 2 * slab], 3 * slab, 3 * slab + (LOSS if has_loss else 0)


def halve(ref, bit, count, send_ref, send_at):
    part = count // 2
    sent = up_to(part, 16)
    kept = up_to(part, 8)
    if part % 16 == 0:
        mine = ref[pl.ds(pl.multiple_of(bit * part, part), part), :]
        theirs = ref[pl.ds(pl.multiple_of((1 - bit) * part, part), part), :]
    else:
        whole = ref[...]
        tall = whole.shape[0]
        mine = pltpu.roll(whole, (tall - bit * part) % tall, 0)[:kept]
        theirs = pltpu.roll(whole, (tall - (1 - bit) * part) % tall, 0)[:sent]
    send_ref[send_at : send_at + sent, :] = theirs.astype(send_ref.dtype)
    return mine


def combine_early_kernel(step, has_loss, bits, *refs):
    refs = list(refs)
    keep_ref, mets = refs[0], refs[1 : 2 + step]
    refs = refs[2 + step :]
    tp_ref = refs.pop(0)
    loss_ref = refs.pop(0) if has_loss else None
    send_ref = refs.pop(0)
    sp_out = refs.pop(0) if step == 2 else None
    tp_out = refs.pop(0)
    loss_out = refs.pop(0) if has_loss else None
    full_more = refs.pop(0)
    full = refs.pop(0) if step == 2 else None
    region, extra_buf, keep_buf, tp_buf, sems = refs
    rows = keep_ref.shape[1]
    half, quarter = rows // 2, rows // 4
    if step == 0:
        count, offsets = half, [(1 - bits[1]) * half]
    elif step == 1:
        count = quarter
        offsets = [bits[1] * half + (1 - bits[2]) * quarter, (1 - bits[2]) * quarter]
    else:
        count = quarter
        offsets = [bits[1] * half + bits[2] * quarter, bits[2] * quarter, 0]

    at = pl.multiple_of(offsets[0], count)
    copies = [
        pltpu.make_async_copy(keep_ref.at[:, pl.ds(at, count), :], keep_buf, sems.at[0]),
        pltpu.make_async_copy(mets[0].at[:, pl.ds(at, count), :], region, sems.at[1]),
    ]
    if step == 0:
        copies += [
            pltpu.make_async_copy(mets[0].at[:, pl.ds(rows, EXTRA), :], extra_buf, sems.at[2]),
            pltpu.make_async_copy(tp_ref, tp_buf, sems.at[3]),
        ]
        tp_ref = tp_buf
    for c in copies:
        c.start()
    for c in copies:
        c.wait()

    tall = full_more.shape[0]
    if step == 0:
        extra = extra_buf[...].reshape(3 * EXTRA, keep_ref.shape[2]).astype(F32)
        arrived, met_loss = extra[:tall], extra[tall : tall + LOSS]
    else:
        extra = mets[step][3 * (rows >> step) :, :].astype(F32)
        skip = LOSS if has_loss else 0
        arrived, met_loss = extra[skip : skip + tall], extra[:LOSS]
    full_more[...] = tp_ref[...] + arrived
    slab = up_to(rows >> (step + 1), 16)
    for b in range(3):
        total = keep_buf[b] + region[b].astype(F32)
        for k in range(1, step + 1):
            here = pl.multiple_of(b * (rows >> k) + offsets[k], count)
            total = total + mets[k][pl.ds(here, count), :].astype(F32)
        if step < 2:
            send_ref[b * slab : (b + 1) * slab, :] = total.astype(BF)
        else:
            full[b] = total
            sp_out[b] = halve(full.at[b], bits[3], count, send_ref, b * slab)
    behind = 3 * slab
    if has_loss:
        loss = loss_ref[...] + joined(met_loss)
        loss_out[...] = loss
        send_ref[behind : behind + LOSS, :] = stacked(loss, LOSS).astype(BF)
        behind += LOSS
    tp_out[...] = halve(full_more, bits[step + 1], 2 * (rows // 4 >> step), send_ref, behind)


def combine_early(step, bits, keep, mets, tp, loss, name):
    has_loss = loss is not None
    rows, width = keep.shape[1:]
    more = rows // 2 >> step
    half = rows >> (step + 1)
    vmem = pl.BlockSpec(memory_space=pltpu.VMEM)
    hbm = pl.BlockSpec(memory_space=pltpu.HBM)
    out_shape = [pltpu.VMEM((payload_rows(half, more // 2, has_loss), width), BF)]
    if step == 2:
        out_shape.append(pltpu.VMEM((3, up_to(half, 8), width), F32))
    out_shape.append(pltpu.VMEM((up_to(more // 2, 8), width), F32))
    if has_loss:
        out_shape.append(pltpu.VMEM((1, width), F32))
    scratch = [pltpu.VMEM((more, width), F32)]
    if step == 2:
        scratch.append(pltpu.VMEM((3, rows // 4, width), F32))
    scratch += [
        pltpu.VMEM((3, rows // 2 if step == 0 else rows // 4, width), BF),
        pltpu.VMEM((3, EXTRA, width), BF),
        pltpu.VMEM((3, rows // 2 if step == 0 else rows // 4, width), F32),
        pltpu.VMEM((rows // 2, width), F32),
        pltpu.SemaphoreType.DMA((4,)),
    ]
    done = list(
        pl.pallas_call(
            functools.partial(combine_early_kernel, step, has_loss),
            in_specs=[
                pl.BlockSpec(memory_space=pltpu.SMEM),
                hbm,
                hbm,
            ]
            + [vmem] * (len(mets) - 1)
            + [hbm if step == 0 else vmem]
            + [vmem] * has_loss,
            out_specs=[vmem] * len(out_shape),
            out_shape=out_shape,
            scratch_shapes=scratch,
            compiler_params=params(12),
            cost_estimate=cost(0, 8 * rows * width),
            name=name,
        )(
            bits,
            in_hbm(keep),
            in_hbm(mets[0]),
            *[in_vmem(x) for x in mets[1:]],
            in_hbm(tp) if step == 0 else in_vmem(tp),
            *([in_vmem(loss)] if has_loss else []),
        )
    )
    send = done.pop(0)
    sp = done.pop(0) if step == 2 else None
    tp = done.pop(0)
    return send, sp, tp, (done.pop(0) if has_loss else None)


def combine_kernel(rows, more, has_loss, bit_ref, met_ref, sp_ref, tp_ref, *rest):
    if has_loss:
        loss_ref, send_ref, sp_out, tp_out, loss_out, full, full_more = rest
    else:
        send_ref, sp_out, tp_out, full, full_more = rest
    bit = bit_ref[0]
    slabs, loss_at, behind = places(rows, has_loss)
    next_slab = up_to(rows // 2, 16)
    for b in range(3):
        tall = full.shape[1]
        full[b] = sp_ref[b] + met_ref[slabs[b] : slabs[b] + tall, :].astype(F32)
        sp_out[b] = halve(full.at[b], bit, rows, send_ref, b * next_slab)
    tall = full_more.shape[0]
    full_more[...] = tp_ref[...] + met_ref[behind : behind + tall, :].astype(F32)
    behind = 3 * next_slab
    if has_loss:
        loss = loss_ref[...] + joined(met_ref[loss_at : loss_at + LOSS, :].astype(F32))
        loss_out[...] = loss
        send_ref[behind : behind + LOSS, :] = stacked(loss, LOSS).astype(send_ref.dtype)
        behind += LOSS
    tp_out[...] = halve(full_more, bit, more, send_ref, behind)


def combine(bit, met, sp, tp, loss, rows, more, name):
    has_loss = loss is not None
    width = met.shape[1]
    out_shape = [
        pltpu.VMEM((payload_rows(rows // 2, more // 2, has_loss), width), BF),
        pltpu.VMEM((3, up_to(rows // 2, 8), width), F32),
        pltpu.VMEM((up_to(more // 2, 8), width), F32),
    ]
    operands = [bit, in_vmem(met), in_vmem(sp), in_vmem(tp)]
    if has_loss:
        out_shape.append(pltpu.VMEM((1, width), F32))
        operands.append(in_vmem(loss))
    vmem = pl.BlockSpec(memory_space=pltpu.VMEM)
    done = pl.pallas_call(
        functools.partial(combine_kernel, rows, more, has_loss),
        in_specs=[pl.BlockSpec(memory_space=pltpu.SMEM)] + [vmem] * (len(operands) - 1),
        out_specs=[vmem] * len(out_shape),
        out_shape=out_shape,
        scratch_shapes=[pltpu.VMEM(sp.shape, F32), pltpu.VMEM(tp.shape, F32)],
        compiler_params=params(12),
        cost_estimate=cost(0, 8 * sp.size),
        name=name,
    )(*operands)
    return done if has_loss else (*done, None)


def on_device(clean, noise, timestep, spatial_weight, temporal_weight):
    frames, rows, cols, channels = clean.shape
    features = temporal_weight.shape[0]
    span = rows * cols
    blocks = lax.axis_size("tm")
    size = 2 * blocks
    tm = lax.axis_index("tm")
    core = lax.axis_index("space")
    both = ("tm", "space")
    step_value = timestep[0].astype(F32)
    angle = math.pi / 2.0 * (step_value + 1.0) / (STEPS + 1.0)
    signal = jnp.cos(angle)
    sigma = jnp.sin(angle)
    positions = frames * blocks * rows * 2 * cols
    scale = jnp.stack([signal, sigma, jnp.float32(math.sqrt(positions))])
    w_spatial = jnp.transpose(spatial_weight, (1, 2, 0, 3))
    w_temporal = jnp.transpose(temporal_weight, (1, 0, 2))

    def mix(c, n):
        return (signal * c.astype(F32) + sigma * n.astype(F32)).astype(BF)

    edge_at = (1 - core) * (rows - 1)
    edge = mix(
        lax.dynamic_slice_in_dim(clean, edge_at, 1, axis=1),
        lax.dynamic_slice_in_dim(noise, edge_at, 1, axis=1),
    )
    met = lax.ppermute(edge, "space", [(0, 1), (1, 0)]).reshape(frames, cols, channels)
    above = jnp.where(core == 0, jnp.zeros_like(met), met)
    below = jnp.where(core == 0, met, jnp.zeros_like(met))
    noisy = mix(clean, noise).reshape(frames, span, channels)
    cross = [(0, 1), (1, 0)]
    core_index = jnp.reshape(core, (1,)).astype(jnp.int32)
    odd = jnp.reshape(tm % 2, (1,)).astype(jnp.int32)
    act, act_one, act_two, der = spatial_forward(odd, noisy, above, below, w_spatial)

    per_clip = CLIP // frames
    shift = CLIP // 4 // frames
    swaps = []
    for low in range(2):
        pairs = [(i, i + 1) for i in range(low, blocks - 1, 2) if (i + 1 + shift) % per_clip != 0]
        swaps.append(pairs + [(j, i) for i, j in pairs])
    act_one = lax.ppermute(act_one, "tm", swaps[0])
    act_two = lax.ppermute(act_two, "tm", swaps[1])
    act_other = lax.ppermute(act, "space", cross)
    lat_own, lat_send = selected_latent(
        core_index, noisy, jnp.asarray(selections(channels), BF), der
    )
    lat_other = lax.ppermute(lat_send, "space", cross)
    flat = (frames, span, channels)
    gp, gp_one, gp_two, loss_lanes, rim = temporal_forward(
        scale,
        odd,
        act,
        act_one,
        act_two,
        w_temporal,
        clean.reshape(flat),
        noise.reshape(flat),
        lat_own,
    )
    gp_one = lax.ppermute(gp_one, "tm", swaps[0])
    gp_two = lax.ppermute(gp_two, "tm", swaps[1])
    gp_other = lax.ppermute(gp, "space", cross)
    rim_other = lax.ppermute(rim, "space", cross)
    bits = []
    for order in ORDERS:
        own = []
        for axis in order:
            value = tm // STRIDES[axis] % RING
            low, high = bit_of(value, 0), bit_of(value, 1)
            own.append(jnp.where(core == 0, high, low))
            own.append(jnp.where(core == 0, low, high))
        bits.append([b.astype(jnp.int32) for b in own])
    first_bits = jnp.stack([b[0] for b in bits])
    extra, *more_keeps, loss = temporal_grad_local(
        jnp.concatenate([first_bits, core_index, jnp.reshape(tm, (1,)).astype(jnp.int32)]),
        act,
        rim,
        act_other,
        rim_other,
        gp,
        gp_other,
        jnp.asarray(selections(features), BF),
        jnp.asarray(reorders(features), BF),
        loss_lanes,
    )
    gh = temporal_backward(odd, gp, gp_one, gp_two, w_temporal, der, loss)
    gh_other = lax.ppermute(gh, "space", cross)
    lat = arranged_latent(
        core_index, lat_own, lat_other, jnp.asarray(reorders(channels), BF), gh
    )
    send_at = jnp.concatenate([core_index, 1 - first_bits])
    keep_at = jnp.concatenate([core_index, first_bits])
    (send_1,) = gradient_half((1,), send_at, lat, gh, gh_other, extra, "spatial_send_first")
    send_2, send_0 = gradient_half((2, 0), send_at, lat, gh, gh_other, extra, "spatial_send_rest")
    sends = [send_0, send_1, send_2]
    keeps = gradient_half((0, 1, 2), keep_at, lat, gh, gh_other, None, "spatial_keep")

    state = [
        (sends[t].reshape(-1, features), None, more_keeps[t], loss if t == 0 else None)
        for t in range(3)
    ]
    arrived = [[], [], []]
    count, more = channels // 4, features // 4
    for step in range(6):
        met = [
            lax.ppermute(state[t][0], both, swap_pairs(ORDERS[t][step // 2], step, size))
            for t in range(3)
        ]
        if step == 5:
            break
        for t in range(3):
            _, sp, tp, total = state[t]
            name = "combine_%d_%d" % (step, t)
            if step < 3:
                arrived[t].append(met[t].reshape(sends[t].shape) if step == 0 else met[t])
                state[t] = combine_early(
                    step, jnp.stack(bits[t]), keeps[t], arrived[t], tp, total, name
                )
            else:
                bit = jnp.reshape(bits[t][step + 1], (1,))
                state[t] = combine(bit, met[t], sp, tp, total, count, more, name)
        count, more = count // 2, more // 2

    spatial_parts, temporal_parts = [], []
    for t in range(3):
        _, sp, tp, total = state[t]
        slabs, loss_at, behind = places(count, total is not None)
        spatial_parts.append(
            jnp.stack(
                [sp[b, :count] + met[t][s : s + count].astype(F32) for b, s in enumerate(slabs)]
            )
        )
        temporal_parts.append(tp[:more] + met[t][behind : behind + more].astype(F32))
        if total is not None:
            loss_sum = jnp.sum(total + joined(met[t][loss_at : loss_at + LOSS].astype(F32)))
    spatial_grad = jnp.transpose(jnp.stack(spatial_parts), (2, 0, 1, 3))
    temporal_grad = jnp.transpose(jnp.stack(temporal_parts), (1, 0, 2))
    return (loss_sum / (positions * features), spatial_grad, temporal_grad)


def solution(mesh):
    placed = (P("tm", "space", None, None), P("tm", "space", None, None), P(), P(), P())
    return jax.shard_map(
        on_device,
        mesh=mesh,
        in_specs=placed,
        out_specs=(P(), P(("tm", "space"), None, None, None), P(("tm", "space"), None, None)),
        check_vma=False,
    )
```

```python
import functools
import math

import jax
import jax.numpy as jnp
import numpy as np
from jax import lax
from jax.experimental import pallas as pl
from jax.experimental.pallas import tpu as pltpu
from jax.sharding import PartitionSpec as P

CLIP = 80
STEPS = 1000
BF = jnp.bfloat16
F32 = jnp.float32
MIB = 1 << 20
STRIDES = (16, 4, 1)
RING = 4
ORDERS = ((0, 1, 2), (1, 2, 0), (2, 0, 1))
LOSS = 16
EXTRA = 64


def params(mib):
    return pltpu.CompilerParams(vmem_limit_bytes=mib * MIB)


def in_hbm(x):
    return pltpu.with_memory_space_constraint(x, pltpu.HBM)


def in_vmem(x):
    return pltpu.with_memory_space_constraint(x, pltpu.VMEM)


def cost(flops, nbytes):
    return pl.CostEstimate(flops=int(flops), bytes_accessed=int(nbytes), transcendentals=0)


def spatial_forward_kernel(
    odd, x_ref, above_ref, below_ref, w_ref, act_ref, one_ref, two_ref, der_ref, xp, acc, taps, sems
):
    order = (1, 0, 2)
    step = pl.program_id(0)
    first = jnp.where(step == 0, 1, jnp.where(step == 1, 0, 2))
    frames, span, channels = x_ref.shape
    cols = above_ref.shape[1]
    features = w_ref.shape[3]
    wide = features // 256 * 256
    rest = features - wide

    @pl.when(step == 0)
    def _():
        for k in range(9):
            pltpu.make_async_copy(w_ref.at[order[k // 3], k % 3], taps.at[k], sems.at[k]).start()
        xp[:, 0:cols, :] = above_ref[...]
        xp[:, cols : cols + span, :] = x_ref[...]
        xp[:, cols + span : span + 2 * cols, :] = below_ref[...]
        acc[...] = jnp.zeros_like(acc)

    start = pl.multiple_of(first * cols, cols)
    piece = xp[:, pl.ds(start, span), :].reshape(frames * span, channels)
    for b in range(3):
        k = 3 * step + b
        pltpu.make_async_copy(w_ref.at[first, b], taps.at[k], sems.at[k]).wait()
        acc[b, :, 0:wide] += jnp.dot(piece, taps[k, :, 0:wide], preferred_element_type=F32)
    ends = jnp.concatenate([taps[3 * step + b, :, wide:] for b in range(3)], axis=1)
    prod = jnp.dot(piece, ends, preferred_element_type=F32)
    for b in range(3):
        acc[b, :, wide:] += prod[:, b * rest : (b + 1) * rest]

    @pl.when(step == 2)
    def _():
        col = lax.broadcasted_iota(jnp.int32, (span, features), 0) % cols

        def one(f, carry):
            rows = pl.ds(pl.multiple_of(f * span, span), span)
            left = jnp.where(col == 0, 0.0, pltpu.roll(acc[0, rows, :], 1, 0))
            right = jnp.where(col == cols - 1, 0.0, pltpu.roll(acc[2, rows, :], span - 1, 0))
            hidden = left + acc[1, rows, :] + right
            sig = 1.0 / (1.0 + jnp.exp(-hidden))
            act_ref[f] = (hidden * sig).astype(BF)
            der_ref[f] = sig * (1.0 + hidden * (1.0 - sig))
            return carry

        lax.fori_loop(0, frames, one, 0)
        one_ref[0] = act_ref[(1 - odd[0]) * (frames - 1)]
        two_ref[0] = act_ref[odd[0] * (frames - 1)]


def spatial_forward(odd, x, above, below, weight):
    frames, span, channels = x.shape
    cols = above.shape[1]
    features = weight.shape[3]
    whole = lambda s: (0, 0, 0)
    return pl.pallas_call(
        spatial_forward_kernel,
        grid=(3,),
        in_specs=[
            pl.BlockSpec(memory_space=pltpu.SMEM),
            pl.BlockSpec(x.shape, whole),
            pl.BlockSpec(above.shape, whole),
            pl.BlockSpec(below.shape, whole),
            pl.BlockSpec(memory_space=pltpu.HBM),
        ],
        out_specs=[
            pl.BlockSpec((frames, span, features), whole),
            pl.BlockSpec((1, span, features), whole),
            pl.BlockSpec((1, span, features), whole),
            pl.BlockSpec((frames, span, features), whole),
        ],
        out_shape=[
            jax.ShapeDtypeStruct((frames, span, features), BF),
            jax.ShapeDtypeStruct((1, span, features), BF),
            jax.ShapeDtypeStruct((1, span, features), BF),
            pltpu.VMEM((frames, span, features), F32),
        ],
        scratch_shapes=[
            pltpu.VMEM((frames, span + 2 * cols, channels), BF),
            pltpu.VMEM((3, frames * span, features), F32),
            pltpu.VMEM((9, channels, features), BF),
            pltpu.SemaphoreType.DMA((9,)),
        ],
        compiler_params=params(40),
        cost_estimate=cost(
            2 * 9 * frames * span * channels * features, 2 * 9 * channels * features
        ),
        name="spatial_forward",
    )(odd, x, above, below, in_hbm(weight))


def temporal_forward_kernel(
    scale, odd, act_ref, one_ref, two_ref, w_ref, clean_ref, noise_ref, *rest
):
    gp_ref, one_out, two_out, loss_ref, rim_ref, ap = rest[1:]
    frames, span, features = act_ref.shape
    factor = scale[2]
    ap[(1 - odd[0]) * (frames + 1)] = one_ref[0]
    ap[odd[0] * (frames + 1)] = two_ref[0]
    ap[1 : frames + 1] = act_ref[...]
    pred = jnp.zeros((frames * span, features), F32)
    for tap in range(3):
        pred = pred + jnp.dot(
            ap[tap : tap + frames].reshape(frames * span, features),
            w_ref[tap],
            preferred_element_type=F32,
        )
    clean = clean_ref[...].reshape(frames * span, features).astype(F32)
    noise = noise_ref[...].reshape(frames * span, features).astype(F32)
    diff = pred - (scale[0] * noise - scale[1] * clean)
    gp_ref[...] = (2.0 * diff / factor).astype(BF).reshape(frames, span, features)
    one_out[0] = gp_ref[(1 - odd[0]) * (frames - 1)]
    two_out[0] = gp_ref[odd[0] * (frames - 1)]
    loss = jnp.sum(diff * diff, axis=0, keepdims=True)
    loss_ref[...] = loss
    rim_ref[0:span, :] = ap[0]
    rim_ref[span : 2 * span, :] = ap[frames + 1]
    rim_ref[2 * span :, :] = stacked(loss, LOSS).astype(BF)


def temporal_forward(scale, odd, act, one, two, weight, clean, noise, token):
    frames, span, features = act.shape
    whole = lambda i: (0, 0, 0)
    head = pl.BlockSpec((frames, span, features), whole)
    halo = pl.BlockSpec((1, span, features), whole)
    return pl.pallas_call(
        temporal_forward_kernel,
        grid=(1,),
        in_specs=[
            pl.BlockSpec(memory_space=pltpu.SMEM),
            pl.BlockSpec(memory_space=pltpu.SMEM),
            head,
            halo,
            halo,
            pl.BlockSpec(weight.shape, whole),
            head,
            head,
            pl.BlockSpec(memory_space=pl.ANY),
        ],
        out_specs=[
            head,
            halo,
            halo,
            pl.BlockSpec((1, features), lambda i: (0, 0)),
            pl.BlockSpec((2 * span + LOSS, features), lambda i: (0, 0)),
        ],
        out_shape=[
            jax.ShapeDtypeStruct((frames, span, features), BF),
            jax.ShapeDtypeStruct((1, span, features), BF),
            jax.ShapeDtypeStruct((1, span, features), BF),
            jax.ShapeDtypeStruct((1, features), F32),
            jax.ShapeDtypeStruct((2 * span + LOSS, features), BF),
        ],
        scratch_shapes=[pltpu.VMEM((frames + 2, span, features), BF)],
        compiler_params=params(16),
        cost_estimate=cost(2 * 3 * frames * span * features * features, 6 * features * features),
        name="temporal_forward",
    )(scale, odd, act, one, two, weight, clean, noise, token)


def thirds(value):
    high = value.astype(BF)
    rest = value - high.astype(F32)
    middle = rest.astype(BF)
    return high, middle, (rest - middle.astype(F32)).astype(BF)


def stacked(value, rows):
    high, middle, low = thirds(value)
    row = lax.broadcasted_iota(jnp.int32, (rows, value.shape[1]), 0)
    parts = [p.astype(F32) for p in (high, middle, low)]
    return jnp.where(
        row == 0, parts[0], jnp.where(row == 1, parts[1], jnp.where(row == 2, parts[2], 0.0))
    )


def joined(rows):
    return (rows[0:1] + rows[1:2]) + rows[2:3]


def temporal_grad_kernel(
    bits_ref,
    act_ref,
    rim_ref,
    act_other_ref,
    rim_other_ref,
    gp_ref,
    gp_other_ref,
    choice_ref,
    reorder_ref,
    loss_ref,
    send_ref,
    keep_0,
    keep_1,
    keep_2,
    sum_ref,
    padded,
    chosen,
    gps,
    total,
    choice,
    reorder,
    sems,
):
    frames, span, features = gp_ref.shape
    core = bits_ref[3]
    half = features // 2
    rows = half // 2
    lanes = loss_ref[...] + joined(rim_other_ref[2 * span : 2 * span + LOSS, :].astype(F32))
    lane = lax.broadcasted_iota(jnp.int32, lanes.shape, 1)
    loss = jnp.where(lane == bits_ref[4], jnp.sum(lanes, axis=1, keepdims=True), 0.0)
    sum_ref[...] = loss
    copies = [
        pltpu.make_async_copy(choice_ref.at[core], choice, sems.at[0]),
        pltpu.make_async_copy(reorder_ref.at[core], reorder, sems.at[1]),
    ]
    for c in copies:
        c.start()
    for which, (act, rim) in enumerate(((act_ref, rim_ref), (act_other_ref, rim_other_ref))):
        padded[which, 0] = rim[0:span, :]
        padded[which, 1 : frames + 1] = act[...]
        padded[which, frames + 1] = rim[span : 2 * span, :]
    for c in copies:
        c.wait()
    chosen[...] = lax.dot_general(
        choice[...],
        padded[...].reshape(-1, features),
        (((1,), (1,)), ((), ())),
        preferred_element_type=F32,
    ).astype(BF)
    gps[0:frames] = gp_ref[...]
    gps[frames:] = gp_other_ref[...]
    for tap, keep in enumerate((keep_0, keep_1, keep_2)):
        here = tap * span
        there = here + (frames + 2) * span
        long = frames * span
        left = jnp.concatenate(
            [chosen[:, here : here + long], chosen[:, there : there + long]], axis=1
        )
        if tap > 0:
            left = jnp.dot(
                reorder[tap - 1], left, preferred_element_type=F32
            ).astype(BF)
        total[...] = jnp.dot(
            left, gps[...].reshape(2 * long, features), preferred_element_type=F32
        )
        bit = bits_ref[tap]
        kept = pl.ds(pl.multiple_of(bit * rows, rows), rows)
        sent = pl.ds(pl.multiple_of((1 - bit) * rows, rows), rows)
        keep[...] = total[kept, :]
        send_ref[tap, 0:rows, :] = total[sent, :].astype(BF)
        send_ref[tap, rows : rows + LOSS, :] = stacked(loss, LOSS).astype(BF)
        send_ref[tap, rows + LOSS :, :] = jnp.zeros(
            (send_ref.shape[1] - rows - LOSS, features), BF
        )


def temporal_grad_local(
    bits, act, rim, act_other, rim_other, gp, gp_other, choice, reorder, loss
):
    frames, span, features = gp.shape
    rows = features // 4
    vmem = pl.BlockSpec(memory_space=pltpu.VMEM)
    return pl.pallas_call(
        temporal_grad_kernel,
        in_specs=[pl.BlockSpec(memory_space=pltpu.SMEM)]
        + [vmem] * 6
        + [pl.BlockSpec(memory_space=pltpu.HBM)] * 2
        + [vmem],
        out_shape=[
            pltpu.VMEM((3, 3 * EXTRA, features), BF),
            *[pltpu.HBM((rows, features), F32) for _ in range(3)],
            pltpu.VMEM((1, features), F32),
        ],
        out_specs=[vmem] * 5,
        scratch_shapes=[
            pltpu.VMEM((2, frames + 2, span, features), BF),
            pltpu.VMEM((features // 2, 2 * (frames + 2) * span), BF),
            pltpu.VMEM((2 * frames, span, features), BF),
            pltpu.VMEM((features // 2, features), F32),
            pltpu.VMEM(choice.shape[1:], BF),
            pltpu.VMEM(reorder.shape[1:], BF),
            pltpu.SemaphoreType.DMA((2,)),
        ],
        compiler_params=params(20),
        cost_estimate=cost(
            2 * 4 * frames * span * features * features, 6 * features * features
        ),
        name="temporal_grad",
    )(bits, act, rim, act_other, rim_other, gp, gp_other, in_hbm(choice), in_hbm(reorder), loss)


def temporal_backward_kernel(
    odd, gp_ref, one_ref, two_ref, w_ref, der_ref, token, out_ref, pad
):
    frames, span, features = gp_ref.shape
    pad[(1 - odd[0]) * (frames + 1)] = one_ref[0]
    pad[odd[0] * (frames + 1)] = two_ref[0]
    pad[1 : frames + 1] = gp_ref[...]
    total = jnp.zeros((frames * span, features), F32)
    for tap in range(3):
        total = total + lax.dot_general(
            pad[2 - tap : 2 - tap + frames].reshape(frames * span, features),
            w_ref[tap],
            (((1,), (1,)), ((), ())),
            preferred_element_type=F32,
        )
    der = der_ref[...].reshape(frames * span, features)
    out_ref[...] = (total * der).astype(BF).reshape(frames, span, features)


def temporal_backward(odd, gp, one, two, weight, der, token):
    frames, span, features = gp.shape
    return pl.pallas_call(
        temporal_backward_kernel,
        in_specs=[pl.BlockSpec(memory_space=pltpu.SMEM)]
        + [pl.BlockSpec(memory_space=pltpu.VMEM)] * 5
        + [pl.BlockSpec(memory_space=pl.ANY)],
        out_shape=pltpu.VMEM((frames, span, features), BF),
        scratch_shapes=[pltpu.VMEM((frames + 2, span, features), BF)],
        compiler_params=params(12),
        cost_estimate=cost(2 * 3 * frames * span * features * features, 6 * features * features),
        name="temporal_backward",
    )(odd, gp, one, two, weight, der, token)


def select_latent_kernel(core_ref, x_ref, choice_ref, token, own_ref, send_ref):
    core = core_ref[0]
    x = x_ref[...].reshape(-1, x_ref.shape[2])
    for out, which in ((send_ref, 1 - core), (own_ref, core)):
        out[...] = lax.dot_general(
            choice_ref[which], x, (((1,), (1,)), ((), ())), preferred_element_type=F32
        ).astype(BF)


def selected_latent(core, x, choice, token):
    frames, span, channels = x.shape
    shape = jax.ShapeDtypeStruct((channels // 2, frames * span), BF)
    vmem = pl.BlockSpec(memory_space=pltpu.VMEM)
    return pl.pallas_call(
        select_latent_kernel,
        in_specs=[
            pl.BlockSpec(memory_space=pltpu.SMEM),
            vmem,
            vmem,
            pl.BlockSpec(memory_space=pl.ANY),
        ],
        out_specs=[vmem, vmem],
        out_shape=[shape, shape],
        compiler_params=params(16),
        cost_estimate=cost(2 * frames * span * channels * channels, 4 * channels * channels),
        name="select_latent",
    )(core, x, choice, token)


def arrange_latent_kernel(
    core_ref, own_ref, other_ref, reorder_ref, token, out_hbm, out_ref, reorder, sem, sems
):
    core = core_ref[0]
    copy = pltpu.make_async_copy(reorder_ref.at[core], reorder, sem)
    copy.start()
    frames = 5
    span = own_ref.shape[1] // frames
    for f in range(frames):
        here = pl.multiple_of((2 * f + core) * span, span)
        there = pl.multiple_of((2 * f + 1 - core) * span, span)
        out_ref[0, :, pl.ds(here, span)] = own_ref[:, f * span : (f + 1) * span]
        out_ref[0, :, pl.ds(there, span)] = other_ref[:, f * span : (f + 1) * span]
    copy.wait()
    copies = [pltpu.make_async_copy(out_ref.at[k], out_hbm.at[k], sems.at[k]) for k in range(3)]
    copies[0].start()
    for third in range(1, 3):
        out_ref[third] = jnp.dot(
            reorder[third - 1], out_ref[0], preferred_element_type=F32
        ).astype(BF)
        copies[third].start()
    for c in copies:
        c.wait()


def arranged_latent(core, own, other, reorder, token):
    half, positions = own.shape
    vmem = pl.BlockSpec(memory_space=pltpu.VMEM)
    return pl.pallas_call(
        arrange_latent_kernel,
        in_specs=[
            pl.BlockSpec(memory_space=pltpu.SMEM),
            vmem,
            vmem,
            pl.BlockSpec(memory_space=pltpu.HBM),
            pl.BlockSpec(memory_space=pl.ANY),
        ],
        out_specs=pl.BlockSpec(memory_space=pltpu.HBM),
        out_shape=pltpu.HBM((3, half, 2 * positions), BF),
        scratch_shapes=[
            pltpu.VMEM((3, half, 2 * positions), BF),
            pltpu.VMEM(reorder.shape[1:], BF),
            pltpu.SemaphoreType.DMA,
            pltpu.SemaphoreType.DMA((3,)),
        ],
        compiler_params=params(16),
        cost_estimate=cost(8 * half * half * positions, 20 * half * positions),
        name="arrange_latent",
    )(core, own, other, in_hbm(reorder), token)


def shifted_gradient(core, own_ref, other_ref, pad):
    frames, span, features = own_ref.shape
    cols = (pad.shape[2] - 2 * span) // 2
    col = lax.broadcasted_iota(jnp.int32, (span, features), 0) % cols
    rim = jnp.zeros((cols, features), BF)

    def one(f, carry):
        for b in range(3):
            pad[b, f, 0:cols, :] = rim
            pad[b, f, cols + 2 * span : 2 * cols + 2 * span, :] = rim
        for ref, place in ((own_ref, core), (other_ref, 1 - core)):
            rows = pl.ds(pl.multiple_of(cols + place * span, cols), span)
            here = ref[f]
            wide = here.astype(F32)
            later = jnp.where(col == cols - 1, 0.0, pltpu.roll(wide, span - 1, 0))
            sooner = jnp.where(col == 0, 0.0, pltpu.roll(wide, 1, 0))
            pad[0, f, rows, :] = later.astype(BF)
            pad[1, f, rows, :] = here
            pad[2, f, rows, :] = sooner.astype(BF)
        return carry

    lax.fori_loop(0, frames, one, 0)


def gradient_send_kernel(thirds, where, lat_ref, own_ref, other_ref, extra_ref, *rest):
    outs, (pad, lat, lat_sems) = rest[: len(thirds)], rest[len(thirds) :]
    frames, span, features = own_ref.shape
    cols = pad.shape[2] // 2 - span
    height = lat.shape[1]
    copies = []
    for k, first in enumerate(thirds):
        rows = pl.ds(pl.multiple_of(where[1 + first] * height, height), height)
        copies.append(
            pltpu.make_async_copy(lat_ref.at[first, rows, :], lat.at[k], lat_sems.at[k])
        )
    for c in copies:
        c.start()
    shifted_gradient(where[0], own_ref, other_ref, pad)
    for k, first in enumerate(thirds):
        copies[k].wait()
        start = (2 - first) * cols
        for second in range(3):
            grad = pad[second, :, start : start + 2 * span, :]
            outs[k][second, 0:height, :] = jnp.dot(
                lat[k], grad.reshape(2 * frames * span, features), preferred_element_type=F32
            ).astype(BF)
            outs[k][second, height:, :] = extra_ref[first, second * EXTRA : (second + 1) * EXTRA, :]


def gradient_send(thirds, where, lat, own, other, extra, name):
    frames, span, features = own.shape
    rows = lat.shape[1] // 2
    cols = 16
    n = len(thirds)
    vmem = pl.BlockSpec(memory_space=pltpu.VMEM)
    hbm = pl.BlockSpec(memory_space=pltpu.HBM)
    return pl.pallas_call(
        functools.partial(gradient_send_kernel, thirds),
        in_specs=[pl.BlockSpec(memory_space=pltpu.SMEM), hbm] + [vmem] * 3,
        out_specs=[vmem] * n,
        out_shape=[pltpu.VMEM((3, rows + EXTRA, features), BF)] * n,
        scratch_shapes=[
            pltpu.VMEM((3, frames, 2 * span + 2 * cols, features), BF),
            pltpu.VMEM((n, rows, lat.shape[2]), BF),
            pltpu.SemaphoreType.DMA((n,)),
        ],
        compiler_params=params(28),
        cost_estimate=cost(1, 1),
        name=name,
    )(where, in_hbm(lat), own, other, in_vmem(extra))


def gradient_keep_kernel(where, lat_ref, own_ref, other_ref, out_ref, pad, lat, lat_sems, sums, sems):
    frames, span, features = own_ref.shape
    cols = pad.shape[2] // 2 - span
    height = lat.shape[1]
    copies = []
    for k in range(3):
        rows = pl.ds(pl.multiple_of(where[1 + k] * height, height), height)
        copies.append(pltpu.make_async_copy(lat_ref.at[k, rows, :], lat.at[k], lat_sems.at[k]))
    for c in copies:
        c.start()
    shifted_gradient(where[0], own_ref, other_ref, pad)
    for c in copies:
        c.wait()

    def one(k, carry):
        start = pl.multiple_of((2 - k) * cols, cols)
        for second in range(3):
            grad = pad[second, :, pl.ds(start, 2 * span), :]
            sums[k, second] = jnp.dot(
                lat[k], grad.reshape(2 * frames * span, features), preferred_element_type=F32
            )
        pltpu.make_async_copy(sums.at[k], out_ref.at[k], sems.at[k]).start()
        return carry

    lax.fori_loop(0, 3, one, 0)
    for k in range(3):
        pltpu.make_async_copy(sums.at[k], out_ref.at[k], sems.at[k]).wait()


def gradient_keep(where, lat, own, other):
    frames, span, features = own.shape
    rows = lat.shape[1] // 2
    cols = 16
    vmem = pl.BlockSpec(memory_space=pltpu.VMEM)
    hbm = pl.BlockSpec(memory_space=pltpu.HBM)
    return pl.pallas_call(
        gradient_keep_kernel,
        in_specs=[pl.BlockSpec(memory_space=pltpu.SMEM), hbm, vmem, vmem],
        out_specs=hbm,
        out_shape=pltpu.HBM((3, 3, rows, features), F32),
        scratch_shapes=[
            pltpu.VMEM((3, frames, 2 * span + 2 * cols, features), BF),
            pltpu.VMEM((3, rows, lat.shape[2]), BF),
            pltpu.SemaphoreType.DMA((3,)),
            pltpu.VMEM((3, 3, rows, features), F32),
            pltpu.SemaphoreType.DMA((3,)),
        ],
        compiler_params=params(28),
        cost_estimate=cost(1, 1),
        name="spatial_keep",
    )(where, in_hbm(lat), own, other)


def bit_of(value, kind):
    if kind == 0:
        return value // 2
    return (value + 1) // 2 % 2


def swap_pairs(axis, step, size):
    pairs = []
    stride = STRIDES[axis]
    for device in range(size):
        tm, core = divmod(device, 2)
        value = tm // stride % RING
        partner = (value ^ 1) if (step + core) % 2 == 0 else (RING - 1 - value)
        pairs.append((device, (tm + (partner - value) * stride) * 2 + core))
    return pairs


def owners(order, core):
    found = []
    for n in range(RING**3):
        place = 0
        for k, axis in enumerate(order):
            digit = n // RING ** (2 - k) % RING
            first, second = divmod(digit, 2)
            low, high = (second, first) if core == 0 else (first, second)
            value = 2 * low + (low ^ high)
            place += value * STRIDES[axis]
        found.append(2 * place + core)
    return np.array(found)


def one_hot(rows, width):
    return (rows[:, None] == np.arange(width)[None, :]).astype(np.float32)


def selections(channels):
    each = channels // (2 * RING**3)
    return np.stack(
        [
            one_hot((owners(ORDERS[0], c)[:, None] * each + np.arange(each)).reshape(-1), channels)
            for c in range(2)
        ]
    )


def reorders(channels):
    each = channels // (2 * RING**3)
    found = []
    for c in range(2):
        base = list(owners(ORDERS[0], c))
        for order in ORDERS[1:]:
            at = np.array([base.index(o) for o in owners(order, c)])
            rows = (at[:, None] * each + np.arange(each)).reshape(-1)
            found.append(one_hot(rows, channels // 2))
    return np.stack(found).reshape(2, 2, channels // 2, channels // 2)


def up_to(n, multiple):
    return -(-n // multiple) * multiple


def payload_rows(rows, more, has_loss):
    return 3 * up_to(rows, 16) + (LOSS if has_loss else 0) + up_to(more, 16)


def places(rows, has_loss):
    slab = up_to(rows, 16)
    return [0, slab, 2 * slab], 3 * slab, 3 * slab + (LOSS if has_loss else 0)


def halve(ref, bit, count, send_ref, send_at):
    part = count // 2
    sent = up_to(part, 16)
    kept = up_to(part, 8)
    if part % 16 == 0:
        mine = ref[pl.ds(pl.multiple_of(bit * part, part), part), :]
        theirs = ref[pl.ds(pl.multiple_of((1 - bit) * part, part), part), :]
    else:
        whole = ref[...]
        tall = whole.shape[0]
        mine = pltpu.roll(whole, (tall - bit * part) % tall, 0)[:kept]
        theirs = pltpu.roll(whole, (tall - (1 - bit) * part) % tall, 0)[:sent]
    send_ref[send_at : send_at + sent, :] = theirs.astype(send_ref.dtype)
    return mine


def combine_first_kernel(third, has_loss, bits, keep_ref, met_ref, tp_ref, *refs):
    refs = list(refs)
    loss_ref = refs.pop(0) if has_loss else None
    send_ref, sp_out, tp_out = refs[:3]
    refs = refs[3:]
    loss_out = refs.pop(0) if has_loss else None
    keep_buf, region, extra_buf, tp_buf, sems = refs
    rows, features = keep_ref.shape[2:]
    count = rows // 2
    copies = [
        pltpu.make_async_copy(met_ref.at[:, pl.ds(rows, EXTRA), :], extra_buf, sems.at[0]),
        pltpu.make_async_copy(tp_ref, tp_buf, sems.at[1]),
    ]
    for k, bit in enumerate((1 - bits[1], bits[1])):
        at = pl.multiple_of(bit * count, count)
        part = pl.ds(at, count)
        copies += [
            pltpu.make_async_copy(
                keep_ref.at[third, :, part, :], keep_buf.at[k], sems.at[2 + 2 * k]
            ),
            pltpu.make_async_copy(met_ref.at[:, part, :], region.at[k], sems.at[3 + 2 * k]),
        ]
    for c in copies:
        c.start()
    for c in copies[:4]:
        c.wait()
    for b in range(3):
        total = keep_buf[0, b] + region[0, b].astype(F32)
        send_ref[b * count : (b + 1) * count, :] = total.astype(BF)
    tall = tp_buf.shape[0]
    extra = extra_buf[...].reshape(3 * EXTRA, features).astype(F32)
    tp_buf[...] += extra[:tall]
    behind = 3 * count
    if has_loss:
        loss = loss_ref[...] + joined(extra[tall : tall + LOSS])
        loss_out[...] = loss
        send_ref[behind : behind + LOSS, :] = stacked(loss, LOSS).astype(BF)
        behind += LOSS
    tp_out[...] = halve(tp_buf, bits[1], tall, send_ref, behind)
    for c in copies[4:]:
        c.wait()
    for b in range(3):
        sp_out[b] = keep_buf[1, b] + region[1, b].astype(F32)


def combine_first(third, bits, keep, met, tp, loss, name):
    has_loss = loss is not None
    rows, width = keep.shape[2:]
    half = rows // 2
    vmem = pl.BlockSpec(memory_space=pltpu.VMEM)
    hbm = pl.BlockSpec(memory_space=pltpu.HBM)
    out_shape = [
        pltpu.VMEM((payload_rows(half, half // 2, has_loss), width), BF),
        pltpu.VMEM((3, half, width), F32),
        pltpu.VMEM((half // 2, width), F32),
    ]
    if has_loss:
        out_shape.append(pltpu.VMEM((1, width), F32))
    done = pl.pallas_call(
        functools.partial(combine_first_kernel, third, has_loss),
        in_specs=[pl.BlockSpec(memory_space=pltpu.SMEM), hbm, hbm, hbm] + [vmem] * has_loss,
        out_specs=[vmem] * len(out_shape),
        out_shape=out_shape,
        scratch_shapes=[
            pltpu.VMEM((2, 3, half, width), F32),
            pltpu.VMEM((2, 3, half, width), BF),
            pltpu.VMEM((3, EXTRA, width), BF),
            pltpu.VMEM((half, width), F32),
            pltpu.SemaphoreType.DMA((6,)),
        ],
        compiler_params=params(16),
        cost_estimate=cost(0, 8 * rows * width),
        name=name,
    )(bits, in_hbm(keep), in_hbm(met), in_hbm(tp), *([in_vmem(loss)] if has_loss else []))
    return done if has_loss else (*done, None)


def combine_kernel(rows, more, has_loss, bit_ref, met_ref, sp_ref, tp_ref, *rest):
    if has_loss:
        loss_ref, send_ref, sp_out, tp_out, loss_out, full, full_more = rest
    else:
        send_ref, sp_out, tp_out, full, full_more = rest
    bit = bit_ref[0]
    slabs, loss_at, behind = places(rows, has_loss)
    next_slab = up_to(rows // 2, 16)
    for b in range(3):
        tall = full.shape[1]
        full[b] = sp_ref[b] + met_ref[slabs[b] : slabs[b] + tall, :].astype(F32)
        sp_out[b] = halve(full.at[b], bit, rows, send_ref, b * next_slab)
    tall = full_more.shape[0]
    full_more[...] = tp_ref[...] + met_ref[behind : behind + tall, :].astype(F32)
    behind = 3 * next_slab
    if has_loss:
        loss = loss_ref[...] + joined(met_ref[loss_at : loss_at + LOSS, :].astype(F32))
        loss_out[...] = loss
        send_ref[behind : behind + LOSS, :] = stacked(loss, LOSS).astype(send_ref.dtype)
        behind += LOSS
    tp_out[...] = halve(full_more, bit, more, send_ref, behind)


def combine(bit, met, sp, tp, loss, rows, more, name):
    has_loss = loss is not None
    width = met.shape[1]
    out_shape = [
        pltpu.VMEM((payload_rows(rows // 2, more // 2, has_loss), width), BF),
        pltpu.VMEM((3, up_to(rows // 2, 8), width), F32),
        pltpu.VMEM((up_to(more // 2, 8), width), F32),
    ]
    operands = [bit, in_vmem(met), in_vmem(sp), in_vmem(tp)]
    if has_loss:
        out_shape.append(pltpu.VMEM((1, width), F32))
        operands.append(in_vmem(loss))
    vmem = pl.BlockSpec(memory_space=pltpu.VMEM)
    done = pl.pallas_call(
        functools.partial(combine_kernel, rows, more, has_loss),
        in_specs=[pl.BlockSpec(memory_space=pltpu.SMEM)] + [vmem] * (len(operands) - 1),
        out_specs=[vmem] * len(out_shape),
        out_shape=out_shape,
        scratch_shapes=[pltpu.VMEM(sp.shape, F32), pltpu.VMEM(tp.shape, F32)],
        compiler_params=params(12),
        cost_estimate=cost(0, 8 * sp.size),
        name=name,
    )(*operands)
    return done if has_loss else (*done, None)


def on_device(clean, noise, timestep, spatial_weight, temporal_weight):
    frames, rows, cols, channels = clean.shape
    features = temporal_weight.shape[0]
    span = rows * cols
    blocks = lax.axis_size("tm")
    size = 2 * blocks
    tm = lax.axis_index("tm")
    core = lax.axis_index("space")
    both = ("tm", "space")
    step_value = timestep[0].astype(F32)
    angle = math.pi / 2.0 * (step_value + 1.0) / (STEPS + 1.0)
    signal = jnp.cos(angle)
    sigma = jnp.sin(angle)
    positions = frames * blocks * rows * 2 * cols
    scale = jnp.stack([signal, sigma, jnp.float32(math.sqrt(positions))])
    w_spatial = jnp.transpose(spatial_weight, (1, 2, 0, 3))
    w_temporal = jnp.transpose(temporal_weight, (1, 0, 2))

    def mix(c, n):
        return (signal * c.astype(F32) + sigma * n.astype(F32)).astype(BF)

    edge_at = (1 - core) * (rows - 1)
    edge = mix(
        lax.dynamic_slice_in_dim(clean, edge_at, 1, axis=1),
        lax.dynamic_slice_in_dim(noise, edge_at, 1, axis=1),
    )
    met = lax.ppermute(edge, "space", [(0, 1), (1, 0)]).reshape(frames, cols, channels)
    above = jnp.where(core == 0, jnp.zeros_like(met), met)
    below = jnp.where(core == 0, met, jnp.zeros_like(met))
    noisy = mix(clean, noise).reshape(frames, span, channels)
    cross = [(0, 1), (1, 0)]
    core_index = jnp.reshape(core, (1,)).astype(jnp.int32)
    odd = jnp.reshape(tm % 2, (1,)).astype(jnp.int32)
    act, act_one, act_two, der = spatial_forward(odd, noisy, above, below, w_spatial)

    per_clip = CLIP // frames
    shift = CLIP // 4 // frames
    swaps = []
    for low in range(2):
        pairs = [(i, i + 1) for i in range(low, blocks - 1, 2) if (i + 1 + shift) % per_clip != 0]
        swaps.append(pairs + [(j, i) for i, j in pairs])
    act_one = lax.ppermute(act_one, "tm", swaps[0])
    act_two = lax.ppermute(act_two, "tm", swaps[1])
    act_other = lax.ppermute(act, "space", cross)
    lat_own, lat_send = selected_latent(
        core_index, noisy, jnp.asarray(selections(channels), BF), der
    )
    lat_other = lax.ppermute(lat_send, "space", cross)
    flat = (frames, span, channels)
    gp, gp_one, gp_two, loss_lanes, rim = temporal_forward(
        scale,
        odd,
        act,
        act_one,
        act_two,
        w_temporal,
        clean.reshape(flat),
        noise.reshape(flat),
        lat_own,
    )
    gp_one = lax.ppermute(gp_one, "tm", swaps[0])
    gp_two = lax.ppermute(gp_two, "tm", swaps[1])
    gp_other = lax.ppermute(gp, "space", cross)
    rim_other = lax.ppermute(rim, "space", cross)
    bits = []
    for order in ORDERS:
        own = []
        for axis in order:
            value = tm // STRIDES[axis] % RING
            low, high = bit_of(value, 0), bit_of(value, 1)
            own.append(jnp.where(core == 0, high, low))
            own.append(jnp.where(core == 0, low, high))
        bits.append([b.astype(jnp.int32) for b in own])
    first_bits = jnp.stack([b[0] for b in bits])
    extra, *more_keeps, loss = temporal_grad_local(
        jnp.concatenate([first_bits, core_index, jnp.reshape(tm, (1,)).astype(jnp.int32)]),
        act,
        rim,
        act_other,
        rim_other,
        gp,
        gp_other,
        jnp.asarray(selections(features), BF),
        jnp.asarray(reorders(features), BF),
        loss_lanes,
    )
    gh = temporal_backward(odd, gp, gp_one, gp_two, w_temporal, der, loss)
    gh_other = lax.ppermute(gh, "space", cross)
    lat = arranged_latent(
        core_index, lat_own, lat_other, jnp.asarray(reorders(channels), BF), gh
    )
    send_at = jnp.concatenate([core_index, 1 - first_bits])
    keep_at = jnp.concatenate([core_index, first_bits])
    (send_1,) = gradient_send((1,), send_at, lat, gh, gh_other, extra, "spatial_send_first")
    send_2, send_0 = gradient_send((2, 0), send_at, lat, gh, gh_other, extra, "spatial_send_rest")
    sends = [send_0, send_1, send_2]
    keeps = gradient_keep(keep_at, lat, gh, gh_other)

    state = [
        (sends[t].reshape(-1, features), None, more_keeps[t], loss if t == 0 else None)
        for t in range(3)
    ]
    count, more = channels // 4, features // 4
    for step in range(6):
        met = [
            lax.ppermute(state[t][0], both, swap_pairs(ORDERS[t][step // 2], step, size))
            for t in range(3)
        ]
        if step == 5:
            break
        for t in range(3):
            _, sp, tp, total = state[t]
            name = "combine_%d_%d" % (step, t)
            if step == 0:
                arrived = met[t].reshape(sends[t].shape)
                state[t] = combine_first(t, jnp.stack(bits[t]), keeps, arrived, tp, total, name)
            else:
                bit = jnp.reshape(bits[t][step + 1], (1,))
                state[t] = combine(bit, met[t], sp, tp, total, count, more, name)
        count, more = count // 2, more // 2

    spatial_parts, temporal_parts = [], []
    for t in range(3):
        _, sp, tp, total = state[t]
        slabs, loss_at, behind = places(count, total is not None)
        spatial_parts.append(
            jnp.stack(
                [sp[b, :count] + met[t][s : s + count].astype(F32) for b, s in enumerate(slabs)]
            )
        )
        temporal_parts.append(tp[:more] + met[t][behind : behind + more].astype(F32))
        if total is not None:
            loss_sum = jnp.sum(total + joined(met[t][loss_at : loss_at + LOSS].astype(F32)))
    spatial_grad = jnp.transpose(jnp.stack(spatial_parts), (2, 0, 1, 3))
    temporal_grad = jnp.transpose(jnp.stack(temporal_parts), (1, 0, 2))
    return (loss_sum / (positions * features), spatial_grad, temporal_grad)


def solution(mesh):
    placed = (P("tm", "space", None, None), P("tm", "space", None, None), P(), P(), P())
    return jax.shard_map(
        on_device,
        mesh=mesh,
        in_specs=placed,
        out_specs=(P(), P(("tm", "space"), None, None, None), P(("tm", "space"), None, None)),
        check_vma=False,
    )
```

```python
import functools
import math

import jax
import jax.numpy as jnp
import numpy as np
from jax import lax
from jax.experimental import pallas as pl
from jax.experimental.pallas import tpu as pltpu
from jax.sharding import PartitionSpec as P

CLIP = 80
STEPS = 1000
BF = jnp.bfloat16
F32 = jnp.float32
MIB = 1 << 20
STRIDES = (16, 4, 1)
RING = 4
ORDERS = ((0, 1, 2), (1, 2, 0), (2, 0, 1))
LOSS = 16
EXTRA = 64


def params(mib):
    return pltpu.CompilerParams(vmem_limit_bytes=mib * MIB)


def in_hbm(x):
    return pltpu.with_memory_space_constraint(x, pltpu.HBM)


def in_vmem(x):
    return pltpu.with_memory_space_constraint(x, pltpu.VMEM)


def cost(flops, nbytes):
    return pl.CostEstimate(flops=int(flops), bytes_accessed=int(nbytes), transcendentals=0)


def spatial_forward_kernel(
    odd, x_ref, above_ref, below_ref, w_ref, act_ref, one_ref, two_ref, der_ref, xp, acc, taps, sems
):
    order = (1, 0, 2)
    step = pl.program_id(0)
    first = jnp.where(step == 0, 1, jnp.where(step == 1, 0, 2))
    frames, span, channels = x_ref.shape
    cols = above_ref.shape[1]
    features = w_ref.shape[3]
    wide = features // 256 * 256
    rest = features - wide

    @pl.when(step == 0)
    def _():
        for k in range(9):
            pltpu.make_async_copy(w_ref.at[order[k // 3], k % 3], taps.at[k], sems.at[k]).start()
        xp[:, 0:cols, :] = above_ref[...]
        xp[:, cols : cols + span, :] = x_ref[...]
        xp[:, cols + span : span + 2 * cols, :] = below_ref[...]
        acc[...] = jnp.zeros_like(acc)

    start = pl.multiple_of(first * cols, cols)
    piece = xp[:, pl.ds(start, span), :].reshape(frames * span, channels)
    for b in range(3):
        k = 3 * step + b
        pltpu.make_async_copy(w_ref.at[first, b], taps.at[k], sems.at[k]).wait()
        acc[b, :, 0:wide] += jnp.dot(piece, taps[k, :, 0:wide], preferred_element_type=F32)
    ends = jnp.concatenate([taps[3 * step + b, :, wide:] for b in range(3)], axis=1)
    prod = jnp.dot(piece, ends, preferred_element_type=F32)
    for b in range(3):
        acc[b, :, wide:] += prod[:, b * rest : (b + 1) * rest]

    @pl.when(step == 2)
    def _():
        col = lax.broadcasted_iota(jnp.int32, (span, features), 0) % cols

        def one(f, carry):
            rows = pl.ds(pl.multiple_of(f * span, span), span)
            left = jnp.where(col == 0, 0.0, pltpu.roll(acc[0, rows, :], 1, 0))
            right = jnp.where(col == cols - 1, 0.0, pltpu.roll(acc[2, rows, :], span - 1, 0))
            hidden = left + acc[1, rows, :] + right
            sig = 1.0 / (1.0 + jnp.exp(-hidden))
            act_ref[f] = (hidden * sig).astype(BF)
            der_ref[f] = sig * (1.0 + hidden * (1.0 - sig))
            return carry

        lax.fori_loop(0, frames, one, 0)
        one_ref[0] = act_ref[(1 - odd[0]) * (frames - 1)]
        two_ref[0] = act_ref[odd[0] * (frames - 1)]


def spatial_forward(odd, x, above, below, weight):
    frames, span, channels = x.shape
    cols = above.shape[1]
    features = weight.shape[3]
    whole = lambda s: (0, 0, 0)
    return pl.pallas_call(
        spatial_forward_kernel,
        grid=(3,),
        in_specs=[
            pl.BlockSpec(memory_space=pltpu.SMEM),
            pl.BlockSpec(x.shape, whole),
            pl.BlockSpec(above.shape, whole),
            pl.BlockSpec(below.shape, whole),
            pl.BlockSpec(memory_space=pltpu.HBM),
        ],
        out_specs=[
            pl.BlockSpec((frames, span, features), whole),
            pl.BlockSpec((1, span, features), whole),
            pl.BlockSpec((1, span, features), whole),
            pl.BlockSpec((frames, span, features), whole),
        ],
        out_shape=[
            jax.ShapeDtypeStruct((frames, span, features), BF),
            jax.ShapeDtypeStruct((1, span, features), BF),
            jax.ShapeDtypeStruct((1, span, features), BF),
            pltpu.VMEM((frames, span, features), F32),
        ],
        scratch_shapes=[
            pltpu.VMEM((frames, span + 2 * cols, channels), BF),
            pltpu.VMEM((3, frames * span, features), F32),
            pltpu.VMEM((9, channels, features), BF),
            pltpu.SemaphoreType.DMA((9,)),
        ],
        compiler_params=params(40),
        cost_estimate=cost(
            2 * 9 * frames * span * channels * features, 2 * 9 * channels * features
        ),
        name="spatial_forward",
    )(odd, x, above, below, in_hbm(weight))


def temporal_forward_kernel(
    scale, odd, act_ref, one_ref, two_ref, w_ref, clean_ref, noise_ref, *rest
):
    gp_ref, one_out, two_out, loss_ref, rim_ref, ap = rest[1:]
    frames, span, features = act_ref.shape
    factor = scale[2]
    ap[(1 - odd[0]) * (frames + 1)] = one_ref[0]
    ap[odd[0] * (frames + 1)] = two_ref[0]
    ap[1 : frames + 1] = act_ref[...]
    pred = jnp.zeros((frames * span, features), F32)
    for tap in range(3):
        pred = pred + jnp.dot(
            ap[tap : tap + frames].reshape(frames * span, features),
            w_ref[tap],
            preferred_element_type=F32,
        )
    clean = clean_ref[...].reshape(frames * span, features).astype(F32)
    noise = noise_ref[...].reshape(frames * span, features).astype(F32)
    diff = pred - (scale[0] * noise - scale[1] * clean)
    gp_ref[...] = (2.0 * diff / factor).astype(BF).reshape(frames, span, features)
    one_out[0] = gp_ref[(1 - odd[0]) * (frames - 1)]
    two_out[0] = gp_ref[odd[0] * (frames - 1)]
    loss = jnp.sum(diff * diff, axis=0, keepdims=True)
    loss_ref[...] = loss
    rim_ref[0:span, :] = ap[0]
    rim_ref[span : 2 * span, :] = ap[frames + 1]
    rim_ref[2 * span :, :] = stacked(loss, LOSS).astype(BF)


def temporal_forward(scale, odd, act, one, two, weight, clean, noise, token):
    frames, span, features = act.shape
    whole = lambda i: (0, 0, 0)
    head = pl.BlockSpec((frames, span, features), whole)
    halo = pl.BlockSpec((1, span, features), whole)
    return pl.pallas_call(
        temporal_forward_kernel,
        grid=(1,),
        in_specs=[
            pl.BlockSpec(memory_space=pltpu.SMEM),
            pl.BlockSpec(memory_space=pltpu.SMEM),
            head,
            halo,
            halo,
            pl.BlockSpec(weight.shape, whole),
            head,
            head,
            pl.BlockSpec(memory_space=pl.ANY),
        ],
        out_specs=[
            head,
            halo,
            halo,
            pl.BlockSpec((1, features), lambda i: (0, 0)),
            pl.BlockSpec((2 * span + LOSS, features), lambda i: (0, 0)),
        ],
        out_shape=[
            jax.ShapeDtypeStruct((frames, span, features), BF),
            jax.ShapeDtypeStruct((1, span, features), BF),
            jax.ShapeDtypeStruct((1, span, features), BF),
            jax.ShapeDtypeStruct((1, features), F32),
            jax.ShapeDtypeStruct((2 * span + LOSS, features), BF),
        ],
        scratch_shapes=[pltpu.VMEM((frames + 2, span, features), BF)],
        compiler_params=params(16),
        cost_estimate=cost(2 * 3 * frames * span * features * features, 6 * features * features),
        name="temporal_forward",
    )(scale, odd, act, one, two, weight, clean, noise, token)


def thirds(value):
    high = value.astype(BF)
    rest = value - high.astype(F32)
    middle = rest.astype(BF)
    return high, middle, (rest - middle.astype(F32)).astype(BF)


def stacked(value, rows):
    high, middle, low = thirds(value)
    row = lax.broadcasted_iota(jnp.int32, (rows, value.shape[1]), 0)
    parts = [p.astype(F32) for p in (high, middle, low)]
    return jnp.where(
        row == 0, parts[0], jnp.where(row == 1, parts[1], jnp.where(row == 2, parts[2], 0.0))
    )


def joined(rows):
    return (rows[0:1] + rows[1:2]) + rows[2:3]


def temporal_grad_kernel(
    bits_ref,
    act_ref,
    rim_ref,
    act_other_ref,
    rim_other_ref,
    gp_ref,
    gp_other_ref,
    choice_ref,
    reorder_ref,
    loss_ref,
    send_ref,
    keep_0,
    keep_1,
    keep_2,
    sum_ref,
    padded,
    chosen,
    gps,
    total,
    choice,
    reorder,
    sems,
):
    frames, span, features = gp_ref.shape
    core = bits_ref[3]
    half = features // 2
    rows = half // 2
    lanes = loss_ref[...] + joined(rim_other_ref[2 * span : 2 * span + LOSS, :].astype(F32))
    lane = lax.broadcasted_iota(jnp.int32, lanes.shape, 1)
    loss = jnp.where(lane == bits_ref[4], jnp.sum(lanes, axis=1, keepdims=True), 0.0)
    sum_ref[...] = loss
    copies = [
        pltpu.make_async_copy(choice_ref.at[core], choice, sems.at[0]),
        pltpu.make_async_copy(reorder_ref.at[core], reorder, sems.at[1]),
    ]
    for c in copies:
        c.start()
    for which, (act, rim) in enumerate(((act_ref, rim_ref), (act_other_ref, rim_other_ref))):
        padded[which, 0] = rim[0:span, :]
        padded[which, 1 : frames + 1] = act[...]
        padded[which, frames + 1] = rim[span : 2 * span, :]
    for c in copies:
        c.wait()
    chosen[...] = lax.dot_general(
        choice[...],
        padded[...].reshape(-1, features),
        (((1,), (1,)), ((), ())),
        preferred_element_type=F32,
    ).astype(BF)
    gps[0:frames] = gp_ref[...]
    gps[frames:] = gp_other_ref[...]
    for tap, keep in enumerate((keep_0, keep_1, keep_2)):
        here = tap * span
        there = here + (frames + 2) * span
        long = frames * span
        left = jnp.concatenate(
            [chosen[:, here : here + long], chosen[:, there : there + long]], axis=1
        )
        if tap > 0:
            left = jnp.dot(
                reorder[tap - 1], left, preferred_element_type=F32
            ).astype(BF)
        total[...] = jnp.dot(
            left, gps[...].reshape(2 * long, features), preferred_element_type=F32
        )
        bit = bits_ref[tap]
        kept = pl.ds(pl.multiple_of(bit * rows, rows), rows)
        sent = pl.ds(pl.multiple_of((1 - bit) * rows, rows), rows)
        keep[...] = total[kept, :]
        send_ref[tap, 0:rows, :] = total[sent, :].astype(BF)
        send_ref[tap, rows : rows + LOSS, :] = stacked(loss, LOSS).astype(BF)
        send_ref[tap, rows + LOSS :, :] = jnp.zeros(
            (send_ref.shape[1] - rows - LOSS, features), BF
        )


def temporal_grad_local(
    bits, act, rim, act_other, rim_other, gp, gp_other, choice, reorder, loss
):
    frames, span, features = gp.shape
    rows = features // 4
    vmem = pl.BlockSpec(memory_space=pltpu.VMEM)
    return pl.pallas_call(
        temporal_grad_kernel,
        in_specs=[pl.BlockSpec(memory_space=pltpu.SMEM)]
        + [vmem] * 6
        + [pl.BlockSpec(memory_space=pltpu.HBM)] * 2
        + [vmem],
        out_shape=[
            pltpu.VMEM((3, 3 * EXTRA, features), BF),
            *[pltpu.HBM((rows, features), F32) for _ in range(3)],
            pltpu.VMEM((1, features), F32),
        ],
        out_specs=[vmem] * 5,
        scratch_shapes=[
            pltpu.VMEM((2, frames + 2, span, features), BF),
            pltpu.VMEM((features // 2, 2 * (frames + 2) * span), BF),
            pltpu.VMEM((2 * frames, span, features), BF),
            pltpu.VMEM((features // 2, features), F32),
            pltpu.VMEM(choice.shape[1:], BF),
            pltpu.VMEM(reorder.shape[1:], BF),
            pltpu.SemaphoreType.DMA((2,)),
        ],
        compiler_params=params(20),
        cost_estimate=cost(
            2 * 4 * frames * span * features * features, 6 * features * features
        ),
        name="temporal_grad",
    )(bits, act, rim, act_other, rim_other, gp, gp_other, in_hbm(choice), in_hbm(reorder), loss)


def temporal_backward_kernel(
    odd, gp_ref, one_ref, two_ref, w_ref, der_ref, token, out_ref, pad
):
    frames, span, features = gp_ref.shape
    pad[(1 - odd[0]) * (frames + 1)] = one_ref[0]
    pad[odd[0] * (frames + 1)] = two_ref[0]
    pad[1 : frames + 1] = gp_ref[...]
    total = jnp.zeros((frames * span, features), F32)
    for tap in range(3):
        total = total + lax.dot_general(
            pad[2 - tap : 2 - tap + frames].reshape(frames * span, features),
            w_ref[tap],
            (((1,), (1,)), ((), ())),
            preferred_element_type=F32,
        )
    der = der_ref[...].reshape(frames * span, features)
    out_ref[...] = (total * der).astype(BF).reshape(frames, span, features)


def temporal_backward(odd, gp, one, two, weight, der, token):
    frames, span, features = gp.shape
    return pl.pallas_call(
        temporal_backward_kernel,
        in_specs=[pl.BlockSpec(memory_space=pltpu.SMEM)]
        + [pl.BlockSpec(memory_space=pltpu.VMEM)] * 5
        + [pl.BlockSpec(memory_space=pl.ANY)],
        out_shape=pltpu.VMEM((frames, span, features), BF),
        scratch_shapes=[pltpu.VMEM((frames + 2, span, features), BF)],
        compiler_params=params(12),
        cost_estimate=cost(2 * 3 * frames * span * features * features, 6 * features * features),
        name="temporal_backward",
    )(odd, gp, one, two, weight, der, token)


def select_latent_kernel(core_ref, x_ref, choice_ref, token, own_ref, send_ref):
    core = core_ref[0]
    x = x_ref[...].reshape(-1, x_ref.shape[2])
    for out, which in ((send_ref, 1 - core), (own_ref, core)):
        out[...] = lax.dot_general(
            choice_ref[which], x, (((1,), (1,)), ((), ())), preferred_element_type=F32
        ).astype(BF)


def selected_latent(core, x, choice, token):
    frames, span, channels = x.shape
    shape = jax.ShapeDtypeStruct((channels // 2, frames * span), BF)
    vmem = pl.BlockSpec(memory_space=pltpu.VMEM)
    return pl.pallas_call(
        select_latent_kernel,
        in_specs=[
            pl.BlockSpec(memory_space=pltpu.SMEM),
            vmem,
            vmem,
            pl.BlockSpec(memory_space=pl.ANY),
        ],
        out_specs=[vmem, vmem],
        out_shape=[shape, shape],
        compiler_params=params(16),
        cost_estimate=cost(2 * frames * span * channels * channels, 4 * channels * channels),
        name="select_latent",
    )(core, x, choice, token)


def arrange_latent_kernel(
    core_ref, own_ref, other_ref, reorder_ref, token, out_hbm, out_ref, reorder, sem, sems
):
    core = core_ref[0]
    copy = pltpu.make_async_copy(reorder_ref.at[core], reorder, sem)
    copy.start()
    frames = 5
    span = own_ref.shape[1] // frames
    for f in range(frames):
        here = pl.multiple_of((2 * f + core) * span, span)
        there = pl.multiple_of((2 * f + 1 - core) * span, span)
        out_ref[0, :, pl.ds(here, span)] = own_ref[:, f * span : (f + 1) * span]
        out_ref[0, :, pl.ds(there, span)] = other_ref[:, f * span : (f + 1) * span]
    copy.wait()
    copies = [pltpu.make_async_copy(out_ref.at[k], out_hbm.at[k], sems.at[k]) for k in range(3)]
    copies[0].start()
    for third in range(1, 3):
        out_ref[third] = jnp.dot(
            reorder[third - 1], out_ref[0], preferred_element_type=F32
        ).astype(BF)
        copies[third].start()
    for c in copies:
        c.wait()


def arranged_latent(core, own, other, reorder, token):
    half, positions = own.shape
    vmem = pl.BlockSpec(memory_space=pltpu.VMEM)
    return pl.pallas_call(
        arrange_latent_kernel,
        in_specs=[
            pl.BlockSpec(memory_space=pltpu.SMEM),
            vmem,
            vmem,
            pl.BlockSpec(memory_space=pltpu.HBM),
            pl.BlockSpec(memory_space=pl.ANY),
        ],
        out_specs=pl.BlockSpec(memory_space=pltpu.HBM),
        out_shape=pltpu.HBM((3, half, 2 * positions), BF),
        scratch_shapes=[
            pltpu.VMEM((3, half, 2 * positions), BF),
            pltpu.VMEM(reorder.shape[1:], BF),
            pltpu.SemaphoreType.DMA,
            pltpu.SemaphoreType.DMA((3,)),
        ],
        compiler_params=params(16),
        cost_estimate=cost(8 * half * half * positions, 20 * half * positions),
        name="arrange_latent",
    )(core, own, other, in_hbm(reorder), token)


def shifted_gradient(core, own_ref, other_ref, pad):
    frames, span, features = own_ref.shape
    cols = (pad.shape[2] - 2 * span) // 2
    col = lax.broadcasted_iota(jnp.int32, (span, features), 0) % cols
    rim = jnp.zeros((cols, features), BF)

    def one(f, carry):
        for b in range(3):
            pad[b, f, 0:cols, :] = rim
            pad[b, f, cols + 2 * span : 2 * cols + 2 * span, :] = rim
        for ref, place in ((own_ref, core), (other_ref, 1 - core)):
            rows = pl.ds(pl.multiple_of(cols + place * span, cols), span)
            here = ref[f]
            wide = here.astype(F32)
            later = jnp.where(col == cols - 1, 0.0, pltpu.roll(wide, span - 1, 0))
            sooner = jnp.where(col == 0, 0.0, pltpu.roll(wide, 1, 0))
            pad[0, f, rows, :] = later.astype(BF)
            pad[1, f, rows, :] = here
            pad[2, f, rows, :] = sooner.astype(BF)
        return carry

    lax.fori_loop(0, frames, one, 0)


def gradient_send_kernel(thirds, where, lat_ref, own_ref, other_ref, extra_ref, *rest):
    outs, (pad, lat, lat_sems, pad_sems) = rest[: len(thirds)], rest[-4:]
    frames, span, features = own_ref.shape
    cols = pad.shape[2] // 2 - span
    height = lat.shape[1]
    copies = []
    for k, first in enumerate(thirds):
        rows = pl.ds(pl.multiple_of(where[1 + first] * height, height), height)
        copies.append(
            pltpu.make_async_copy(lat_ref.at[first, rows, :], lat.at[k], lat_sems.at[k])
        )
    for c in copies:
        c.start()
    shifted_gradient(where[0], own_ref, other_ref, pad)
    leaving = []
    if len(thirds) > 1:
        pad_out = rest[len(thirds)]
        for b in range(3):
            leaving.append(pltpu.make_async_copy(pad.at[b], pad_out.at[b], pad_sems.at[b]))
            leaving[b].start()
    for k, first in enumerate(thirds):
        copies[k].wait()
        start = (2 - first) * cols
        for second in range(3):
            grad = pad[second, :, start : start + 2 * span, :]
            outs[k][second, 0:height, :] = jnp.dot(
                lat[k], grad.reshape(2 * frames * span, features), preferred_element_type=F32
            ).astype(BF)
            outs[k][second, height:, :] = extra_ref[first, second * EXTRA : (second + 1) * EXTRA, :]
    for c in leaving:
        c.wait()


def gradient_send(thirds, where, lat, own, other, extra, name):
    frames, span, features = own.shape
    rows = lat.shape[1] // 2
    cols = 16
    n = len(thirds)
    vmem = pl.BlockSpec(memory_space=pltpu.VMEM)
    hbm = pl.BlockSpec(memory_space=pltpu.HBM)
    return pl.pallas_call(
        functools.partial(gradient_send_kernel, thirds),
        in_specs=[pl.BlockSpec(memory_space=pltpu.SMEM), hbm] + [vmem] * 3,
        out_specs=[vmem] * n + [hbm] * (n > 1),
        out_shape=[pltpu.VMEM((3, rows + EXTRA, features), BF)] * n
        + [pltpu.HBM((3, frames, 2 * span + 2 * cols, features), BF)] * (n > 1),
        scratch_shapes=[
            pltpu.VMEM((3, frames, 2 * span + 2 * cols, features), BF),
            pltpu.VMEM((n, rows, lat.shape[2]), BF),
            pltpu.SemaphoreType.DMA((n,)),
            pltpu.SemaphoreType.DMA((3,)),
        ],
        compiler_params=params(28),
        cost_estimate=cost(1, 1),
        name=name,
    )(where, in_hbm(lat), own, other, in_vmem(extra))


def gradient_keep_kernel(where, lat_ref, pad_ref, out_ref, pad, lat, lat_sems, pad_sems, sums, sems):
    frames = pad.shape[1]
    cols = 16
    span = pad.shape[2] // 2 - cols
    features = pad.shape[3]
    height = lat.shape[1]
    copies = []
    for k in range(3):
        rows = pl.ds(pl.multiple_of(where[1 + k] * height, height), height)
        copies.append(pltpu.make_async_copy(lat_ref.at[k, rows, :], lat.at[k], lat_sems.at[k]))
    pltpu.make_async_copy(pad_ref.at[0], pad.at[0], pad_sems.at[0]).start()
    for c in copies:
        c.start()
    for b in range(1, 3):
        pltpu.make_async_copy(pad_ref.at[b], pad.at[b], pad_sems.at[b]).start()
    for c in copies:
        c.wait()

    def one(b, carry):
        pltpu.make_async_copy(pad_ref.at[b], pad.at[b], pad_sems.at[b]).wait()
        for k in range(3):
            start = (2 - k) * cols
            grad = pad[b, :, start : start + 2 * span, :]
            sums[k, b] = jnp.dot(
                lat[k], grad.reshape(2 * frames * span, features), preferred_element_type=F32
            )
            pltpu.make_async_copy(sums.at[k, b], out_ref.at[k, b], sems.at[k, b]).start()
        return carry

    lax.fori_loop(0, 3, one, 0)
    for b in range(3):
        for k in range(3):
            pltpu.make_async_copy(sums.at[k, b], out_ref.at[k, b], sems.at[k, b]).wait()


def gradient_keep(where, lat, pad):
    features = pad.shape[3]
    rows = lat.shape[1] // 2
    hbm = pl.BlockSpec(memory_space=pltpu.HBM)
    return pl.pallas_call(
        gradient_keep_kernel,
        in_specs=[pl.BlockSpec(memory_space=pltpu.SMEM), hbm, hbm],
        out_specs=hbm,
        out_shape=pltpu.HBM((3, 3, rows, features), F32),
        scratch_shapes=[
            pltpu.VMEM(pad.shape, BF),
            pltpu.VMEM((3, rows, lat.shape[2]), BF),
            pltpu.SemaphoreType.DMA((3,)),
            pltpu.SemaphoreType.DMA((3,)),
            pltpu.VMEM((3, 3, rows, features), F32),
            pltpu.SemaphoreType.DMA((3, 3)),
        ],
        compiler_params=params(28),
        cost_estimate=cost(1, 1),
        name="spatial_keep",
    )(where, in_hbm(lat), in_hbm(pad))


def bit_of(value, kind):
    if kind == 0:
        return value // 2
    return (value + 1) // 2 % 2


def swap_pairs(axis, step, size):
    pairs = []
    stride = STRIDES[axis]
    for device in range(size):
        tm, core = divmod(device, 2)
        value = tm // stride % RING
        partner = (value ^ 1) if (step + core) % 2 == 0 else (RING - 1 - value)
        pairs.append((device, (tm + (partner - value) * stride) * 2 + core))
    return pairs


def owners(order, core):
    found = []
    for n in range(RING**3):
        place = 0
        for k, axis in enumerate(order):
            digit = n // RING ** (2 - k) % RING
            first, second = divmod(digit, 2)
            low, high = (second, first) if core == 0 else (first, second)
            value = 2 * low + (low ^ high)
            place += value * STRIDES[axis]
        found.append(2 * place + core)
    return np.array(found)


def one_hot(rows, width):
    return (rows[:, None] == np.arange(width)[None, :]).astype(np.float32)


def selections(channels):
    each = channels // (2 * RING**3)
    return np.stack(
        [
            one_hot((owners(ORDERS[0], c)[:, None] * each + np.arange(each)).reshape(-1), channels)
            for c in range(2)
        ]
    )


def reorders(channels):
    each = channels // (2 * RING**3)
    found = []
    for c in range(2):
        base = list(owners(ORDERS[0], c))
        for order in ORDERS[1:]:
            at = np.array([base.index(o) for o in owners(order, c)])
            rows = (at[:, None] * each + np.arange(each)).reshape(-1)
            found.append(one_hot(rows, channels // 2))
    return np.stack(found).reshape(2, 2, channels // 2, channels // 2)


def up_to(n, multiple):
    return -(-n // multiple) * multiple


def payload_rows(rows, more, has_loss):
    return 3 * up_to(rows, 16) + (LOSS if has_loss else 0) + up_to(more, 16)


def places(rows, has_loss):
    slab = up_to(rows, 16)
    return [0, slab, 2 * slab], 3 * slab, 3 * slab + (LOSS if has_loss else 0)


def halve(ref, bit, count, send_ref, send_at):
    part = count // 2
    sent = up_to(part, 16)
    kept = up_to(part, 8)
    if part % 16 == 0:
        mine = ref[pl.ds(pl.multiple_of(bit * part, part), part), :]
        theirs = ref[pl.ds(pl.multiple_of((1 - bit) * part, part), part), :]
    else:
        whole = ref[...]
        tall = whole.shape[0]
        mine = pltpu.roll(whole, (tall - bit * part) % tall, 0)[:kept]
        theirs = pltpu.roll(whole, (tall - (1 - bit) * part) % tall, 0)[:sent]
    send_ref[send_at : send_at + sent, :] = theirs.astype(send_ref.dtype)
    return mine


def combine_first_kernel(third, has_loss, bits, keep_ref, met_ref, tp_ref, *refs):
    refs = list(refs)
    loss_ref = refs.pop(0) if has_loss else None
    send_ref, sp_out, tp_out = refs[:3]
    refs = refs[3:]
    loss_out = refs.pop(0) if has_loss else None
    keep_buf, region, extra_buf, tp_buf, sems = refs
    rows, features = keep_ref.shape[2:]
    count = rows // 2
    copies = [
        pltpu.make_async_copy(met_ref.at[:, pl.ds(rows, EXTRA), :], extra_buf, sems.at[0]),
        pltpu.make_async_copy(tp_ref, tp_buf, sems.at[1]),
    ]
    for k, bit in enumerate((1 - bits[1], bits[1])):
        at = pl.multiple_of(bit * count, count)
        part = pl.ds(at, count)
        copies += [
            pltpu.make_async_copy(
                keep_ref.at[third, :, part, :], keep_buf.at[k], sems.at[2 + 2 * k]
            ),
            pltpu.make_async_copy(met_ref.at[:, part, :], region.at[k], sems.at[3 + 2 * k]),
        ]
    for c in copies:
        c.start()
    for c in copies[:4]:
        c.wait()
    for b in range(3):
        total = keep_buf[0, b] + region[0, b].astype(F32)
        send_ref[b * count : (b + 1) * count, :] = total.astype(BF)
    tall = tp_buf.shape[0]
    extra = extra_buf[...].reshape(3 * EXTRA, features).astype(F32)
    tp_buf[...] += extra[:tall]
    behind = 3 * count
    if has_loss:
        loss = loss_ref[...] + joined(extra[tall : tall + LOSS])
        loss_out[...] = loss
        send_ref[behind : behind + LOSS, :] = stacked(loss, LOSS).astype(BF)
        behind += LOSS
    tp_out[...] = halve(tp_buf, bits[1], tall, send_ref, behind)
    for c in copies[4:]:
        c.wait()
    for b in range(3):
        sp_out[b] = keep_buf[1, b] + region[1, b].astype(F32)


def combine_first(third, bits, keep, met, tp, loss, name):
    has_loss = loss is not None
    rows, width = keep.shape[2:]
    half = rows // 2
    vmem = pl.BlockSpec(memory_space=pltpu.VMEM)
    hbm = pl.BlockSpec(memory_space=pltpu.HBM)
    out_shape = [
        pltpu.VMEM((payload_rows(half, half // 2, has_loss), width), BF),
        pltpu.VMEM((3, half, width), F32),
        pltpu.VMEM((half // 2, width), F32),
    ]
    if has_loss:
        out_shape.append(pltpu.VMEM((1, width), F32))
    done = pl.pallas_call(
        functools.partial(combine_first_kernel, third, has_loss),
        in_specs=[pl.BlockSpec(memory_space=pltpu.SMEM), hbm, hbm, hbm] + [vmem] * has_loss,
        out_specs=[vmem] * len(out_shape),
        out_shape=out_shape,
        scratch_shapes=[
            pltpu.VMEM((2, 3, half, width), F32),
            pltpu.VMEM((2, 3, half, width), BF),
            pltpu.VMEM((3, EXTRA, width), BF),
            pltpu.VMEM((half, width), F32),
            pltpu.SemaphoreType.DMA((6,)),
        ],
        compiler_params=params(16),
        cost_estimate=cost(0, 8 * rows * width),
        name=name,
    )(bits, in_hbm(keep), in_hbm(met), in_hbm(tp), *([in_vmem(loss)] if has_loss else []))
    return done if has_loss else (*done, None)


def combine_kernel(rows, more, has_loss, bit_ref, met_ref, sp_ref, tp_ref, *rest):
    if has_loss:
        loss_ref, send_ref, sp_out, tp_out, loss_out, full, full_more = rest
    else:
        send_ref, sp_out, tp_out, full, full_more = rest
    bit = bit_ref[0]
    slabs, loss_at, behind = places(rows, has_loss)
    next_slab = up_to(rows // 2, 16)
    for b in range(3):
        tall = full.shape[1]
        full[b] = sp_ref[b] + met_ref[slabs[b] : slabs[b] + tall, :].astype(F32)
        sp_out[b] = halve(full.at[b], bit, rows, send_ref, b * next_slab)
    tall = full_more.shape[0]
    full_more[...] = tp_ref[...] + met_ref[behind : behind + tall, :].astype(F32)
    behind = 3 * next_slab
    if has_loss:
        loss = loss_ref[...] + joined(met_ref[loss_at : loss_at + LOSS, :].astype(F32))
        loss_out[...] = loss
        send_ref[behind : behind + LOSS, :] = stacked(loss, LOSS).astype(send_ref.dtype)
        behind += LOSS
    tp_out[...] = halve(full_more, bit, more, send_ref, behind)


def combine(bit, met, sp, tp, loss, rows, more, name):
    has_loss = loss is not None
    width = met.shape[1]
    out_shape = [
        pltpu.VMEM((payload_rows(rows // 2, more // 2, has_loss), width), BF),
        pltpu.VMEM((3, up_to(rows // 2, 8), width), F32),
        pltpu.VMEM((up_to(more // 2, 8), width), F32),
    ]
    operands = [bit, in_vmem(met), in_vmem(sp), in_vmem(tp)]
    if has_loss:
        out_shape.append(pltpu.VMEM((1, width), F32))
        operands.append(in_vmem(loss))
    vmem = pl.BlockSpec(memory_space=pltpu.VMEM)
    done = pl.pallas_call(
        functools.partial(combine_kernel, rows, more, has_loss),
        in_specs=[pl.BlockSpec(memory_space=pltpu.SMEM)] + [vmem] * (len(operands) - 1),
        out_specs=[vmem] * len(out_shape),
        out_shape=out_shape,
        scratch_shapes=[pltpu.VMEM(sp.shape, F32), pltpu.VMEM(tp.shape, F32)],
        compiler_params=params(12),
        cost_estimate=cost(0, 8 * sp.size),
        name=name,
    )(*operands)
    return done if has_loss else (*done, None)


def on_device(clean, noise, timestep, spatial_weight, temporal_weight):
    frames, rows, cols, channels = clean.shape
    features = temporal_weight.shape[0]
    span = rows * cols
    blocks = lax.axis_size("tm")
    size = 2 * blocks
    tm = lax.axis_index("tm")
    core = lax.axis_index("space")
    both = ("tm", "space")
    step_value = timestep[0].astype(F32)
    angle = math.pi / 2.0 * (step_value + 1.0) / (STEPS + 1.0)
    signal = jnp.cos(angle)
    sigma = jnp.sin(angle)
    positions = frames * blocks * rows * 2 * cols
    scale = jnp.stack([signal, sigma, jnp.float32(math.sqrt(positions))])
    w_spatial = jnp.transpose(spatial_weight, (1, 2, 0, 3))
    w_temporal = jnp.transpose(temporal_weight, (1, 0, 2))

    def mix(c, n):
        return (signal * c.astype(F32) + sigma * n.astype(F32)).astype(BF)

    edge_at = (1 - core) * (rows - 1)
    edge = mix(
        lax.dynamic_slice_in_dim(clean, edge_at, 1, axis=1),
        lax.dynamic_slice_in_dim(noise, edge_at, 1, axis=1),
    )
    met = lax.ppermute(edge, "space", [(0, 1), (1, 0)]).reshape(frames, cols, channels)
    above = jnp.where(core == 0, jnp.zeros_like(met), met)
    below = jnp.where(core == 0, met, jnp.zeros_like(met))
    noisy = mix(clean, noise).reshape(frames, span, channels)
    cross = [(0, 1), (1, 0)]
    core_index = jnp.reshape(core, (1,)).astype(jnp.int32)
    odd = jnp.reshape(tm % 2, (1,)).astype(jnp.int32)
    act, act_one, act_two, der = spatial_forward(odd, noisy, above, below, w_spatial)

    per_clip = CLIP // frames
    shift = CLIP // 4 // frames
    swaps = []
    for low in range(2):
        pairs = [(i, i + 1) for i in range(low, blocks - 1, 2) if (i + 1 + shift) % per_clip != 0]
        swaps.append(pairs + [(j, i) for i, j in pairs])
    act_one = lax.ppermute(act_one, "tm", swaps[0])
    act_two = lax.ppermute(act_two, "tm", swaps[1])
    act_other = lax.ppermute(act, "space", cross)
    lat_own, lat_send = selected_latent(
        core_index, noisy, jnp.asarray(selections(channels), BF), der
    )
    lat_other = lax.ppermute(lat_send, "space", cross)
    flat = (frames, span, channels)
    gp, gp_one, gp_two, loss_lanes, rim = temporal_forward(
        scale,
        odd,
        act,
        act_one,
        act_two,
        w_temporal,
        clean.reshape(flat),
        noise.reshape(flat),
        lat_own,
    )
    gp_one = lax.ppermute(gp_one, "tm", swaps[0])
    gp_two = lax.ppermute(gp_two, "tm", swaps[1])
    gp_other = lax.ppermute(gp, "space", cross)
    rim_other = lax.ppermute(rim, "space", cross)
    bits = []
    for order in ORDERS:
        own = []
        for axis in order:
            value = tm // STRIDES[axis] % RING
            low, high = bit_of(value, 0), bit_of(value, 1)
            own.append(jnp.where(core == 0, high, low))
            own.append(jnp.where(core == 0, low, high))
        bits.append([b.astype(jnp.int32) for b in own])
    first_bits = jnp.stack([b[0] for b in bits])
    extra, *more_keeps, loss = temporal_grad_local(
        jnp.concatenate([first_bits, core_index, jnp.reshape(tm, (1,)).astype(jnp.int32)]),
        act,
        rim,
        act_other,
        rim_other,
        gp,
        gp_other,
        jnp.asarray(selections(features), BF),
        jnp.asarray(reorders(features), BF),
        loss_lanes,
    )
    gh = temporal_backward(odd, gp, gp_one, gp_two, w_temporal, der, loss)
    gh_other = lax.ppermute(gh, "space", cross)
    lat = arranged_latent(
        core_index, lat_own, lat_other, jnp.asarray(reorders(channels), BF), gh
    )
    send_at = jnp.concatenate([core_index, 1 - first_bits])
    keep_at = jnp.concatenate([core_index, first_bits])
    (send_1,) = gradient_send((1,), send_at, lat, gh, gh_other, extra, "spatial_send_first")
    send_2, send_0, shifted = gradient_send((2, 0), send_at, lat, gh, gh_other, extra, "spatial_send_rest")
    sends = [send_0, send_1, send_2]
    keeps = gradient_keep(keep_at, lat, shifted)

    state = [
        (sends[t].reshape(-1, features), None, more_keeps[t], loss if t == 0 else None)
        for t in range(3)
    ]
    count, more = channels // 4, features // 4
    for step in range(6):
        met = [
            lax.ppermute(state[t][0], both, swap_pairs(ORDERS[t][step // 2], step, size))
            for t in range(3)
        ]
        if step == 5:
            break
        for t in range(3):
            _, sp, tp, total = state[t]
            name = "combine_%d_%d" % (step, t)
            if step == 0:
                arrived = met[t].reshape(sends[t].shape)
                state[t] = combine_first(t, jnp.stack(bits[t]), keeps, arrived, tp, total, name)
            else:
                bit = jnp.reshape(bits[t][step + 1], (1,))
                state[t] = combine(bit, met[t], sp, tp, total, count, more, name)
        count, more = count // 2, more // 2

    spatial_parts, temporal_parts = [], []
    for t in range(3):
        _, sp, tp, total = state[t]
        slabs, loss_at, behind = places(count, total is not None)
        spatial_parts.append(
            jnp.stack(
                [sp[b, :count] + met[t][s : s + count].astype(F32) for b, s in enumerate(slabs)]
            )
        )
        temporal_parts.append(tp[:more] + met[t][behind : behind + more].astype(F32))
        if total is not None:
            loss_sum = jnp.sum(total + joined(met[t][loss_at : loss_at + LOSS].astype(F32)))
    spatial_grad = jnp.transpose(jnp.stack(spatial_parts), (2, 0, 1, 3))
    temporal_grad = jnp.transpose(jnp.stack(temporal_parts), (1, 0, 2))
    return (loss_sum / (positions * features), spatial_grad, temporal_grad)


def solution(mesh):
    placed = (P("tm", "space", None, None), P("tm", "space", None, None), P(), P(), P())
    return jax.shard_map(
        on_device,
        mesh=mesh,
        in_specs=placed,
        out_specs=(P(), P(("tm", "space"), None, None, None), P(("tm", "space"), None, None)),
        check_vma=False,
    )
```
